32 devices in a mesh: dp: 8 (over y, x, core), seq: 4 (over z).
Axes of the slice: x: 2, y: 2, z: 4, core: 2. Of those that a mesh axis runs over, the one named last changes fastest.
Arguments:
- tokens: bfloat16 [8, 1024, 1024], P('dp', 'seq'), may hold values from -6 to 6
- noise_steps: int32 [8], P('dp'), may hold values from 0 to 999
- w_qkv: bfloat16 [1024, 3072], P('dp'), may hold values from -0.1875 to 0.1875
- w_out: bfloat16 [1024, 1024], P('dp'), may hold values from -3.5 to 3.5
- w_up: bfloat16 [1024, 4096], P('dp'), may hold values from -0.1875 to 0.1875
- w_down: bfloat16 [4096, 1024], P('dp'), may hold values from -0.09375 to 0.09375
- w_time: bfloat16 [256, 4096], P(None, 'dp'), may hold values from -0.375 to 0.375
- cotangent: bfloat16 [8, 1024, 1024], P('dp', 'seq'), may hold values from -6 to 6
Outputs:
- result: bfloat16 [8, 1024, 1024], P('dp', 'seq')
- grad_tokens: float32 [8, 1024, 1024], P('dp', 'seq')
- grad_qkv: float32 [1024, 3072], P('dp')
- grad_proj: float32 [1024, 1024], P('dp')
- grad_up: float32 [1024, 4096], P('dp')
- grad_down: float32 [4096, 1024], P('dp')
- grad_time: float32 [256, 4096], P(None, 'dp')
The draws below stay inside these ranges and needn't reach their ends.
All inputs are finite; a program needn't handle non-finite values.
Results may differ from the reference program's by a relative error of at most 0.015.
Values may be sent and summed in bfloat16 or wider, within the bound.
No kernel may reach another device: no remote copies, remote signals or barrier semaphores. Data moves between devices by JAX's collectives and lax.ppermute only.
A program may use at most 192 MiB of HBM per device.

```python
import math
import jax
import jax.numpy as jnp
from jax import lax

D = 1024
HEADS = 16
HEAD_DIM = 64
FF = 4096
TE = 256
NTIME = 1000
LEN = 1024
SEQS = 8


def with_ends(result, rng, smallest, top_value):
    place = [jax.random.randint(jax.random.fold_in(rng, axis), (), 0, length) for axis, length in enumerate(result.shape)]
    main_axis = result.shape.index(max(result.shape))
    beside = place[:main_axis] + [(place[main_axis] + 1) % result.shape[main_axis]] + place[main_axis + 1:]
    return result.at[tuple(place)].set(smallest).at[tuple(beside)].set(top_value)


def block_levels(rng, dims, cuts, least, high):
    def one(position, parts):
        heights = jax.random.uniform(jax.random.fold_in(jax.random.fold_in(rng, 6), position), (parts,), jnp.float32, least / len(cuts), high / len(cuts))
        return jnp.repeat(jnp.exp(heights), dims[position] // parts).reshape((-1,) + (1,) * (len(dims) - position - 1))

    level = one(*cuts[0])
    for cut in cuts[1:]:
        level = level * one(*cut)
    return level


def centred(own_key, shape, spread, limit, cuts=(), kind=jnp.bfloat16):
    result = jax.random.normal(own_key, shape, jnp.float32) * spread
    if len(cuts) > 0:
        result = block_levels(own_key, shape, cuts, -0.22, 0.18) * result
    return jnp.clip(result, min=-limit, max=limit).astype(kind)


def setup_inputs(seed: int = 0) -> dict:
    streams_of = jax.random.split(jax.random.key(seed), 9)
    tokens = centred(streams_of[0], (SEQS, LEN, D), 1.0, 6.0, ((0, 8), (1, 4)))
    noise_steps = with_ends(jax.random.randint(streams_of[1], (SEQS,), 0, NTIME), jax.random.fold_in(streams_of[1], 1), 0, NTIME - 1).astype(jnp.int32)
    w_qkv = centred(streams_of[2], (D, 3 * D), D ** -0.5, 0.1875, ((0, 8),))
    w_out = centred(streams_of[3], (D, D), (max(3 * D // LEN, 1)) ** -0.5, 3.5, ((0, 8),))
    w_up = centred(streams_of[4], (D, FF), D ** -0.5, 0.1875, ((0, 8),))
    w_down = centred(streams_of[5], (FF, D), FF ** -0.5, 0.09375, ((0, 8),))
    w_time = centred(streams_of[6], (TE, 4 * D), TE ** -0.5, 0.375, ((1, 8),))
    cotangent = centred(streams_of[7], (SEQS, LEN, D), 1.0, 6.0, ((0, 8), (1, 4)))
    return dict(tokens=tokens, noise_steps=noise_steps, w_qkv=w_qkv, w_out=w_out, w_up=w_up, w_down=w_down, w_time=w_time, cotangent=cotangent)


highest = lax.Precision.HIGHEST

@jax.custom_vjp
def low(v):
    return lax.optimization_barrier(v.astype(jnp.bfloat16)).astype(jnp.float32)

@jax.custom_vjp
def low_back(v):
    return v

def low_keep(v):
    return (low(v), None)

def low_pass(kept, grad):
    return (grad,)

def back_keep(v):
    return (v, None)

def back_low(kept, grad):
    return (low(grad),)
low.defvjp(low_keep, low_pass)
low_back.defvjp(back_keep, back_low)

def norm_rows(values_in):
    centered = values_in - lax.optimization_barrier(jnp.mean(values_in, axis=-1, keepdims=True))
    return centered * lax.rsqrt(lax.optimization_barrier(jnp.mean(centered * centered, axis=-1, keepdims=True)) + 1e-05)

def time_embedding(noise_step):
    half_dim = TE // 2
    frequency = jnp.exp(-math.log(10000.0) * jnp.arange(half_dim, dtype=jnp.float32) / half_dim)
    angles = noise_step.astype(jnp.float32)[..., None] * frequency
    return jnp.concatenate([jnp.sin(angles), jnp.cos(angles)], axis=-1)

def rotate(values_in, positions, direction):
    half_dim = values_in.shape[-1] // 2
    frequency = jnp.exp(-math.log(10000.0) * jnp.arange(half_dim, dtype=jnp.float32) / half_dim)
    angles = positions[:, None, None] * frequency
    cosine = jnp.cos(angles)
    sine_wave = direction * jnp.sin(angles)
    first_half = values_in[..., :half_dim]
    second_half = values_in[..., half_dim:]
    return jnp.concatenate([first_half * cosine - second_half * sine_wave, first_half * sine_wave + second_half * cosine], axis=-1)

def layer_forward(source, noise_step, w_qkv, w_out, w_up, w_down, w_time):
    condition = jnp.dot(time_embedding(noise_step), w_time, precision=highest)
    scale_a, shift_a, scale_b, shift_b = jnp.split(condition, 4)
    input_a = low(norm_rows(source) * (1.0 + scale_a) + shift_a)
    projected = low_back(jnp.dot(input_a, w_qkv, precision=highest))
    head_view = projected.reshape(LEN, 3, HEADS, HEAD_DIM)
    positions = jnp.arange(LEN, dtype=jnp.float32)
    queries = low_back(low(rotate(head_view[:, 0], positions, 1.0)))
    key_rows = low_back(low(rotate(head_view[:, 1], positions, 1.0)))
    values = low_back(low(head_view[:, 2]))
    score_scale = 1.0 / math.sqrt(HEAD_DIM)
    block_rows = min(512, LEN)

    def attend_block(query_block):
        scores = low_back(jnp.einsum('qhd,khd->hqk', query_block, key_rows, precision=highest) * score_scale)
        row_top = lax.optimization_barrier(jnp.max(scores, axis=-1, keepdims=True))
        exponent = jnp.exp(scores - row_top)
        attn_probs = low(exponent / lax.optimization_barrier(jnp.sum(exponent, axis=-1, keepdims=True)))
        return jnp.einsum('hqk,khd->qhd', attn_probs, values, precision=highest)
    attended = lax.map(jax.checkpoint(attend_block), queries.reshape(LEN // block_rows, block_rows, HEADS, HEAD_DIM))
    mixed_tok = low_back(low(attended.reshape(LEN, HEADS * HEAD_DIM)))
    middle = source + low_back(jnp.dot(mixed_tok, w_out, precision=highest))
    input_b = low(norm_rows(middle) * (1.0 + scale_b) + shift_b)
    upper = low_back(jnp.dot(input_b, w_up, precision=highest))
    hidden = low(jax.nn.gelu(upper, approximate=False))
    return middle + jnp.dot(hidden, w_down, precision=highest)

def reference(tokens, noise_steps, w_qkv, w_out, w_up, w_down, w_time, cotangent):
    weights = (w_qkv.astype(jnp.float32), w_out.astype(jnp.float32), w_up.astype(jnp.float32), w_down.astype(jnp.float32), w_time.astype(jnp.float32))

    def per_sequence(running, item_in):
        seq_tokens, noise_step, cot_seq = item_in

        def forward_only(source, qkv_in, out_in, up_in, down_in, time_in):
            return layer_forward(source, noise_step, qkv_in, out_in, up_in, down_in, time_in)
        layer_out, pullback = jax.vjp(forward_only, seq_tokens.astype(jnp.float32), weights[0], weights[1], weights[2], weights[3], weights[4])
        gradients = pullback(cot_seq.astype(jnp.float32))
        running = tuple((summed + gradient for summed, gradient in zip(running, gradients[1:])))
        return (running, (layer_out.astype(jnp.bfloat16), gradients[0]))
    zero_grads = tuple((jnp.zeros(weight.shape, jnp.float32) for weight in weights))
    totals, (outputs, grad_input) = lax.scan(per_sequence, zero_grads, (tokens, noise_steps, cotangent))
    return (outputs, grad_input, totals[0], totals[1], totals[2], totals[3], totals[4])
```

```python
from functools import partial
import math

import jax
import jax.numpy as jnp
from jax import lax
from jax.sharding import PartitionSpec as P

HEAD_DIM = 64
TE = 256

highest = lax.Precision.HIGHEST
bf16 = jnp.bfloat16
f32 = jnp.float32


def normalize(values_in):
    centered = values_in - jnp.mean(values_in, axis=-1, keepdims=True)
    inverse = lax.rsqrt(jnp.mean(centered * centered, axis=-1, keepdims=True) + 1e-05)
    return (centered * inverse, inverse)


def norm_back(gradient, normed, inverse):
    return inverse * (
        gradient
        - jnp.mean(gradient, axis=-1, keepdims=True)
        - normed * jnp.mean(gradient * normed, axis=-1, keepdims=True)
    )


def time_embedding(noise_step):
    half_dim = TE // 2
    frequency = jnp.exp(-math.log(10000.0) * jnp.arange(half_dim, dtype=f32) / half_dim)
    angles = noise_step.astype(f32)[..., None] * frequency
    return jnp.concatenate([jnp.sin(angles), jnp.cos(angles)], axis=-1)


def rotate(values_in, positions, direction):
    half_dim = values_in.shape[-1] // 2
    frequency = jnp.exp(-math.log(10000.0) * jnp.arange(half_dim, dtype=f32) / half_dim)
    angles = positions[:, None, None] * frequency
    cosine = jnp.cos(angles)
    sine_wave = direction * jnp.sin(angles)
    first_half = values_in[..., :half_dim]
    second_half = values_in[..., half_dim:]
    return jnp.concatenate(
        [
            first_half * cosine - second_half * sine_wave,
            first_half * sine_wave + second_half * cosine,
        ],
        axis=-1,
    )


def hop(values_in, bit):
    count = lax.axis_size("dp")
    return lax.ppermute(values_in, "dp", [(i, i ^ bit) for i in range(count)])


def core_groups():
    count = lax.axis_size("dp")
    return [[i for i in range(count) if i % 2 == core] for core in range(2)]


def gather_chips(block):
    chips = lax.axis_size("dp") // 2
    if chips != 4:
        return lax.all_gather(block, "dp", axis=0, tiled=True, axis_index_groups=core_groups())
    rows = block.shape[0]
    half = rows // 2
    chip = lax.axis_index("dp") // 2
    from_x = hop(block, 2)
    from_y = hop(block, 4)
    far_top = hop(from_y[:half], 2)
    far_low = hop(from_x[half:], 4)
    out = jnp.zeros((chips * rows,) + block.shape[1:], block.dtype)
    for piece, other, shift in (
        (block, 0, 0),
        (from_x, 1, 0),
        (from_y, 2, 0),
        (far_top, 3, 0),
        (far_low, 3, half),
    ):
        out = lax.dynamic_update_slice_in_dim(out, piece, (chip ^ other) * rows + shift, axis=0)
    return out


def scatter_chips(parts):
    chips = lax.axis_size("dp") // 2
    if chips != 4:
        flat = parts.reshape((-1,) + parts.shape[2:])
        return lax.psum_scatter(
            flat, "dp", scatter_dimension=0, tiled=True, axis_index_groups=core_groups()
        ).astype(f32)
    half = parts.shape[1] // 2
    chip = lax.axis_index("dp") // 2
    own, to_x, to_y, to_far = [
        lax.dynamic_index_in_dim(parts, chip ^ other, 0, keepdims=False) for other in range(4)
    ]
    on_x = hop(to_far[:half], 2)
    on_y = hop(to_far[half:], 4)
    to_y = jnp.concatenate([to_y[:half] + on_x, to_y[half:]], axis=0)
    to_x = jnp.concatenate([to_x[:half], to_x[half:] + on_y], axis=0)
    return own.astype(f32) + hop(to_x, 2).astype(f32) + hop(to_y, 4).astype(f32)


def both_cores(half_block):
    chips = lax.axis_size("dp") // 2
    core = lax.axis_index("dp") % 2
    other = hop(half_block, 1)
    shape = (chips, half_block.shape[0] // chips) + half_block.shape[1:]
    mine, theirs = half_block.reshape(shape), other.reshape(shape)
    first = jnp.where(core == 0, mine, theirs)
    second = jnp.where(core == 0, theirs, mine)
    joined = jnp.stack([first, second], axis=1)
    return joined.reshape((-1,) + half_block.shape[1:])


def sum_cores(full):
    count = lax.axis_size("dp")
    core = lax.axis_index("dp") % 2
    view = full.reshape((count // 2, 2, full.shape[0] // count) + full.shape[1:])
    mine = lax.dynamic_index_in_dim(view, core, 1, keepdims=False)
    theirs = lax.dynamic_index_in_dim(view, 1 - core, 1, keepdims=False)
    return (mine.astype(f32) + hop(theirs.astype(bf16), 1).astype(f32)).astype(bf16)


def turn(values_in, step):
    count = lax.axis_size("seq")
    return lax.ppermute(values_in, "seq", [(i, (i + step) % count) for i in range(count)])


def shift(values_in, step):
    count = lax.axis_size("seq")
    return lax.ppermute(
        values_in, "seq", [(i, i + step) for i in range(count) if 0 <= i + step < count]
    )


def gather_seq(block):
    count = lax.axis_size("seq")
    place = lax.axis_index("seq")
    lower, upper = [block], [block]
    for _ in range(count - 1):
        lower.append(shift(lower[-1], 1))
        upper.append(shift(upper[-1], -1))
    return [block] + [
        jnp.where(place + step < count, upper[step], lower[count - step])
        for step in range(1, count)
    ]


def scatter_seq(blocks):
    count = len(blocks)
    right = left = None
    for step in range(1, count):
        going_right = blocks[count - step]
        going_left = blocks[step]
        if right is not None:
            going_right = going_right + right.astype(f32)
            going_left = going_left + left.astype(f32)
        right = shift(going_right.astype(bf16), 1)
        left = shift(going_left.astype(bf16), -1)
    return blocks[0] + right.astype(f32) + left.astype(f32)


def sum_seq(values_in):
    count = lax.axis_size("seq")
    if count != 4:
        return lax.psum(values_in.astype(bf16), "seq").astype(f32)
    place = lax.axis_index("seq")
    inner = lax.ppermute(values_in.astype(bf16), "seq", [(0, 1), (3, 2)])
    pair = values_in + inner.astype(f32)
    across = lax.ppermute(pair.astype(bf16), "seq", [(1, 2), (2, 1)])
    total = pair + across.astype(f32)
    outer = lax.ppermute(total.astype(bf16), "seq", [(1, 0), (2, 3)])
    return jnp.where((place == 0) | (place == 3), outer.astype(f32), total)


def attend_forward(queries, key_rows, values):
    scores = jnp.einsum("qhd,khd->hqk", queries, key_rows, preferred_element_type=f32) / math.sqrt(
        HEAD_DIM
    )
    row_top = jnp.max(scores, axis=-1, keepdims=True)
    exponent = jnp.exp(scores - row_top)
    row_total = jnp.sum(exponent, axis=-1, keepdims=True)
    probs = (exponent / row_total).astype(bf16)
    attended = jnp.einsum("hqk,khd->qhd", probs, values, preferred_element_type=f32)
    return attended.astype(bf16), (row_top + jnp.log(row_total))


def attend_backward(queries, key_rows, values, log_total, grad_attn):
    score_scale = 1.0 / math.sqrt(HEAD_DIM)
    scores = (
        jnp.einsum("qhd,khd->hqk", queries, key_rows, preferred_element_type=f32) * score_scale
    )
    probs = jnp.exp(scores - log_total)
    grad_probs = jnp.einsum("qhd,khd->hqk", grad_attn, values, preferred_element_type=f32)
    grad_scores = (
        probs * (grad_probs - jnp.sum(probs * grad_probs, axis=-1, keepdims=True))
    ).astype(bf16)
    grad_queries = (
        jnp.einsum("hqk,khd->qhd", grad_scores, key_rows, preferred_element_type=f32) * score_scale
    )
    grad_keys = (
        jnp.einsum("hqk,qhd->khd", grad_scores, queries, preferred_element_type=f32) * score_scale
    )
    grad_values = jnp.einsum(
        "hqk,qhd->khd", probs.astype(bf16), grad_attn, preferred_element_type=f32
    )
    return grad_queries.astype(bf16), grad_keys.astype(bf16), grad_values.astype(bf16)


def per_device(tokens, noise_steps, w_qkv, w_out, w_up, w_down, w_time, cotangent):
    dp_count, seq_parts = lax.axis_size("dp"), lax.axis_size("seq")
    chips = dp_count // 2
    core = lax.axis_index("dp") % 2
    place = lax.axis_index("seq")
    _, rows, width = tokens.shape
    group = width // seq_parts
    source = tokens[0]
    cot = cotangent[0]

    token_blocks = gather_seq(source)

    steps_all = lax.all_to_all(
        jnp.broadcast_to(noise_steps.astype(f32), (dp_count,)),
        "dp",
        split_axis=0,
        concat_axis=0,
        tiled=True,
    )
    embed_all = time_embedding(steps_all)
    cond_part = jnp.dot(embed_all, w_time.astype(f32), precision=highest)
    condition = lax.all_to_all(cond_part, "dp", split_axis=0, concat_axis=0, tiled=True).reshape(
        4, width
    )
    scale_a, shift_a, scale_b, shift_b = [condition[i][None, :] for i in range(4)]

    qkv_cols = lax.dynamic_index_in_dim(
        w_qkv.reshape(-1, 3, seq_parts, group), place, 2, keepdims=False
    ).reshape(-1, 3 * group)
    qkv_all = both_cores(gather_chips(qkv_cols))
    unit_view = w_up.reshape(w_up.shape[0], chips, 2, -1)
    up_mine = lax.dynamic_index_in_dim(unit_view, core, 2, keepdims=False).reshape(
        w_up.shape[0], -1
    )
    up_theirs = lax.dynamic_index_in_dim(unit_view, 1 - core, 2, keepdims=False).reshape(
        w_up.shape[0], -1
    )
    up_other = hop(up_theirs, 1)
    up_block = jnp.where(
        core == 0,
        jnp.concatenate([up_mine, up_other], axis=0),
        jnp.concatenate([up_other, up_mine], axis=0),
    )
    up_all = gather_chips(up_block)
    out_all = both_cores(gather_chips(w_out))
    down_all = gather_chips(w_down)
    cot_both = jnp.concatenate([cot, hop(cot, 1)], axis=0)

    full = jnp.concatenate(token_blocks, axis=0).astype(f32)
    normed_a, inverse_a = normalize(full)
    input_a = (normed_a * (1.0 + scale_a) + shift_a).astype(bf16)
    projected = jnp.dot(input_a, qkv_all, preferred_element_type=f32)
    block_place = (place + jnp.arange(seq_parts)) % seq_parts
    positions = (block_place[:, None] * rows + jnp.arange(rows)).reshape(-1).astype(f32)
    head_view = projected.reshape(seq_parts * rows, 3, -1, HEAD_DIM)
    queries = rotate(head_view[:, 0], positions, 1.0).astype(bf16)
    key_rows = rotate(head_view[:, 1], positions, 1.0).astype(bf16)
    values = head_view[:, 2].astype(bf16)
    attended, log_total = attend_forward(queries, key_rows, values)
    attended = attended.reshape(seq_parts, rows, group)
    pieces = [attended[0]] + [turn(attended[s], s) for s in range(1, seq_parts)]
    stacked = jnp.stack(pieces)
    mixed = jnp.concatenate(
        [
            lax.dynamic_index_in_dim(stacked, (place - g) % seq_parts, 0, keepdims=False)
            for g in range(seq_parts)
        ],
        axis=-1,
    )
    middle = source.astype(f32) + jnp.dot(mixed, out_all, preferred_element_type=f32)
    normed_b, inverse_b = normalize(middle)
    input_b = (normed_b * (1.0 + scale_b) + shift_b).astype(bf16)

    input_both = jnp.concatenate([input_b, hop(input_b, 1)], axis=0)
    upper = jnp.dot(input_both, up_all, preferred_element_type=f32)
    grad_hidden = lax.dot_general(
        cot_both, down_all, (((1,), (1,)), ((), ())), preferred_element_type=f32
    )
    hidden, gelu_pull = jax.vjp(partial(jax.nn.gelu, approximate=False), upper)
    hidden = hidden.astype(bf16)
    grad_upper = gelu_pull(grad_hidden)[0].astype(bf16)
    grad_in_part = lax.dot_general(
        grad_upper, up_all, (((1,), (1,)), ((), ())), preferred_element_type=f32
    )
    grad_in_b = grad_in_part[:rows] + hop(grad_in_part[rows:].astype(bf16), 1).astype(f32)
    out_part = jnp.dot(hidden, down_all, preferred_element_type=f32)
    result = (
        middle + out_part[:rows] + hop(out_part[rows:].astype(bf16), 1).astype(f32)
    ).astype(bf16)

    grad_down_part = lax.dot_general(
        hidden, cot_both, (((0,), (0,)), ((), ())), preferred_element_type=f32
    ).astype(bf16)
    grad_up_part = lax.dot_general(
        input_both, grad_upper, (((0,), (0,)), ((), ())), preferred_element_type=f32
    ).astype(bf16)

    grad_scale_b = jnp.sum(grad_in_b * normed_b, axis=0)
    grad_shift_b = jnp.sum(grad_in_b, axis=0)
    grad_middle = cot.astype(f32) + norm_back(grad_in_b * (1.0 + scale_b), normed_b, inverse_b)
    grad_branch = grad_middle.astype(bf16)
    grad_mixed = lax.dot_general(
        grad_branch, out_all, (((1,), (1,)), ((), ())), preferred_element_type=f32
    ).astype(bf16)
    to_heads = grad_mixed.reshape(rows, seq_parts, group)
    grad_pieces = [
        lax.dynamic_index_in_dim(to_heads, (place - s) % seq_parts, 1, keepdims=False)
        for s in range(seq_parts)
    ]
    grad_attn = jnp.concatenate(
        [grad_pieces[0]] + [turn(grad_pieces[s], -s) for s in range(1, seq_parts)], axis=0
    )
    grad_proj_part = lax.dot_general(
        mixed, grad_branch, (((0,), (0,)), ((), ())), preferred_element_type=f32
    )
    grad_q, grad_k, grad_v = attend_backward(
        queries,
        key_rows,
        values,
        log_total,
        grad_attn.reshape(seq_parts * rows, -1, HEAD_DIM),
    )
    grad_q = rotate(grad_q.astype(f32), positions, -1.0).astype(bf16)
    grad_k = rotate(grad_k.astype(f32), positions, -1.0).astype(bf16)
    grad_projected = jnp.stack([grad_q, grad_k, grad_v], axis=1).reshape(seq_parts * rows, -1)
    grad_in_a_part = lax.dot_general(
        grad_projected, qkv_all, (((1,), (1,)), ((), ())), preferred_element_type=f32
    )
    grad_qkv_part = lax.dot_general(
        input_a, grad_projected, (((0,), (0,)), ((), ())), preferred_element_type=f32
    )
    grad_in_a = scatter_seq(
        [grad_in_a_part[s * rows : (s + 1) * rows] for s in range(seq_parts)]
    )
    grad_scale_a = jnp.sum(grad_in_a_part * normed_a, axis=0)
    grad_shift_a = jnp.sum(grad_in_a_part, axis=0)
    grad_tokens = grad_middle + norm_back(
        grad_in_a * (1.0 + scale_a), normed_a[:rows], inverse_a[:rows]
    )

    grad_down = sum_seq(scatter_chips(grad_down_part.reshape(chips, -1, width)))
    grad_up_rows = scatter_chips(grad_up_part.reshape(chips, -1, grad_up_part.shape[1]))
    up_halves = grad_up_rows.reshape(2, -1, grad_up_rows.shape[1])
    keep = lax.dynamic_index_in_dim(up_halves, core, 0, keepdims=False)
    give = lax.dynamic_index_in_dim(up_halves, 1 - core, 0, keepdims=False)
    keep = keep.reshape(keep.shape[0], chips, -1)
    take = hop(give.astype(bf16), 1).astype(f32).reshape(keep.shape)
    grad_up = sum_seq(
        jnp.stack([jnp.where(core == 0, keep, take), jnp.where(core == 0, take, keep)], axis=2)
        .reshape(keep.shape[0], -1)
    )
    grad_proj = sum_seq(scatter_chips(sum_cores(grad_proj_part)))
    grad_qkv_cols = scatter_chips(sum_cores(grad_qkv_part)).astype(bf16)
    qkv_ring = jnp.stack(gather_seq(grad_qkv_cols))
    grad_qkv = jnp.stack(
        [
            lax.dynamic_index_in_dim(qkv_ring, (g - place) % seq_parts, 0, keepdims=False).reshape(
                -1, 3, group
            )
            for g in range(seq_parts)
        ],
        axis=2,
    )
    grad_qkv = grad_qkv.reshape(-1, 3 * width).astype(f32)
    grad_condition = jnp.concatenate([grad_scale_a, grad_shift_a, grad_scale_b, grad_shift_b])
    cond_cols = lax.all_to_all(
        grad_condition.reshape(dp_count, -1), "dp", split_axis=0, concat_axis=0, tiled=True
    )
    cond_sum = cond_cols
    for s in range(1, seq_parts):
        cond_sum = cond_sum + turn(cond_cols, s)
    grad_time = jnp.dot(embed_all.T, cond_sum, precision=highest)
    return (result[None], grad_tokens[None], grad_qkv, grad_proj, grad_up, grad_down, grad_time)


def solution(mesh):
    in_specs = (
        P("dp", "seq", None),
        P("dp"),
        P("dp", None),
        P("dp", None),
        P("dp", None),
        P("dp", None),
        P(None, "dp"),
        P("dp", "seq", None),
    )
    out_specs = (
        P("dp", "seq", None),
        P("dp", "seq", None),
        P("dp", None),
        P("dp", None),
        P("dp", None),
        P("dp", None),
        P(None, "dp"),
    )
    return jax.shard_map(
        per_device, mesh=mesh, in_specs=in_specs, out_specs=out_specs, check_vma=False
    )
```

```python
from functools import partial
import math

import jax
import jax.numpy as jnp
from jax import lax
from jax.experimental import pallas as pl
from jax.experimental.pallas import tpu as pltpu
from jax.sharding import PartitionSpec as P

HEAD_DIM = 64
TE = 256

highest = lax.Precision.HIGHEST
bf16 = jnp.bfloat16
f32 = jnp.float32


def normalize(values_in):
    centered = values_in - jnp.mean(values_in, axis=-1, keepdims=True)
    inverse = lax.rsqrt(jnp.mean(centered * centered, axis=-1, keepdims=True) + 1e-05)
    return (centered * inverse, inverse)


def norm_back(gradient, normed, inverse):
    return inverse * (
        gradient
        - jnp.mean(gradient, axis=-1, keepdims=True)
        - normed * jnp.mean(gradient * normed, axis=-1, keepdims=True)
    )


def time_embedding(noise_step):
    half_dim = TE // 2
    frequency = jnp.exp(-math.log(10000.0) * jnp.arange(half_dim, dtype=f32) / half_dim)
    angles = noise_step.astype(f32)[..., None] * frequency
    return jnp.concatenate([jnp.sin(angles), jnp.cos(angles)], axis=-1)


def rotate(values_in, positions, direction):
    half_dim = values_in.shape[-1] // 2
    frequency = jnp.exp(-math.log(10000.0) * jnp.arange(half_dim, dtype=f32) / half_dim)
    angles = positions[:, None, None] * frequency
    cosine = jnp.cos(angles)
    sine_wave = direction * jnp.sin(angles)
    first_half = values_in[..., :half_dim]
    second_half = values_in[..., half_dim:]
    return jnp.concatenate(
        [
            first_half * cosine - second_half * sine_wave,
            first_half * sine_wave + second_half * cosine,
        ],
        axis=-1,
    )


def hop(values_in, bit):
    count = lax.axis_size("dp")
    return lax.ppermute(values_in, "dp", [(i, i ^ bit) for i in range(count)])


def core_groups():
    count = lax.axis_size("dp")
    return [[i for i in range(count) if i % 2 == core] for core in range(2)]


def gather_chips(block):
    chips = lax.axis_size("dp") // 2
    if chips != 4:
        return lax.all_gather(block, "dp", axis=0, tiled=True, axis_index_groups=core_groups())
    rows = block.shape[0]
    half = rows // 2
    chip = lax.axis_index("dp") // 2
    from_x = hop(block, 2)
    from_y = hop(block, 4)
    far_top = hop(from_y[:half], 2)
    far_low = hop(from_x[half:], 4)
    out = jnp.zeros((chips * rows,) + block.shape[1:], block.dtype)
    for piece, other, shift in (
        (block, 0, 0),
        (from_x, 1, 0),
        (from_y, 2, 0),
        (far_top, 3, 0),
        (far_low, 3, half),
    ):
        out = lax.dynamic_update_slice_in_dim(out, piece, (chip ^ other) * rows + shift, axis=0)
    return out


def scatter_chips(parts):
    chips = lax.axis_size("dp") // 2
    if chips != 4:
        flat = parts.reshape((-1,) + parts.shape[2:])
        return lax.psum_scatter(
            flat, "dp", scatter_dimension=0, tiled=True, axis_index_groups=core_groups()
        ).astype(f32)
    half = parts.shape[1] // 2
    chip = lax.axis_index("dp") // 2
    own, to_x, to_y, to_far = [
        lax.dynamic_index_in_dim(parts, chip ^ other, 0, keepdims=False) for other in range(4)
    ]
    on_x = hop(to_far[:half], 2)
    on_y = hop(to_far[half:], 4)
    to_y = jnp.concatenate([to_y[:half] + on_x, to_y[half:]], axis=0)
    to_x = jnp.concatenate([to_x[:half], to_x[half:] + on_y], axis=0)
    return own.astype(f32) + hop(to_x, 2).astype(f32) + hop(to_y, 4).astype(f32)


def both_cores(half_block):
    chips = lax.axis_size("dp") // 2
    core = lax.axis_index("dp") % 2
    other = hop(half_block, 1)
    shape = (chips, half_block.shape[0] // chips) + half_block.shape[1:]
    mine, theirs = half_block.reshape(shape), other.reshape(shape)
    first = jnp.where(core == 0, mine, theirs)
    second = jnp.where(core == 0, theirs, mine)
    joined = jnp.stack([first, second], axis=1)
    return joined.reshape((-1,) + half_block.shape[1:])


def sum_cores(full):
    count = lax.axis_size("dp")
    core = lax.axis_index("dp") % 2
    view = full.reshape((count // 2, 2, full.shape[0] // count) + full.shape[1:])
    mine = lax.dynamic_index_in_dim(view, core, 1, keepdims=False)
    theirs = lax.dynamic_index_in_dim(view, 1 - core, 1, keepdims=False)
    return (mine.astype(f32) + hop(theirs.astype(bf16), 1).astype(f32)).astype(bf16)


def turn(values_in, step):
    count = lax.axis_size("seq")
    return lax.ppermute(values_in, "seq", [(i, (i + step) % count) for i in range(count)])


def shift(values_in, step):
    count = lax.axis_size("seq")
    return lax.ppermute(
        values_in, "seq", [(i, i + step) for i in range(count) if 0 <= i + step < count]
    )


def gather_seq(block):
    count = lax.axis_size("seq")
    place = lax.axis_index("seq")
    lower, upper = [block], [block]
    for _ in range(count - 1):
        lower.append(shift(lower[-1], 1))
        upper.append(shift(upper[-1], -1))
    return [block] + [
        jnp.where(place + step < count, upper[step], lower[count - step])
        for step in range(1, count)
    ]


def scatter_seq(blocks):
    count = len(blocks)
    right = left = None
    for step in range(1, count):
        going_right = blocks[count - step]
        going_left = blocks[step]
        if right is not None:
            going_right = going_right + right.astype(f32)
            going_left = going_left + left.astype(f32)
        right = shift(going_right.astype(bf16), 1)
        left = shift(going_left.astype(bf16), -1)
    return blocks[0] + right.astype(f32) + left.astype(f32)


def sum_seq(values_in):
    count = lax.axis_size("seq")
    if count != 4:
        return lax.psum(values_in.astype(bf16), "seq").astype(f32)
    place = lax.axis_index("seq")
    inner = lax.ppermute(values_in.astype(bf16), "seq", [(0, 1), (3, 2)])
    pair = values_in + inner.astype(f32)
    across = lax.ppermute(pair.astype(bf16), "seq", [(1, 2), (2, 1)])
    total = pair + across.astype(f32)
    outer = lax.ppermute(total.astype(bf16), "seq", [(1, 0), (2, 3)])
    return jnp.where((place == 0) | (place == 3), outer.astype(f32), total)


def attend_forward(queries, key_rows, values):
    scores = jnp.einsum("qhd,khd->hqk", queries, key_rows, preferred_element_type=f32) / math.sqrt(
        HEAD_DIM
    )
    row_top = jnp.max(scores, axis=-1, keepdims=True)
    exponent = jnp.exp(scores - row_top)
    row_total = jnp.sum(exponent, axis=-1, keepdims=True)
    probs = (exponent / row_total).astype(bf16)
    attended = jnp.einsum("hqk,khd->qhd", probs, values, preferred_element_type=f32)
    return attended.astype(bf16), (row_top + jnp.log(row_total))


def attend_backward(queries, key_rows, values, log_total, grad_attn):
    score_scale = 1.0 / math.sqrt(HEAD_DIM)
    scores = (
        jnp.einsum("qhd,khd->hqk", queries, key_rows, preferred_element_type=f32) * score_scale
    )
    probs = jnp.exp(scores - log_total)
    grad_probs = jnp.einsum("qhd,khd->hqk", grad_attn, values, preferred_element_type=f32)
    grad_scores = (
        probs * (grad_probs - jnp.sum(probs * grad_probs, axis=-1, keepdims=True))
    ).astype(bf16)
    grad_queries = (
        jnp.einsum("hqk,khd->qhd", grad_scores, key_rows, preferred_element_type=f32) * score_scale
    )
    grad_keys = (
        jnp.einsum("hqk,qhd->khd", grad_scores, queries, preferred_element_type=f32) * score_scale
    )
    grad_values = jnp.einsum(
        "hqk,qhd->khd", probs.astype(bf16), grad_attn, preferred_element_type=f32
    )
    return grad_queries.astype(bf16), grad_keys.astype(bf16), grad_values.astype(bf16)


def per_device_any(tokens, noise_steps, w_qkv, w_out, w_up, w_down, w_time, cotangent):
    dp_count, seq_parts = lax.axis_size("dp"), lax.axis_size("seq")
    chips = dp_count // 2
    core = lax.axis_index("dp") % 2
    place = lax.axis_index("seq")
    _, rows, width = tokens.shape
    group = width // seq_parts
    source = tokens[0]
    cot = cotangent[0]

    token_blocks = gather_seq(source)

    steps_all = lax.all_to_all(
        jnp.broadcast_to(noise_steps.astype(f32), (dp_count,)),
        "dp",
        split_axis=0,
        concat_axis=0,
        tiled=True,
    )
    embed_all = time_embedding(steps_all)
    cond_part = jnp.dot(embed_all, w_time.astype(f32), precision=highest)
    condition = lax.all_to_all(cond_part, "dp", split_axis=0, concat_axis=0, tiled=True).reshape(
        4, width
    )
    scale_a, shift_a, scale_b, shift_b = [condition[i][None, :] for i in range(4)]

    qkv_cols = lax.dynamic_index_in_dim(
        w_qkv.reshape(-1, 3, seq_parts, group), place, 2, keepdims=False
    ).reshape(-1, 3 * group)
    qkv_all = both_cores(gather_chips(qkv_cols))
    unit_view = w_up.reshape(w_up.shape[0], chips, 2, -1)
    up_mine = lax.dynamic_index_in_dim(unit_view, core, 2, keepdims=False).reshape(
        w_up.shape[0], -1
    )
    up_theirs = lax.dynamic_index_in_dim(unit_view, 1 - core, 2, keepdims=False).reshape(
        w_up.shape[0], -1
    )
    up_other = hop(up_theirs, 1)
    up_block = jnp.where(
        core == 0,
        jnp.concatenate([up_mine, up_other], axis=0),
        jnp.concatenate([up_other, up_mine], axis=0),
    )
    up_all = gather_chips(up_block)
    out_all = both_cores(gather_chips(w_out))
    down_all = gather_chips(w_down)
    cot_both = jnp.concatenate([cot, hop(cot, 1)], axis=0)

    full = jnp.concatenate(token_blocks, axis=0).astype(f32)
    normed_a, inverse_a = normalize(full)
    input_a = (normed_a * (1.0 + scale_a) + shift_a).astype(bf16)
    projected = jnp.dot(input_a, qkv_all, preferred_element_type=f32)
    block_place = (place + jnp.arange(seq_parts)) % seq_parts
    positions = (block_place[:, None] * rows + jnp.arange(rows)).reshape(-1).astype(f32)
    head_view = projected.reshape(seq_parts * rows, 3, -1, HEAD_DIM)
    queries = rotate(head_view[:, 0], positions, 1.0).astype(bf16)
    key_rows = rotate(head_view[:, 1], positions, 1.0).astype(bf16)
    values = head_view[:, 2].astype(bf16)
    attended, log_total = attend_forward(queries, key_rows, values)
    attended = attended.reshape(seq_parts, rows, group)
    pieces = [attended[0]] + [turn(attended[s], s) for s in range(1, seq_parts)]
    stacked = jnp.stack(pieces)
    mixed = jnp.concatenate(
        [
            lax.dynamic_index_in_dim(stacked, (place - g) % seq_parts, 0, keepdims=False)
            for g in range(seq_parts)
        ],
        axis=-1,
    )
    middle = source.astype(f32) + jnp.dot(mixed, out_all, preferred_element_type=f32)
    normed_b, inverse_b = normalize(middle)
    input_b = (normed_b * (1.0 + scale_b) + shift_b).astype(bf16)

    input_both = jnp.concatenate([input_b, hop(input_b, 1)], axis=0)
    upper = jnp.dot(input_both, up_all, preferred_element_type=f32)
    grad_hidden = lax.dot_general(
        cot_both, down_all, (((1,), (1,)), ((), ())), preferred_element_type=f32
    )
    hidden, gelu_pull = jax.vjp(partial(jax.nn.gelu, approximate=False), upper)
    hidden = hidden.astype(bf16)
    grad_upper = gelu_pull(grad_hidden)[0].astype(bf16)
    grad_in_part = lax.dot_general(
        grad_upper, up_all, (((1,), (1,)), ((), ())), preferred_element_type=f32
    )
    grad_in_b = grad_in_part[:rows] + hop(grad_in_part[rows:].astype(bf16), 1).astype(f32)
    out_part = jnp.dot(hidden, down_all, preferred_element_type=f32)
    result = (
        middle + out_part[:rows] + hop(out_part[rows:].astype(bf16), 1).astype(f32)
    ).astype(bf16)

    grad_down_part = lax.dot_general(
        hidden, cot_both, (((0,), (0,)), ((), ())), preferred_element_type=f32
    ).astype(bf16)
    grad_up_part = lax.dot_general(
        input_both, grad_upper, (((0,), (0,)), ((), ())), preferred_element_type=f32
    ).astype(bf16)

    grad_scale_b = jnp.sum(grad_in_b * normed_b, axis=0)
    grad_shift_b = jnp.sum(grad_in_b, axis=0)
    grad_middle = cot.astype(f32) + norm_back(grad_in_b * (1.0 + scale_b), normed_b, inverse_b)
    grad_branch = grad_middle.astype(bf16)
    grad_mixed = lax.dot_general(
        grad_branch, out_all, (((1,), (1,)), ((), ())), preferred_element_type=f32
    ).astype(bf16)
    to_heads = grad_mixed.reshape(rows, seq_parts, group)
    grad_pieces = [
        lax.dynamic_index_in_dim(to_heads, (place - s) % seq_parts, 1, keepdims=False)
        for s in range(seq_parts)
    ]
    grad_attn = jnp.concatenate(
        [grad_pieces[0]] + [turn(grad_pieces[s], -s) for s in range(1, seq_parts)], axis=0
    )
    grad_proj_part = lax.dot_general(
        mixed, grad_branch, (((0,), (0,)), ((), ())), preferred_element_type=f32
    )
    grad_q, grad_k, grad_v = attend_backward(
        queries,
        key_rows,
        values,
        log_total,
        grad_attn.reshape(seq_parts * rows, -1, HEAD_DIM),
    )
    grad_q = rotate(grad_q.astype(f32), positions, -1.0).astype(bf16)
    grad_k = rotate(grad_k.astype(f32), positions, -1.0).astype(bf16)
    grad_projected = jnp.stack([grad_q, grad_k, grad_v], axis=1).reshape(seq_parts * rows, -1)
    grad_in_a_part = lax.dot_general(
        grad_projected, qkv_all, (((1,), (1,)), ((), ())), preferred_element_type=f32
    )
    grad_qkv_part = lax.dot_general(
        input_a, grad_projected, (((0,), (0,)), ((), ())), preferred_element_type=f32
    )
    grad_in_a = scatter_seq(
        [grad_in_a_part[s * rows : (s + 1) * rows] for s in range(seq_parts)]
    )
    grad_scale_a = jnp.sum(grad_in_a_part * normed_a, axis=0)
    grad_shift_a = jnp.sum(grad_in_a_part, axis=0)
    grad_tokens = grad_middle + norm_back(
        grad_in_a * (1.0 + scale_a), normed_a[:rows], inverse_a[:rows]
    )

    grad_down = sum_seq(scatter_chips(grad_down_part.reshape(chips, -1, width)))
    grad_up_rows = scatter_chips(grad_up_part.reshape(chips, -1, grad_up_part.shape[1]))
    up_halves = grad_up_rows.reshape(2, -1, grad_up_rows.shape[1])
    keep = lax.dynamic_index_in_dim(up_halves, core, 0, keepdims=False)
    give = lax.dynamic_index_in_dim(up_halves, 1 - core, 0, keepdims=False)
    keep = keep.reshape(keep.shape[0], chips, -1)
    take = hop(give.astype(bf16), 1).astype(f32).reshape(keep.shape)
    grad_up = sum_seq(
        jnp.stack([jnp.where(core == 0, keep, take), jnp.where(core == 0, take, keep)], axis=2)
        .reshape(keep.shape[0], -1)
    )
    grad_proj = sum_seq(scatter_chips(sum_cores(grad_proj_part)))
    grad_qkv_cols = scatter_chips(sum_cores(grad_qkv_part)).astype(bf16)
    qkv_ring = jnp.stack(gather_seq(grad_qkv_cols))
    grad_qkv = jnp.stack(
        [
            lax.dynamic_index_in_dim(qkv_ring, (g - place) % seq_parts, 0, keepdims=False).reshape(
                -1, 3, group
            )
            for g in range(seq_parts)
        ],
        axis=2,
    )
    grad_qkv = grad_qkv.reshape(-1, 3 * width).astype(f32)
    grad_condition = jnp.concatenate([grad_scale_a, grad_shift_a, grad_scale_b, grad_shift_b])
    cond_cols = lax.all_to_all(
        grad_condition.reshape(dp_count, -1), "dp", split_axis=0, concat_axis=0, tiled=True
    )
    cond_sum = cond_cols
    for s in range(1, seq_parts):
        cond_sum = cond_sum + turn(cond_cols, s)
    grad_time = jnp.dot(embed_all.T, cond_sum, precision=highest)
    return (result[None], grad_tokens[None], grad_qkv, grad_proj, grad_up, grad_down, grad_time)


NT = (((1,), (1,)), ((), ()))
TN = (((0,), (0,)), ((), ()))
VMEM = pl.BlockSpec(memory_space=pltpu.VMEM)
SMEM = pl.BlockSpec(memory_space=pltpu.SMEM)
LANES = 128


def call(kernel, name, outs, me, *operands, scratch=(), flops=10**8, limit=40):
    moved = sum(x.size * x.dtype.itemsize for x in operands)
    return pl.pallas_call(
        kernel,
        name=name,
        out_shape=[jax.ShapeDtypeStruct(shape, kind) for shape, kind in outs],
        in_specs=[SMEM] + [VMEM] * len(operands),
        out_specs=[VMEM] * len(outs),
        scratch_shapes=list(scratch),
        compiler_params=pltpu.CompilerParams(vmem_limit_bytes=limit * 2**20),
        cost_estimate=pl.CostEstimate(flops=flops, bytes_accessed=moved, transcendentals=0),
    )(me, *operands)


def dot(left, right, dims=(((1,), (0,)), ((), ()))):
    return lax.dot_general(left, right, dims, preferred_element_type=f32)


def lanes(start, size):
    return pl.ds(pl.multiple_of(start, LANES), size)


def partner(values_in):
    half = HEAD_DIM // 2
    lane = lax.broadcasted_iota(jnp.int32, values_in.shape, 1)
    return jnp.where(
        lane % HEAD_DIM < half,
        pltpu.roll(values_in, values_in.shape[1] - half, 1),
        pltpu.roll(values_in, half, 1),
    )


def pack_kernel(me, w_qkv, w_out, w_up, first, up_keep, up_give):
    core, place = me[1], me[2]
    width = w_out.shape[1]
    group = width // 4
    for part in range(3):
        first[:, part * group : (part + 1) * group] = w_qkv[
            :, lanes(part * width + place * group, group)
        ]
    first[:, 3 * group :] = w_out[...]
    units = w_up.shape[1] // 8
    for chip in range(4):
        at = slice(chip * units, (chip + 1) * units)
        up_keep[:, at] = w_up[:, lanes((2 * chip + core) * units, units)]
        up_give[:, at] = w_up[:, lanes((2 * chip + 1 - core) * units, units)]


def pack_ffn_kernel(me, keep, take, w_down, out):
    core = me[1]
    rows, half = keep.shape[0], keep.shape[1] // 2
    for j in range(2):
        at = slice(j * half, (j + 1) * half)
        out[lanes(2 * j * rows + core * rows, rows), :] = keep[:, at]
        out[lanes(2 * j * rows + (1 - core) * rows, rows), :] = take[:, at]
    out[4 * rows :, :] = w_down[...]


def unpack_kernel(me, *refs):
    qkv_all, out_all = refs[-2:]
    chip, core = me[0], me[1]
    rows = refs[0].shape[0]
    cut = qkv_all.shape[1]
    for side in range(2):
        owner = core if side == 0 else 1 - core
        own, on_x, on_y, top, low = refs[5 * side : 5 * side + 5]
        for piece, other, start in (
            (own, 0, 0),
            (on_x, 1, 0),
            (on_y, 2, 0),
            (top, 3, 0),
            (low, 3, rows // 2),
        ):
            at = pl.ds(
                pl.multiple_of(((chip ^ other) * 2 + owner) * rows + start, rows // 2),
                piece.shape[0],
            )
            qkv_all[at, :] = piece[:, :cut]
            out_all[at, :] = piece[:, cut:]


def qkv_kernel(me, *refs):
    blocks = refs[:7]
    scale, shift, weight, cosine, sine, normed, input_a, q_out, k_out, v_out = refs[7:]
    place = me[2]
    rows, group = blocks[0].shape[0], q_out.shape[1]
    for s in range(4):
        at = slice(s * rows, (s + 1) * rows)
        block = blocks[0][...].astype(f32)
        if s:
            block = jnp.where(
                place + s < 4, blocks[s][...].astype(f32), blocks[7 - s][...].astype(f32)
            )
        centred, _ = normalize(block)
        normed[at, :] = centred
        low = (centred * (1.0 + scale[...]) + shift[...]).astype(bf16)
        input_a[at, :] = low
        for part, out in enumerate((q_out, k_out, v_out)):
            projected = dot(low, weight[:, part * group : (part + 1) * group])
            if part == 2:
                out[at, :] = projected.astype(bf16)
                continue
            for j in range(0, group, LANES):
                piece = projected[:, j : j + LANES]
                piece = piece * cosine[at, :] + partner(piece) * sine[at, :]
                if part == 0:
                    piece = piece * (1.0 / math.sqrt(HEAD_DIM))
                out[at, j : j + LANES] = piece.astype(bf16)


def attend_kernel(me, queries, keys, values, out, log_total):
    count, group = queries.shape
    step = 512
    lane = lax.broadcasted_iota(jnp.int32, (step, LANES), 1)
    for i in range(0, count, step):
        at = slice(i, i + step)
        stats = jnp.zeros((step, LANES), f32)
        for j in range(group // LANES):
            cols = slice(j * LANES, (j + 1) * LANES)
            halves = []
            for side in range(2):
                query = jnp.where(
                    lane // HEAD_DIM == side, queries[at, cols], jnp.zeros((), bf16)
                )
                scores = dot(query, keys[:, cols], NT)
                top = jnp.max(scores, axis=1, keepdims=True)
                exponent = jnp.exp(scores - top)
                total = jnp.sum(exponent, axis=1, keepdims=True)
                halves.append(dot(exponent.astype(bf16), values[:, cols]) / total)
                stats = jnp.where(lane == 2 * j + side, top + jnp.log(total), stats)
            out[at, cols] = jnp.where(lane < HEAD_DIM, halves[0], halves[1]).astype(bf16)
        log_total[:, at] = jnp.transpose(stats)[:8]


def attend_back_kernel(
    me, queries, keys, values, g0, g1, g2, g3, log_total, cosine, sine, out, key_sum, value_sum, query_t
):
    count, group = queries.shape
    step = 512
    rows = g0.shape[0]
    pieces = (g0, g1, g2, g3)
    keys_t = jnp.transpose(keys[...])
    lane = lax.broadcasted_iota(jnp.int32, (step, LANES), 1)
    for j in range(group // LANES):
        cols = slice(j * LANES, (j + 1) * LANES)
        for i in range(0, count, step):
            at = slice(i, i + step)
            grad = jnp.concatenate(
                [pieces[(i + n) // rows][:, cols] for n in range(0, step, rows)], axis=0
            )
            for side in range(2):
                head = 2 * j + side
                mine = slice(head * HEAD_DIM, (head + 1) * HEAD_DIM)
                keep = lane // HEAD_DIM == side
                query = jnp.where(keep, queries[at, cols], jnp.zeros((), bf16))
                grad_mine = jnp.where(keep, grad, jnp.zeros((), bf16))
                probs = jnp.exp(dot(keys[:, cols], query, NT) - log_total[head : head + 1, at])
                grad_probs = dot(values[:, cols], grad_mine, NT)
                delta = jnp.sum(probs * grad_probs, axis=0, keepdims=True)
                grad_scores = (probs * (grad_probs - delta)).astype(bf16)
                value_part = dot(probs.astype(bf16), grad_mine)
                key_part = dot(grad_scores, query)
                if i == 0 and side == 0:
                    value_sum[...] = value_part
                    key_sum[...] = key_part
                else:
                    value_sum[...] += value_part
                    key_sum[...] += key_part
                query_t[mine, at] = dot(keys_t[mine], grad_scores)
        turned = key_sum[...]
        turned = turned * cosine[...] - partner(turned) * sine[...]
        out[:, group + j * LANES : group + (j + 1) * LANES] = turned.astype(bf16)
        out[:, 2 * group + j * LANES : 2 * group + (j + 1) * LANES] = value_sum[...].astype(bf16)
        turned = jnp.transpose(query_t[cols, :]) * (1.0 / math.sqrt(HEAD_DIM))
        turned = turned * cosine[...] - partner(turned) * sine[...]
        out[:, cols] = turned.astype(bf16)


def middle_kernel(
    me, source, p0, p1, p2, p3, out_all, scale, shift, mixed, middle, input_b, keep, give
):
    core, place = me[1], me[2]
    group = p0.shape[1]
    for s, piece in enumerate((p0, p1, p2, p3)):
        mixed[:, lanes(lax.rem(place - s + 4, 4) * group, group)] = piece[...]
    value = source[...].astype(f32) + dot(mixed[...], out_all[...])
    middle[...] = value
    normed, _ = normalize(value)
    input_b[...] = (normed * (1.0 + scale[...]) + shift[...]).astype(bf16)
    part = out_all.shape[0] // 8
    for chip in range(4):
        at = slice(chip * part, (chip + 1) * part)
        keep[:, at] = mixed[:, lanes((2 * chip + core) * part, part)]
        give[:, at] = mixed[:, lanes((2 * chip + 1 - core) * part, part)]


def ffn_kernel(
    me, in_own, in_other, cot_own, cot_other, own, on_x, on_y, top, low,
    out_own, out_give, grad_own, grad_give, hidden, grad_upper, out_sum, grad_sum,
):
    chip = me[0]
    rows, width = in_own.shape
    units = low.shape[0]
    depth = top.shape[0] // 2
    inputs = jnp.concatenate([in_own[...], in_other[...]], axis=0)
    cot = jnp.concatenate([cot_own[...], cot_other[...]], axis=0)
    for r, block in enumerate((own, on_x, on_y, low)):
        owner = chip ^ r
        at = (pl.ds(pl.multiple_of((owner // 2) * depth, depth), depth), lanes((owner % 2) * units, units))
        upper = None
        for r2, up in enumerate((own, on_x, on_y, top)):
            left = jnp.concatenate(
                [ref[:, lanes((chip ^ r2) * depth, depth)] for ref in (in_own, in_other)], axis=0
            )
            term = dot(left, up[at])
            upper = term if upper is None else upper + term
        bell = 0.5 + 0.5 * lax.erf(upper * math.sqrt(0.5))
        value = (upper * bell).astype(bf16)
        slope = bell + upper * jnp.exp(upper * upper * -0.5) * (1.0 / math.sqrt(2.0 * math.pi))
        down = block[...] if r == 3 else block[2 * depth :, :]
        grad = (dot(cot, down, NT) * slope).astype(bf16)
        hidden[:, r * units : (r + 1) * units] = value
        grad_upper[:, lanes(owner * units, units)] = grad
        term = dot(value, down)
        if r:
            out_sum[...] += term
        else:
            out_sum[...] = term
        for r2, up in enumerate((own, on_x, on_y, top)):
            cols = lanes((chip ^ r2) * depth, depth)
            term = dot(grad, up[at], NT)
            if r:
                grad_sum[:, cols] += term
            else:
                grad_sum[:, cols] = term
    out_own[...] = out_sum[:rows, :]
    out_give[...] = out_sum[rows:, :].astype(bf16)
    grad_own[...] = grad_sum[:rows, :]
    grad_give[...] = grad_sum[rows:, :].astype(bf16)


def grad_down_kernel(me, hidden, cot_own, cot_other, send_x, send_y, late_x, late_y, own):
    rows = cot_own.shape[0]
    units = own.shape[0]
    half = units // 2

    def block(r):
        cols = slice(r * units, (r + 1) * units)
        return dot(hidden[:rows, cols], cot_own[...], TN) + dot(
            hidden[rows:, cols], cot_other[...], TN
        )

    across = block(3).astype(bf16)
    send_x[:half, :] = across[:half]
    send_y[:half, :] = across[half:]
    on_x = block(1).astype(bf16)
    send_x[half:, :] = on_x[:half]
    late_x[...] = on_x[half:]
    on_y = block(2).astype(bf16)
    send_y[half:, :] = on_y[half:]
    late_y[...] = on_y[:half]
    own[...] = block(0)


def grad_up_kernel(
    me, in_own, in_other, grad_upper, mixed_own, mixed_other, branch_own, branch_other,
    send_x, send_y, late_x, late_y, own,
):
    chip = me[0]
    rows, width = in_own.shape
    depth = width // 4
    part = mixed_own.shape[1] // 4
    half = part // 2

    def block(r):
        cols = lanes((chip ^ r) * depth, depth)
        up = dot(in_own[:, cols], grad_upper[:rows, :], TN) + dot(
            in_other[:, cols], grad_upper[rows:, :], TN
        )
        cols = lanes((chip ^ r) * part, part)
        proj = dot(mixed_own[:, cols], branch_own[...], TN) + dot(
            mixed_other[:, cols], branch_other[...], TN
        )
        return (up[:, :width], proj[:half]), (up[:, width:], proj[half:])

    def put(ref, slot, count, pair):
        ref[slot * depth : (slot + 1) * depth, :] = pair[0].astype(ref.dtype)
        at = count * depth + slot * half
        ref[at : at + half, :] = pair[1].astype(ref.dtype)

    top, low = block(3)
    put(send_x, 0, 2, top)
    put(send_y, 0, 2, low)
    top, low = block(1)
    put(send_x, 1, 2, top)
    put(late_x, 0, 1, low)
    top, low = block(2)
    put(late_y, 0, 1, top)
    put(send_y, 1, 2, low)
    top, low = block(0)
    put(own, 0, 2, top)
    put(own, 1, 2, low)


def back_b_kernel(
    me, grad_own, grad_take, out_own, out_take, middle, cot, scale, out_all,
    result, grad_middle, branch, sums, g0, g1, g2, g3,
):
    place = me[2]
    group = g0.shape[1]
    result[...] = (middle[...] + out_own[...] + out_take[...].astype(f32)).astype(bf16)
    normed, inverse = normalize(middle[...])
    grad_in = grad_own[...] + grad_take[...].astype(f32)
    sums[0:1, :] = jnp.sum(grad_in * normed, axis=0, keepdims=True)
    sums[1:2, :] = jnp.sum(grad_in, axis=0, keepdims=True)
    grad = cot[...].astype(f32) + norm_back(grad_in * (1.0 + scale[...]), normed, inverse)
    grad_middle[...] = grad
    low = grad.astype(bf16)
    branch[...] = low
    for s, piece in enumerate((g0, g1, g2, g3)):
        at = pl.ds(pl.multiple_of(lax.rem(place - s + 4, 4) * group, group), group)
        piece[...] = dot(low, out_all[at, :], NT).astype(bf16)


def back_a_kernel(me, grad_projected, weight, normed, own, right, left, across, sums):
    rows = own.shape[0]
    first = second = None
    for s, out in ((3, right), (1, left), (2, across), (0, own)):
        at = slice(s * rows, (s + 1) * rows)
        grad = dot(grad_projected[at, :], weight[...], NT)
        out[...] = grad.astype(out.dtype)
        one = jnp.sum(grad * normed[at, :], axis=0, keepdims=True)
        two = jnp.sum(grad, axis=0, keepdims=True)
        first, second = (one, two) if first is None else (first + one, second + two)
    sums[0:1, :] = first
    sums[1:2, :] = second


def grad_qkv_kernel(me, input_a, grad_projected, keep, give):
    core = me[1]
    part = keep.shape[0] // 4
    for out, owner in ((give, 1 - core), (keep, core)):
        for chip in range(4):
            cols = lanes((2 * chip + owner) * part, part)
            out[chip * part : (chip + 1) * part, :] = dot(
                input_a[:, cols], grad_projected[...], TN
            ).astype(out.dtype)


def pair_kernel(me, keep, take, send_x, send_y, late_x, late_y, own):
    chip = me[0]
    part = own.shape[0]
    half = part // 2

    def block(r, low):
        at = pl.ds(pl.multiple_of((chip ^ r) * part + low * half, half), half)
        return keep[at, :] + take[at, :].astype(f32)

    send_x[:half, :] = block(3, 0).astype(bf16)
    send_x[half:, :] = block(1, 0).astype(bf16)
    send_y[:half, :] = block(3, 1).astype(bf16)
    send_y[half:, :] = block(2, 1).astype(bf16)
    late_x[...] = block(1, 1).astype(bf16)
    late_y[...] = block(2, 0).astype(bf16)
    own[:half, :] = block(0, 0)
    own[half:, :] = block(0, 1)


def tokens_kernel(me, own, right, left, source, scale, grad_middle, out):
    grad_in = own[...] + right[...].astype(f32) + left[...].astype(f32)
    normed, inverse = normalize(source[...].astype(f32))
    out[...] = grad_middle[...] + norm_back(grad_in * (1.0 + scale[...]), normed, inverse)


def finish_qkv_kernel(me, p0, p1, p2, p3, out):
    place = me[2]
    group = p0.shape[1] // 3
    width = out.shape[1] // 3
    for s, piece in enumerate((p0, p1, p2, p3)):
        for part in range(3):
            at = part * width + lax.rem(place - s + 4, 4) * group
            out[:, lanes(at, group)] = piece[:, part * group : (part + 1) * group].astype(f32)


def finish_up_kernel(me, inner0, inner1, outer0, outer1, up, proj):
    core, place = me[1], me[2]
    rows = up.shape[0]
    units = up.shape[1] // 8
    ends = (place == 0) | (place == 3)
    total = [
        jnp.where(ends, outer[...].astype(f32), inner[...])
        for inner, outer in ((inner0, outer0), (inner1, outer1))
    ]
    for half in range(2):
        for side, owner in ((0, core), (1, 1 - core)):
            for n in range(2):
                up[:, lanes((2 * (2 * half + n) + owner) * units, units)] = total[half][
                    side * rows : (side + 1) * rows, n * units : (n + 1) * units
                ]
        proj[half * (rows // 2) : (half + 1) * (rows // 2), :] = total[half][2 * rows :, :]


def after(values_in, *others):
    return lax.optimization_barrier((values_in,) + others)[0]


def relay_sums(send_x, send_y, late_x, late_y, own, splits):
    got_x, got_y = hop(send_x, 2), hop(send_y, 4)
    far_x, far_y, near_x, near_y, at = [], [], [], [], 0
    for size in splits:
        far_x.append(got_x[at : at + size])
        far_y.append(got_y[at : at + size])
        near_x.append(got_x[at + size : at + 2 * size])
        near_y.append(got_y[at + size : at + 2 * size])
        at += 2 * size
    join = partial(jnp.concatenate, axis=0)
    next_x = (late_x.astype(f32) + join(far_y).astype(f32)).astype(bf16)
    next_y = (late_y.astype(f32) + join(far_x).astype(f32)).astype(bf16)
    last_x, last_y = hop(next_x, 2), hop(next_y, 4)
    out, at, seen = [], 0, 0
    for n, size in enumerate(splits):
        top = own[at : at + size] + near_x[n].astype(f32) + last_y[seen : seen + size].astype(f32)
        low = (
            own[at + size : at + 2 * size]
            + near_y[n].astype(f32)
            + last_x[seen : seen + size].astype(f32)
        )
        out.append((top, low))
        at += 2 * size
        seen += size
    return out, (got_x, got_y)


def line_sum(values_in):
    inner = lax.ppermute(values_in.astype(bf16), "seq", [(0, 1), (3, 2)])
    pair = values_in + inner.astype(f32)
    across = lax.ppermute(pair.astype(bf16), "seq", [(1, 2), (2, 1)])
    total = pair + across.astype(f32)
    return total, lax.ppermute(total.astype(bf16), "seq", [(1, 0), (2, 3)])


def per_device(tokens, noise_steps, w_qkv, w_out, w_up, w_down, w_time, cotangent):
    index, place = lax.axis_index("dp"), lax.axis_index("seq")
    me = jnp.stack([index // 2, index % 2, place]).astype(jnp.int32)
    core = index % 2
    _, rows, width = tokens.shape
    group = width // 4
    count = 4 * rows
    hidden_units = w_up.shape[1]
    part = w_out.shape[0]
    source, cot = tokens[0], cotangent[0]

    upper1, lower1 = shift(source, -1), shift(source, 1)
    first, up_keep, up_give = call(
        pack_kernel,
        "pack",
        [((part, 3 * group + width), bf16)] + [((part, hidden_units // 2), bf16)] * 2,
        me,
        w_qkv,
        w_out,
        w_up,
    )
    first_x, first_y = hop(first, 2), hop(first, 4)
    up_take = hop(up_give, 1)
    cot_other = hop(cot, 1)
    (ffn,) = call(
        pack_ffn_kernel,
        "pack_ffn",
        [((4 * part + w_down.shape[0], hidden_units // 4), bf16)],
        me,
        up_keep,
        up_take,
        w_down,
    )
    steps_all = lax.all_to_all(
        jnp.broadcast_to(noise_steps.astype(f32), (8,)),
        "dp",
        split_axis=0,
        concat_axis=0,
        tiled=True,
    )
    embed_all = time_embedding(steps_all)
    cond_part = jnp.dot(embed_all, w_time.astype(f32), precision=highest)
    condition = lax.all_to_all(cond_part, "dp", split_axis=0, concat_axis=0, tiled=True).reshape(
        4, width
    )
    scale_a, shift_a, scale_b, shift_b = [condition[i : i + 1] for i in range(4)]
    upper1, lower1, first_x, first_y = lax.optimization_barrier(
        (upper1, lower1, first_x, first_y)
    )
    upper2, lower2 = shift(upper1, -1), shift(lower1, 1)
    first_top, first_low = hop(first_y[: part // 2], 2), hop(first_x[part // 2 :], 4)
    ffn = after(ffn, first_x)
    ffn_x, ffn_y = hop(ffn, 2), hop(ffn, 4)
    upper2, lower2, first_top, first_low = lax.optimization_barrier(
        (upper2, lower2, first_top, first_low)
    )
    upper3, lower3 = shift(upper2, -1), shift(lower2, 1)
    mine = (first, first_x, first_y, first_top, first_low)
    theirs = [hop(piece, 1) for piece in mine]
    qkv_all, out_all = call(
        unpack_kernel,
        "unpack",
        [((width, 3 * group), bf16), ((width, width), bf16)],
        me,
        *mine,
        *theirs,
    )
    half = HEAD_DIM // 2
    frequency = jnp.exp(-math.log(10000.0) * jnp.arange(half, dtype=f32) / half)
    block_place = (place + jnp.arange(4)) % 4
    positions = (block_place[:, None] * rows + jnp.arange(rows)).reshape(-1).astype(f32)
    angles = positions[:, None] * frequency
    cosine, sine = jnp.cos(angles), jnp.sin(angles)
    cosine = jnp.concatenate([cosine] * 4, axis=1)
    sine = jnp.concatenate([-sine, sine] * 2, axis=1)

    normed_a, input_a, queries, keys, values = call(
        qkv_kernel,
        "qkv",
        [((count, width), f32), ((count, width), bf16)] + [((count, group), bf16)] * 3,
        me,
        source,
        upper1,
        upper2,
        upper3,
        lower1,
        lower2,
        lower3,
        scale_a,
        shift_a,
        qkv_all,
        cosine,
        sine,
        flops=6 * count * width * group,
    )
    attended, log_total = call(
        attend_kernel,
        "attend",
        [((count, group), bf16), ((8, count), f32)],
        me,
        queries,
        keys,
        values,
        flops=16 * count * count * group,
    )
    attended, ffn_x, ffn_y = lax.optimization_barrier((attended, ffn_x, ffn_y))
    cut = ffn.shape[0] // 2
    ffn_top, ffn_low = hop(ffn_y[:cut], 2), hop(ffn_x[cut:], 4)
    pieces = [attended[:rows]] + [
        turn(attended[s * rows : (s + 1) * rows], s) for s in range(1, 4)
    ]
    mixed, middle, input_b, mixed_keep, mixed_give = call(
        middle_kernel,
        "middle",
        [((rows, width), bf16), ((rows, width), f32), ((rows, width), bf16)]
        + [((rows, width // 2), bf16)] * 2,
        me,
        source,
        *pieces,
        out_all,
        scale_b,
        shift_b,
        flops=2 * rows * width * width,
    )
    input_other = hop(input_b, 1)
    mixed_take = hop(mixed_give, 1)

    units = hidden_units // 2
    out_own, out_give, grad_own, grad_give, hidden, grad_upper = call(
        ffn_kernel,
        "ffn",
        [((rows, width), f32), ((rows, width), bf16)] * 2 + [((2 * rows, units), bf16)] * 2,
        me,
        input_b,
        input_other,
        cot,
        cot_other,
        ffn,
        ffn_x,
        ffn_y,
        ffn_top,
        ffn_low,
        scratch=[pltpu.VMEM((2 * rows, width), f32)] * 2,
        flops=16 * rows * width * units,
    )
    grad_take, out_take = hop(grad_give, 1), hop(out_give, 1)
    down_rows = w_down.shape[0]
    down_parts = call(
        grad_down_kernel,
        "grad_down",
        [((down_rows, width), bf16)] * 2
        + [((down_rows // 2, width), bf16)] * 2
        + [((down_rows, width), f32)],
        me,
        hidden,
        cot,
        cot_other,
        flops=4 * rows * width * units,
    )
    down_sums, down_first = relay_sums(*down_parts, (down_rows // 2,))
    result, grad_middle, branch, sums_b, *to_heads = call(
        back_b_kernel,
        "back_b",
        [((rows, width), bf16), ((rows, width), f32), ((rows, width), bf16), ((2, width), f32)]
        + [((rows, group), bf16)] * 4,
        me,
        grad_own,
        grad_take,
        out_own,
        out_take,
        middle,
        cot,
        scale_b,
        out_all,
        flops=2 * rows * width * width,
    )
    grad_heads = [to_heads[0]] + [turn(to_heads[s], -s) for s in range(1, 4)]
    branch_other = hop(branch, 1)
    up_rows = 2 * width // 4 + part
    up_parts = call(
        grad_up_kernel,
        "grad_up",
        [((up_rows, width), bf16)] * 2
        + [((up_rows // 2, width), bf16)] * 2
        + [((up_rows, width), f32)],
        me,
        input_b,
        input_other,
        grad_upper,
        mixed_keep,
        mixed_take,
        branch,
        branch_other,
        flops=4 * rows * width * units,
    )
    up_x, up_y = after(up_parts[0], down_first[0]), after(up_parts[1], down_first[1])
    up_sums, _ = relay_sums(up_x, up_y, *up_parts[2:], (width // 4, part // 2))
    (grad_projected,) = call(
        attend_back_kernel,
        "attend_back",
        [((count, 3 * group), bf16)],
        me,
        queries,
        keys,
        values,
        *grad_heads,
        log_total,
        cosine,
        sine,
        scratch=[pltpu.VMEM((count, LANES), f32)] * 2 + [pltpu.VMEM((group, count), f32)],
        flops=40 * count * count * group,
    )
    grad_a, right, left, across, sums_a = call(
        back_a_kernel,
        "back_a",
        [((rows, width), f32)] + [((rows, width), bf16)] * 2 + [((rows, width), bf16), ((2, width), f32)],
        me,
        grad_projected,
        qkv_all,
        normed_a,
        flops=6 * count * width * group,
    )
    got_right, got_left = shift(right, 1), shift(left, -1)
    keep, give = call(
        grad_qkv_kernel,
        "grad_qkv",
        [((width // 2, 3 * group), f32), ((width // 2, 3 * group), bf16)],
        me,
        input_a,
        grad_projected,
        flops=6 * count * width * group,
    )
    qkv_parts = call(
        pair_kernel,
        "pair",
        [((part, 3 * group), bf16)] * 2
        + [((part // 2, 3 * group), bf16)] * 2
        + [((part, 3 * group), f32)],
        me,
        keep,
        hop(give, 1),
    )
    qkv_sums, _ = relay_sums(*qkv_parts, (part // 2,))
    got_right, got_left = (
        shift((across.astype(f32) + got_right.astype(f32)).astype(bf16), 1),
        shift((across.astype(f32) + got_left.astype(f32)).astype(bf16), -1),
    )
    got_right, got_left = (
        shift((left.astype(f32) + got_right.astype(f32)).astype(bf16), 1),
        shift((right.astype(f32) + got_left.astype(f32)).astype(bf16), -1),
    )
    (grad_tokens,) = call(
        tokens_kernel,
        "tokens",
        [((rows, width), f32)],
        me,
        grad_a,
        got_right,
        got_left,
        source,
        scale_a,
        grad_middle,
    )

    ends = (place == 0) | (place == 3)
    down_lines = [line_sum(piece) for piece in down_sums[0]]
    grad_down = jnp.concatenate(
        [jnp.where(ends, outer.astype(f32), inner) for inner, outer in down_lines], axis=0
    )
    up_lines = []
    for n in range(2):
        rows_both = up_sums[0][n].reshape(2, part, width)
        own_rows = lax.dynamic_index_in_dim(rows_both, core, 0, keepdims=False)
        other_rows = lax.dynamic_index_in_dim(rows_both, 1 - core, 0, keepdims=False)
        taken = hop(other_rows.astype(bf16), 1).astype(f32)
        up_lines.append(line_sum(jnp.concatenate([own_rows, taken, up_sums[1][n]], axis=0)))
    grad_up, grad_proj = call(
        finish_up_kernel,
        "finish_up",
        [((part, hidden_units), f32), ((part, width), f32)],
        me,
        up_lines[0][0],
        up_lines[1][0],
        up_lines[0][1],
        up_lines[1][1],
    )
    qkv_cols = jnp.concatenate(qkv_sums[0], axis=0).astype(bf16)
    (grad_qkv,) = call(
        finish_qkv_kernel,
        "finish_qkv",
        [((part, 3 * width), f32)],
        me,
        qkv_cols,
        *[turn(qkv_cols, s) for s in range(1, 4)],
    )
    grad_condition = jnp.concatenate([sums_a, sums_b], axis=0)
    cond_cols = lax.all_to_all(
        grad_condition.reshape(8, -1), "dp", split_axis=0, concat_axis=0, tiled=True
    )
    cond_sum = cond_cols
    for s in range(1, 4):
        cond_sum = cond_sum + turn(cond_cols, s)
    grad_time = jnp.dot(embed_all.T, cond_sum, precision=highest)
    return (result[None], grad_tokens[None], grad_qkv, grad_proj, grad_up, grad_down, grad_time)


def solution(mesh):
    in_specs = (
        P("dp", "seq", None),
        P("dp"),
        P("dp", None),
        P("dp", None),
        P("dp", None),
        P("dp", None),
        P(None, "dp"),
        P("dp", "seq", None),
    )
    out_specs = (
        P("dp", "seq", None),
        P("dp", "seq", None),
        P("dp", None),
        P("dp", None),
        P("dp", None),
        P("dp", None),
        P(None, "dp"),
    )
    square = mesh.shape["dp"] == 8 and mesh.shape["seq"] == 4
    return jax.shard_map(
        per_device if square else per_device_any, mesh=mesh, in_specs=in_specs, out_specs=out_specs, check_vma=False
    )
```

```python
from functools import partial
import math

import jax
import jax.numpy as jnp
from jax import lax
from jax.experimental import pallas as pl
from jax.experimental.pallas import tpu as pltpu
from jax.sharding import PartitionSpec as P

HEAD_DIM = 64
TE = 256

highest = lax.Precision.HIGHEST
bf16 = jnp.bfloat16
f32 = jnp.float32


def normalize(values_in):
    centered = values_in - jnp.mean(values_in, axis=-1, keepdims=True)
    inverse = lax.rsqrt(jnp.mean(centered * centered, axis=-1, keepdims=True) + 1e-05)
    return (centered * inverse, inverse)


def norm_back(gradient, normed, inverse):
    return inverse * (
        gradient
        - jnp.mean(gradient, axis=-1, keepdims=True)
        - normed * jnp.mean(gradient * normed, axis=-1, keepdims=True)
    )


def time_embedding(noise_step):
    half_dim = TE // 2
    frequency = jnp.exp(-math.log(10000.0) * jnp.arange(half_dim, dtype=f32) / half_dim)
    angles = noise_step.astype(f32)[..., None] * frequency
    return jnp.concatenate([jnp.sin(angles), jnp.cos(angles)], axis=-1)


def rotate(values_in, positions, direction):
    half_dim = values_in.shape[-1] // 2
    frequency = jnp.exp(-math.log(10000.0) * jnp.arange(half_dim, dtype=f32) / half_dim)
    angles = positions[:, None, None] * frequency
    cosine = jnp.cos(angles)
    sine_wave = direction * jnp.sin(angles)
    first_half = values_in[..., :half_dim]
    second_half = values_in[..., half_dim:]
    return jnp.concatenate(
        [
            first_half * cosine - second_half * sine_wave,
            first_half * sine_wave + second_half * cosine,
        ],
        axis=-1,
    )


def hop(values_in, bit):
    count = lax.axis_size("dp")
    return lax.ppermute(values_in, "dp", [(i, i ^ bit) for i in range(count)])


def core_groups():
    count = lax.axis_size("dp")
    return [[i for i in range(count) if i % 2 == core] for core in range(2)]


def gather_chips(block):
    chips = lax.axis_size("dp") // 2
    if chips != 4:
        return lax.all_gather(block, "dp", axis=0, tiled=True, axis_index_groups=core_groups())
    rows = block.shape[0]
    half = rows // 2
    chip = lax.axis_index("dp") // 2
    from_x = hop(block, 2)
    from_y = hop(block, 4)
    far_top = hop(from_y[:half], 2)
    far_low = hop(from_x[half:], 4)
    out = jnp.zeros((chips * rows,) + block.shape[1:], block.dtype)
    for piece, other, shift in (
        (block, 0, 0),
        (from_x, 1, 0),
        (from_y, 2, 0),
        (far_top, 3, 0),
        (far_low, 3, half),
    ):
        out = lax.dynamic_update_slice_in_dim(out, piece, (chip ^ other) * rows + shift, axis=0)
    return out


def scatter_chips(parts):
    chips = lax.axis_size("dp") // 2
    if chips != 4:
        flat = parts.reshape((-1,) + parts.shape[2:])
        return lax.psum_scatter(
            flat, "dp", scatter_dimension=0, tiled=True, axis_index_groups=core_groups()
        ).astype(f32)
    half = parts.shape[1] // 2
    chip = lax.axis_index("dp") // 2
    own, to_x, to_y, to_far = [
        lax.dynamic_index_in_dim(parts, chip ^ other, 0, keepdims=False) for other in range(4)
    ]
    on_x = hop(to_far[:half], 2)
    on_y = hop(to_far[half:], 4)
    to_y = jnp.concatenate([to_y[:half] + on_x, to_y[half:]], axis=0)
    to_x = jnp.concatenate([to_x[:half], to_x[half:] + on_y], axis=0)
    return own.astype(f32) + hop(to_x, 2).astype(f32) + hop(to_y, 4).astype(f32)


def both_cores(half_block):
    chips = lax.axis_size("dp") // 2
    core = lax.axis_index("dp") % 2
    other = hop(half_block, 1)
    shape = (chips, half_block.shape[0] // chips) + half_block.shape[1:]
    mine, theirs = half_block.reshape(shape), other.reshape(shape)
    first = jnp.where(core == 0, mine, theirs)
    second = jnp.where(core == 0, theirs, mine)
    joined = jnp.stack([first, second], axis=1)
    return joined.reshape((-1,) + half_block.shape[1:])


def sum_cores(full):
    count = lax.axis_size("dp")
    core = lax.axis_index("dp") % 2
    view = full.reshape((count // 2, 2, full.shape[0] // count) + full.shape[1:])
    mine = lax.dynamic_index_in_dim(view, core, 1, keepdims=False)
    theirs = lax.dynamic_index_in_dim(view, 1 - core, 1, keepdims=False)
    return (mine.astype(f32) + hop(theirs.astype(bf16), 1).astype(f32)).astype(bf16)


def turn(values_in, step):
    count = lax.axis_size("seq")
    return lax.ppermute(values_in, "seq", [(i, (i + step) % count) for i in range(count)])


def shift(values_in, step):
    count = lax.axis_size("seq")
    return lax.ppermute(
        values_in, "seq", [(i, i + step) for i in range(count) if 0 <= i + step < count]
    )


def gather_seq(block):
    count = lax.axis_size("seq")
    place = lax.axis_index("seq")
    lower, upper = [block], [block]
    for _ in range(count - 1):
        lower.append(shift(lower[-1], 1))
        upper.append(shift(upper[-1], -1))
    return [block] + [
        jnp.where(place + step < count, upper[step], lower[count - step])
        for step in range(1, count)
    ]


def scatter_seq(blocks):
    count = len(blocks)
    right = left = None
    for step in range(1, count):
        going_right = blocks[count - step]
        going_left = blocks[step]
        if right is not None:
            going_right = going_right + right.astype(f32)
            going_left = going_left + left.astype(f32)
        right = shift(going_right.astype(bf16), 1)
        left = shift(going_left.astype(bf16), -1)
    return blocks[0] + right.astype(f32) + left.astype(f32)


def sum_seq(values_in):
    count = lax.axis_size("seq")
    if count != 4:
        return lax.psum(values_in.astype(bf16), "seq").astype(f32)
    place = lax.axis_index("seq")
    inner = lax.ppermute(values_in.astype(bf16), "seq", [(0, 1), (3, 2)])
    pair = values_in + inner.astype(f32)
    across = lax.ppermute(pair.astype(bf16), "seq", [(1, 2), (2, 1)])
    total = pair + across.astype(f32)
    outer = lax.ppermute(total.astype(bf16), "seq", [(1, 0), (2, 3)])
    return jnp.where((place == 0) | (place == 3), outer.astype(f32), total)


def attend_forward(queries, key_rows, values):
    scores = jnp.einsum("qhd,khd->hqk", queries, key_rows, preferred_element_type=f32) / math.sqrt(
        HEAD_DIM
    )
    row_top = jnp.max(scores, axis=-1, keepdims=True)
    exponent = jnp.exp(scores - row_top)
    row_total = jnp.sum(exponent, axis=-1, keepdims=True)
    probs = (exponent / row_total).astype(bf16)
    attended = jnp.einsum("hqk,khd->qhd", probs, values, preferred_element_type=f32)
    return attended.astype(bf16), (row_top + jnp.log(row_total))


def attend_backward(queries, key_rows, values, log_total, grad_attn):
    score_scale = 1.0 / math.sqrt(HEAD_DIM)
    scores = (
        jnp.einsum("qhd,khd->hqk", queries, key_rows, preferred_element_type=f32) * score_scale
    )
    probs = jnp.exp(scores - log_total)
    grad_probs = jnp.einsum("qhd,khd->hqk", grad_attn, values, preferred_element_type=f32)
    grad_scores = (
        probs * (grad_probs - jnp.sum(probs * grad_probs, axis=-1, keepdims=True))
    ).astype(bf16)
    grad_queries = (
        jnp.einsum("hqk,khd->qhd", grad_scores, key_rows, preferred_element_type=f32) * score_scale
    )
    grad_keys = (
        jnp.einsum("hqk,qhd->khd", grad_scores, queries, preferred_element_type=f32) * score_scale
    )
    grad_values = jnp.einsum(
        "hqk,qhd->khd", probs.astype(bf16), grad_attn, preferred_element_type=f32
    )
    return grad_queries.astype(bf16), grad_keys.astype(bf16), grad_values.astype(bf16)


def per_device_any(tokens, noise_steps, w_qkv, w_out, w_up, w_down, w_time, cotangent):
    dp_count, seq_parts = lax.axis_size("dp"), lax.axis_size("seq")
    chips = dp_count // 2
    core = lax.axis_index("dp") % 2
    place = lax.axis_index("seq")
    _, rows, width = tokens.shape
    group = width // seq_parts
    source = tokens[0]
    cot = cotangent[0]

    token_blocks = gather_seq(source)

    steps_all = lax.all_to_all(
        jnp.broadcast_to(noise_steps.astype(f32), (dp_count,)),
        "dp",
        split_axis=0,
        concat_axis=0,
        tiled=True,
    )
    embed_all = time_embedding(steps_all)
    cond_part = jnp.dot(embed_all, w_time.astype(f32), precision=highest)
    condition = lax.all_to_all(cond_part, "dp", split_axis=0, concat_axis=0, tiled=True).reshape(
        4, width
    )
    scale_a, shift_a, scale_b, shift_b = [condition[i][None, :] for i in range(4)]

    qkv_cols = lax.dynamic_index_in_dim(
        w_qkv.reshape(-1, 3, seq_parts, group), place, 2, keepdims=False
    ).reshape(-1, 3 * group)
    qkv_all = both_cores(gather_chips(qkv_cols))
    unit_view = w_up.reshape(w_up.shape[0], chips, 2, -1)
    up_mine = lax.dynamic_index_in_dim(unit_view, core, 2, keepdims=False).reshape(
        w_up.shape[0], -1
    )
    up_theirs = lax.dynamic_index_in_dim(unit_view, 1 - core, 2, keepdims=False).reshape(
        w_up.shape[0], -1
    )
    up_other = hop(up_theirs, 1)
    up_block = jnp.where(
        core == 0,
        jnp.concatenate([up_mine, up_other], axis=0),
        jnp.concatenate([up_other, up_mine], axis=0),
    )
    up_all = gather_chips(up_block)
    out_all = both_cores(gather_chips(w_out))
    down_all = gather_chips(w_down)
    cot_both = jnp.concatenate([cot, hop(cot, 1)], axis=0)

    full = jnp.concatenate(token_blocks, axis=0).astype(f32)
    normed_a, inverse_a = normalize(full)
    input_a = (normed_a * (1.0 + scale_a) + shift_a).astype(bf16)
    projected = jnp.dot(input_a, qkv_all, preferred_element_type=f32)
    block_place = (place + jnp.arange(seq_parts)) % seq_parts
    positions = (block_place[:, None] * rows + jnp.arange(rows)).reshape(-1).astype(f32)
    head_view = projected.reshape(seq_parts * rows, 3, -1, HEAD_DIM)
    queries = rotate(head_view[:, 0], positions, 1.0).astype(bf16)
    key_rows = rotate(head_view[:, 1], positions, 1.0).astype(bf16)
    values = head_view[:, 2].astype(bf16)
    attended, log_total = attend_forward(queries, key_rows, values)
    attended = attended.reshape(seq_parts, rows, group)
    pieces = [attended[0]] + [turn(attended[s], s) for s in range(1, seq_parts)]
    stacked = jnp.stack(pieces)
    mixed = jnp.concatenate(
        [
            lax.dynamic_index_in_dim(stacked, (place - g) % seq_parts, 0, keepdims=False)
            for g in range(seq_parts)
        ],
        axis=-1,
    )
    middle = source.astype(f32) + jnp.dot(mixed, out_all, preferred_element_type=f32)
    normed_b, inverse_b = normalize(middle)
    input_b = (normed_b * (1.0 + scale_b) + shift_b).astype(bf16)

    input_both = jnp.concatenate([input_b, hop(input_b, 1)], axis=0)
    upper = jnp.dot(input_both, up_all, preferred_element_type=f32)
    grad_hidden = lax.dot_general(
        cot_both, down_all, (((1,), (1,)), ((), ())), preferred_element_type=f32
    )
    hidden, gelu_pull = jax.vjp(partial(jax.nn.gelu, approximate=False), upper)
    hidden = hidden.astype(bf16)
    grad_upper = gelu_pull(grad_hidden)[0].astype(bf16)
    grad_in_part = lax.dot_general(
        grad_upper, up_all, (((1,), (1,)), ((), ())), preferred_element_type=f32
    )
    grad_in_b = grad_in_part[:rows] + hop(grad_in_part[rows:].astype(bf16), 1).astype(f32)
    out_part = jnp.dot(hidden, down_all, preferred_element_type=f32)
    result = (
        middle + out_part[:rows] + hop(out_part[rows:].astype(bf16), 1).astype(f32)
    ).astype(bf16)

    grad_down_part = lax.dot_general(
        hidden, cot_both, (((0,), (0,)), ((), ())), preferred_element_type=f32
    ).astype(bf16)
    grad_up_part = lax.dot_general(
        input_both, grad_upper, (((0,), (0,)), ((), ())), preferred_element_type=f32
    ).astype(bf16)

    grad_scale_b = jnp.sum(grad_in_b * normed_b, axis=0)
    grad_shift_b = jnp.sum(grad_in_b, axis=0)
    grad_middle = cot.astype(f32) + norm_back(grad_in_b * (1.0 + scale_b), normed_b, inverse_b)
    grad_branch = grad_middle.astype(bf16)
    grad_mixed = lax.dot_general(
        grad_branch, out_all, (((1,), (1,)), ((), ())), preferred_element_type=f32
    ).astype(bf16)
    to_heads = grad_mixed.reshape(rows, seq_parts, group)
    grad_pieces = [
        lax.dynamic_index_in_dim(to_heads, (place - s) % seq_parts, 1, keepdims=False)
        for s in range(seq_parts)
    ]
    grad_attn = jnp.concatenate(
        [grad_pieces[0]] + [turn(grad_pieces[s], -s) for s in range(1, seq_parts)], axis=0
    )
    grad_proj_part = lax.dot_general(
        mixed, grad_branch, (((0,), (0,)), ((), ())), preferred_element_type=f32
    )
    grad_q, grad_k, grad_v = attend_backward(
        queries,
        key_rows,
        values,
        log_total,
        grad_attn.reshape(seq_parts * rows, -1, HEAD_DIM),
    )
    grad_q = rotate(grad_q.astype(f32), positions, -1.0).astype(bf16)
    grad_k = rotate(grad_k.astype(f32), positions, -1.0).astype(bf16)
    grad_projected = jnp.stack([grad_q, grad_k, grad_v], axis=1).reshape(seq_parts * rows, -1)
    grad_in_a_part = lax.dot_general(
        grad_projected, qkv_all, (((1,), (1,)), ((), ())), preferred_element_type=f32
    )
    grad_qkv_part = lax.dot_general(
        input_a, grad_projected, (((0,), (0,)), ((), ())), preferred_element_type=f32
    )
    grad_in_a = scatter_seq(
        [grad_in_a_part[s * rows : (s + 1) * rows] for s in range(seq_parts)]
    )
    grad_scale_a = jnp.sum(grad_in_a_part * normed_a, axis=0)
    grad_shift_a = jnp.sum(grad_in_a_part, axis=0)
    grad_tokens = grad_middle + norm_back(
        grad_in_a * (1.0 + scale_a), normed_a[:rows], inverse_a[:rows]
    )

    grad_down = sum_seq(scatter_chips(grad_down_part.reshape(chips, -1, width)))
    grad_up_rows = scatter_chips(grad_up_part.reshape(chips, -1, grad_up_part.shape[1]))
    up_halves = grad_up_rows.reshape(2, -1, grad_up_rows.shape[1])
    keep = lax.dynamic_index_in_dim(up_halves, core, 0, keepdims=False)
    give = lax.dynamic_index_in_dim(up_halves, 1 - core, 0, keepdims=False)
    keep = keep.reshape(keep.shape[0], chips, -1)
    take = hop(give.astype(bf16), 1).astype(f32).reshape(keep.shape)
    grad_up = sum_seq(
        jnp.stack([jnp.where(core == 0, keep, take), jnp.where(core == 0, take, keep)], axis=2)
        .reshape(keep.shape[0], -1)
    )
    grad_proj = sum_seq(scatter_chips(sum_cores(grad_proj_part)))
    grad_qkv_cols = scatter_chips(sum_cores(grad_qkv_part)).astype(bf16)
    qkv_ring = jnp.stack(gather_seq(grad_qkv_cols))
    grad_qkv = jnp.stack(
        [
            lax.dynamic_index_in_dim(qkv_ring, (g - place) % seq_parts, 0, keepdims=False).reshape(
                -1, 3, group
            )
            for g in range(seq_parts)
        ],
        axis=2,
    )
    grad_qkv = grad_qkv.reshape(-1, 3 * width).astype(f32)
    grad_condition = jnp.concatenate([grad_scale_a, grad_shift_a, grad_scale_b, grad_shift_b])
    cond_cols = lax.all_to_all(
        grad_condition.reshape(dp_count, -1), "dp", split_axis=0, concat_axis=0, tiled=True
    )
    cond_sum = cond_cols
    for s in range(1, seq_parts):
        cond_sum = cond_sum + turn(cond_cols, s)
    grad_time = jnp.dot(embed_all.T, cond_sum, precision=highest)
    return (result[None], grad_tokens[None], grad_qkv, grad_proj, grad_up, grad_down, grad_time)


NT = (((1,), (1,)), ((), ()))
TN = (((0,), (0,)), ((), ()))
VMEM = pl.BlockSpec(memory_space=pltpu.VMEM)
SMEM = pl.BlockSpec(memory_space=pltpu.SMEM)
LANES = 128


def call(kernel, name, outs, me, *operands, scratch=(), fetch=(), store=(), limit=8):
    count, total = len(operands), len(operands) + len(outs)
    held = [(operands[n].shape, operands[n].dtype) for n in fetch] + [outs[n] for n in store]

    def body(me_ref, *refs):
        inputs, results, rest = list(refs[:count]), list(refs[count:total]), refs[total:]
        buffers, rest = rest[: len(held)], rest[len(held) :]
        sems, rest = (rest[0], rest[1:]) if held else (None, rest)
        copies = []
        for k, n in enumerate(fetch):
            copies.append(pltpu.make_async_copy(inputs[n], buffers[k], sems.at[k]))
            inputs[n] = buffers[k]
        for copy in copies:
            copy.start()
        for copy in copies:
            copy.wait()
        copies = []
        for k, n in enumerate(store, len(fetch)):
            copies.append(pltpu.make_async_copy(buffers[k], results[n], sems.at[k]))
            results[n] = buffers[k]
        kernel(me_ref, *inputs, *results, *rest)
        for copy in copies:
            copy.start()
        for copy in copies:
            copy.wait()

    own = [pltpu.VMEM(shape, kind) for shape, kind in held]
    own += [pltpu.SemaphoreType.DMA((len(held),))] if held else []
    size = sum(math.prod(shape) * jnp.dtype(kind).itemsize for shape, kind in held)
    far = pl.BlockSpec(memory_space=pltpu.HBM)
    results = pl.pallas_call(
        body,
        name=name,
        out_shape=[jax.ShapeDtypeStruct(shape, kind) for shape, kind in outs],
        in_specs=[SMEM] + [far if n in fetch else VMEM for n in range(count)],
        out_specs=[far if n in store else VMEM for n in range(len(outs))],
        scratch_shapes=own + list(scratch),
        compiler_params=pltpu.CompilerParams(vmem_limit_bytes=limit * 2**20 + size),
        cost_estimate=pl.CostEstimate(flops=0, bytes_accessed=0, transcendentals=0),
    )(me, *operands)
    return list(results)


def dot(left, right, dims=(((1,), (0,)), ((), ()))):
    return lax.dot_general(left, right, dims, preferred_element_type=f32)


def lanes(start, size):
    return pl.ds(pl.multiple_of(start, LANES), size)


def partner(values_in):
    half = HEAD_DIM // 2
    lane = lax.broadcasted_iota(jnp.int32, values_in.shape, 1)
    return jnp.where(
        lane % HEAD_DIM < half,
        pltpu.roll(values_in, values_in.shape[1] - half, 1),
        pltpu.roll(values_in, half, 1),
    )


def pick_first_kernel(me, w_qkv, w_out, out):
    width = w_out.shape[1]
    group = width // 4
    for part in range(3):
        out[:, part * group : (part + 1) * group] = w_qkv[
            :, lanes(part * width + me[2] * group, group)
        ]
    out[:, 3 * group :] = w_out[...]


def pick_rest_kernel(me, w_up, cot, *outs):
    part = w_up.shape[0]
    units = w_up.shape[1] // 4
    for r, out in enumerate(outs):
        out[:part, :] = w_up[:, lanes((me[0] ^ r) * units, units)]
        out[part:, :] = cot[...]


def stack_kernel(me, *refs):
    pieces, out = refs[:-1], refs[-1]
    part = out.shape[0] // 4
    for r, piece in enumerate(pieces):
        out[lanes((me[0] ^ r) * part, part), :] = piece[:part, :]


def weave_kernel(me, mine, theirs, *outs):
    core = me[1]
    rows = mine.shape[0] // 4
    for half, owner in ((mine, core), (theirs, 1 - core)):
        for chip in range(4):
            start = 0
            for out in outs:
                stop = start + out.shape[1]
                out[lanes((2 * chip + owner) * rows, rows), :] = half[
                    chip * rows : (chip + 1) * rows, start:stop
                ]
                start = stop


def qkv_kernel(me, *refs):
    own, a1, a2, a3, b1, b2 = refs[:6]
    scale, shift, weight, cosine, sine, q_out, k_out, v_out, normed, input_a, *again = refs[6:]
    ends = (me[2] == 0) | (me[2] == 3)
    rows, group = own.shape[0], q_out.shape[1]
    for s, (one, two) in enumerate(((own, None), (a1, None), (a2, b2), (a3, b1))):
        at = slice(s * rows, (s + 1) * rows)
        block = one[...].astype(f32)
        if two is not None:
            block = jnp.where(ends, block, two[...].astype(f32))
        centred, _ = normalize(block)
        normed[at, :] = centred.astype(bf16)
        low = (centred * (1.0 + scale[...]) + shift[...]).astype(bf16)
        input_a[at, :] = low
        for part, out in enumerate((q_out, k_out, v_out)):
            projected = dot(low, weight[:, part * group : (part + 1) * group])
            if part == 2:
                out[at, :] = projected.astype(bf16)
                continue
            for j in range(0, group, LANES):
                piece = projected[:, j : j + LANES]
                piece = piece * cosine[at, :] + partner(piece) * sine[at, :]
                if part == 0:
                    piece = piece * (1.0 / math.sqrt(HEAD_DIM))
                out[at, j : j + LANES] = piece.astype(bf16)
    for ref, kept in zip(again, (q_out, k_out, v_out, cosine, sine)):
        ref[...] = kept[...]


def attend_kernel(me, queries, keys, values, out, log_total):
    count, group = queries.shape
    step = 512
    lane = lax.broadcasted_iota(jnp.int32, (step, LANES), 1)

    def block(i, carry):
        at = pl.ds(pl.multiple_of(i * step, step), step)
        stats = jnp.zeros((step, LANES), f32)
        for j in range(group // LANES):
            cols = slice(j * LANES, (j + 1) * LANES)
            halves = []
            for side in range(2):
                query = jnp.where(
                    lane // HEAD_DIM == side, queries[at, cols], jnp.zeros((), bf16)
                )
                scores = dot(query, keys[:, cols], NT)
                top = jnp.max(scores, axis=1, keepdims=True)
                exponent = jnp.exp(scores - top)
                total = jnp.sum(exponent, axis=1, keepdims=True)
                halves.append(dot(exponent.astype(bf16), values[:, cols]) / total)
                stats = jnp.where(lane == 2 * j + side, top + jnp.log(total), stats)
            out[at, cols] = jnp.where(lane < HEAD_DIM, halves[0], halves[1]).astype(bf16)
        log_total[:, at] = jnp.transpose(stats)[:8]
        return carry

    lax.fori_loop(0, count // step, block, 0)


def attend_back_kernel(
    me, queries, keys, values, g0, g1, g2, g3, log_total, cosine, sine, out, key_sum, value_sum, query_t
):
    count, group = queries.shape
    step = 512
    rows = g0.shape[0]
    pieces = (g0, g1, g2, g3)
    keys_t = jnp.transpose(keys[...])
    lane = lax.broadcasted_iota(jnp.int32, (step, LANES), 1)
    for j in range(group // LANES):
        cols = slice(j * LANES, (j + 1) * LANES)
        for i in range(0, count, step):
            at = slice(i, i + step)
            grad = jnp.concatenate(
                [pieces[(i + n) // rows][:, cols] for n in range(0, step, rows)], axis=0
            )
            for side in range(2):
                head = 2 * j + side
                mine = slice(head * HEAD_DIM, (head + 1) * HEAD_DIM)
                keep = lane // HEAD_DIM == side
                query = jnp.where(keep, queries[at, cols], jnp.zeros((), bf16))
                grad_mine = jnp.where(keep, grad, jnp.zeros((), bf16))
                probs = jnp.exp(dot(keys[:, cols], query, NT) - log_total[head : head + 1, at])
                grad_probs = dot(values[:, cols], grad_mine, NT)
                delta = jnp.sum(probs * grad_probs, axis=0, keepdims=True)
                grad_scores = (probs * (grad_probs - delta)).astype(bf16)
                value_part = dot(probs.astype(bf16), grad_mine)
                key_part = dot(grad_scores, query)
                if i == 0 and side == 0:
                    value_sum[...] = value_part
                    key_sum[...] = key_part
                else:
                    value_sum[...] += value_part
                    key_sum[...] += key_part
                query_t[mine, at] = dot(keys_t[mine], grad_scores)
        turned = key_sum[...]
        turned = turned * cosine[...] - partner(turned) * sine[...]
        out[:, group + j * LANES : group + (j + 1) * LANES] = turned.astype(bf16)
        out[:, 2 * group + j * LANES : 2 * group + (j + 1) * LANES] = value_sum[...].astype(bf16)
        turned = jnp.transpose(query_t[cols, :]) * (1.0 / math.sqrt(HEAD_DIM))
        turned = turned * cosine[...] - partner(turned) * sine[...]
        out[:, cols] = turned.astype(bf16)


def middle_kernel(me, source, p0, p1, p2, p3, out_all, scale, shift, mixed, middle, input_b):
    place = me[2]
    group = p0.shape[1]
    for s, piece in enumerate((p0, p1, p2, p3)):
        mixed[:, lanes((place ^ s) * group, group)] = piece[...]
    value = source[...].astype(f32) + dot(mixed[...], out_all[...])
    middle[...] = value
    normed, _ = normalize(value)
    input_b[...] = (normed * (1.0 + scale[...]) + shift[...]).astype(bf16)


def ffn_kernel(
    me, inputs, packed, up, down_own, down_other, grad_in, out, hidden, grad_upper, grad_sum, out_sum
):
    core = me[1]
    units = down_own.shape[0]
    cot = packed[packed.shape[0] - inputs.shape[0] :, :]
    for n, (down, owner) in enumerate(((down_own, core), (down_other, 1 - core))):
        cols = lanes(owner * units, units)
        upper = dot(inputs[...], up[:, cols])
        bell = 0.5 + 0.5 * lax.erf(upper * math.sqrt(0.5))
        slope = bell + upper * jnp.exp(upper * upper * -0.5) * (1.0 / math.sqrt(2.0 * math.pi))
        grad = (dot(cot, down[...], NT) * slope).astype(bf16)
        grad_upper[:, cols] = grad
        value = (upper * bell).astype(bf16)
        hidden[:, n * units : (n + 1) * units] = value
        if n == 0:
            grad_sum[...] = dot(grad, up[:, cols], NT)
            out_sum[...] = dot(value, down[...])
        else:
            grad_in[...] = (grad_sum[...] + dot(grad, up[:, cols], NT)).astype(grad_in.dtype)
            out[...] = (out_sum[...] + dot(value, down[...])).astype(out.dtype)


def grad_down_kernel(me, *refs):
    hidden, cots, (give, keep) = refs[:4], refs[4:8], refs[8:]
    units = keep.shape[0]
    rows = hidden[0].shape[0]
    for out, start in ((give, units), (keep, 0)):
        total = None
        for left, packed in zip(hidden, cots):
            cot = packed[packed.shape[0] - rows :, :]
            term = dot(left[:, start : start + units], cot, TN)
            total = term if total is None else total + term
        out[...] = total.astype(out.dtype)


def grad_up_kernel(me, *refs):
    grads, tokens, (give, keep) = refs[:4], refs[4:8], refs[8:]
    core = me[1]
    part = keep.shape[0] // 4
    grad = jnp.concatenate([ref[...] for ref in grads], axis=0)
    for out, owner in ((give, 1 - core), (keep, core)):
        for chip in range(4):
            cols = lanes((2 * chip + owner) * part, part)
            left = jnp.concatenate([ref[:, cols] for ref in tokens], axis=0)
            out[chip * part : (chip + 1) * part, :] = dot(left, grad, TN).astype(out.dtype)


def pair_up_kernel(me, keep, take, proj_keep, proj_take, *outs):
    chip = me[0]
    part, width = keep.shape[0] // 4, keep.shape[1]
    for r, out in enumerate(outs):
        at = lanes((chip ^ r) * part, part)
        out[:, :width] = (keep[at, :] + take[at, :].astype(f32)).astype(out.dtype)
        out[:, width:] = (proj_keep[at, :] + proj_take[at, :].astype(f32)).astype(out.dtype)


def halve_kernel(me, keep, take, mine, send):
    low = lax.rem(me[2], 2)
    half = mine.shape[0]
    at = lanes(low * half, half)
    mine[...] = keep[at, :] + take[at, :].astype(f32)
    at = lanes((1 - low) * half, half)
    send[...] = (keep[at, :] + take[at, :].astype(f32)).astype(bf16)


def collect_kernel(me, p0, p1, p2, p3, out):
    chip = me[0]
    width = p0.shape[1] // 2
    total = None
    for r, piece in enumerate((p0, p1, p2, p3)):
        out[:, lanes((chip ^ r) * width, width)] = piece[:, :width].astype(out.dtype)
        term = piece[:, width:].astype(f32)
        total = term if total is None else total + term
    out[:, 4 * width :] = total.astype(out.dtype)


def back_b_kernel(
    me, g0, g1, g2, g3, middle, cot, scale, out_all,
    grad_middle, branch, sums, h0, h1, h2, h3,
):
    place = me[2]
    group = h0.shape[1]
    normed, inverse = normalize(middle[...])
    grad_in = g0[...]
    for more in (g1, g2, g3):
        grad_in = grad_in + more[...].astype(f32)
    sums[0:1, :] = jnp.sum(grad_in * normed, axis=0, keepdims=True)
    sums[1:2, :] = jnp.sum(grad_in, axis=0, keepdims=True)
    grad = cot[...].astype(f32) + norm_back(grad_in * (1.0 + scale[...]), normed, inverse)
    grad_middle[...] = grad
    low = grad.astype(bf16)
    branch[...] = low
    for s, piece in enumerate((h0, h1, h2, h3)):
        at = pl.ds(pl.multiple_of((place ^ s) * group, group), group)
        piece[...] = dot(low, out_all[at, :], NT).astype(bf16)


def back_a_kernel(me, grad_projected, weight, normed, own, across, pair, sums):
    rows = own.shape[0]
    first = second = None
    for s in (1, 3, 2, 0):
        at = slice(s * rows, (s + 1) * rows)
        grad = dot(grad_projected[at, :], weight[...], NT)
        if s % 2:
            pair[s // 2 * rows : (s // 2 + 1) * rows, :] = grad.astype(bf16)
        else:
            (across if s else own)[...] = grad
        one = jnp.sum(grad * normed[at, :].astype(f32), axis=0, keepdims=True)
        two = jnp.sum(grad, axis=0, keepdims=True)
        first, second = (one, two) if first is None else (first + one, second + two)
    sums[0:1, :] = first
    sums[1:2, :] = second


def grad_qkv_kernel(me, input_a, grad_projected, give, keep):
    core = me[1]
    part = keep.shape[0] // 4
    for out, owner in ((give, 1 - core), (keep, core)):
        for chip in range(4):
            cols = lanes((2 * chip + owner) * part, part)
            out[chip * part : (chip + 1) * part, :] = dot(
                input_a[:, cols], grad_projected[...], TN
            ).astype(out.dtype)


def pair_kernel(me, keep, take, *outs):
    chip = me[0]
    part = keep.shape[0] // 4
    for r, out in enumerate(outs):
        at = lanes((chip ^ r) * part, part)
        out[...] = (keep[at, :] + take[at, :].astype(f32)).astype(out.dtype)


def tokens_kernel(me, own, across, source, scale, grad_middle, out):
    grad_in = own[...] + across[...].astype(f32)
    normed, inverse = normalize(source[...].astype(f32))
    out[...] = grad_middle[...] + norm_back(grad_in * (1.0 + scale[...]), normed, inverse)


def finish_qkv_kernel(me, p0, p1, p2, p3, out):
    place = me[2]
    group = p0.shape[1] // 3
    width = out.shape[1] // 3
    for s, piece in enumerate((p0, p1, p2, p3)):
        for part in range(3):
            at = part * width + (place ^ s) * group
            out[:, lanes(at, group)] = piece[:, part * group : (part + 1) * group].astype(f32)


def swap_seq(values_in, bits):
    return lax.ppermute(values_in, "seq", [(i, i ^ bits) for i in range(4)])


def halve_pair(values_in, place):
    half = values_in.shape[0] // 2
    mine = lax.dynamic_slice_in_dim(values_in, place % 2 * half, half)
    other = lax.dynamic_slice_in_dim(values_in, (1 - place % 2) * half, half)
    return mine, other.astype(bf16)


class Halving:
    def __init__(self, held, send, place):
        self.held, self.send, self.low, self.high = held, send, place % 2, place // 2

    def across_ready(self):
        self.held = self.held + swap_seq(self.send, 1).astype(f32)
        half = self.held.shape[0] // 2
        self.send = lax.dynamic_slice_in_dim(self.held, (1 - self.high) * half, half).astype(bf16)

    def across(self):
        half = self.held.shape[0] // 2
        mine = lax.dynamic_slice_in_dim(self.held, self.high * half, half)
        self.held = (mine + swap_seq(self.send, 2).astype(f32)).astype(bf16)

    def join(self, bit, bits):
        other = swap_seq(self.held, bits)
        first = jnp.where(bit == 0, self.held, other)
        second = jnp.where(bit == 0, other, self.held)
        self.held = jnp.concatenate([first, second], axis=0)

    def back_across(self):
        self.join(self.high, 2)

    def back_pair(self):
        self.join(self.low, 1)


def outward(values_in):
    return lax.ppermute(values_in, "seq", [(1, 0), (2, 3)])


def middle_swap(values_in):
    return lax.ppermute(values_in, "seq", [(1, 2), (2, 1)])


def tie(*values_in):
    return lax.optimization_barrier(values_in)


def spread(values_in):
    return [values_in] + [hop(values_in, 2 * r) for r in range(1, 4)]


def deal(blocks):
    return [blocks[0]] + [hop(blocks[r].astype(bf16), 2 * r) for r in range(1, 4)]


def total_of(pieces):
    total = pieces[0]
    for piece in pieces[1:]:
        total = total + piece.astype(f32)
    return total


def per_device(tokens, noise_steps, w_qkv, w_out, w_up, w_down, w_time, cotangent):
    index, place = lax.axis_index("dp"), lax.axis_index("seq")
    me = jnp.stack([index // 2, index % 2, place]).astype(jnp.int32)
    _, rows, width = tokens.shape
    group = width // 4
    count = 4 * rows
    part = w_out.shape[0]
    units = w_down.shape[0]
    source, cot = tokens[0], cotangent[0]

    half = HEAD_DIM // 2
    lane = jnp.arange(LANES)
    frequency = jnp.exp(-math.log(10000.0) * (lane % half).astype(f32) / half)
    block_place = place ^ jnp.arange(4)
    positions = (block_place[:, None] * rows + jnp.arange(rows)).reshape(-1).astype(f32)
    angles = positions[:, None] * frequency
    cosine = jnp.cos(angles)
    sine = jnp.sin(angles) * jnp.where(lane % HEAD_DIM < half, -1.0, 1.0)

    a1, b1 = swap_seq(source, 1), middle_swap(source)
    size = 3 * group + width
    (first,) = call(
        pick_first_kernel,
        "pick_first",
        [((part, size), bf16)],
        me,
        w_qkv,
        w_out,
        fetch=(0, 1),
    )
    steps_all = lax.all_to_all(
        jnp.broadcast_to(noise_steps.astype(f32), (8,)),
        "dp",
        split_axis=0,
        concat_axis=0,
        tiled=True,
    )
    first, steps_all = tie(first, steps_all)
    first_mine = spread(first)
    a1, b1 = tie(a1, b1)

    a2, b2 = outward(b1), middle_swap(a1)
    packed = call(
        pick_rest_kernel,
        "pick_rest",
        [((part + rows, width), bf16)] * 4,
        me,
        w_up,
        cot,
        fetch=(0, 1),
        store=(0, 1, 2, 3),
    )
    embed_all = time_embedding(steps_all)
    cond_part = jnp.dot(embed_all, w_time.astype(f32), precision=highest)
    condition = lax.all_to_all(cond_part, "dp", split_axis=0, concat_axis=0, tiled=True).reshape(
        4, width
    )
    a2, b2, condition, cosine, sine, down_late, *more = tie(
        a2, b2, condition, cosine, sine, w_down, *first_mine, *packed
    )
    first_mine, packed = more[:4], more[4:]

    a3 = outward(b2)
    packed = deal(packed)
    (first_half,) = call(
        stack_kernel, "stack_first", [((4 * part, size), bf16)], me, *first_mine, store=(0,)
    )
    qkv_all, out_all = call(
        weave_kernel,
        "weave_first",
        [((width, 3 * group), bf16), ((width, width), bf16)],
        me,
        first_half,
        hop(first_half, 1),
        fetch=(0, 1),
    )
    a3, qkv_all = tie(a3, qkv_all)
    scale_a, shift_a, scale_b, shift_b = [condition[i : i + 1] for i in range(4)]

    queries, keys, values, normed_a, input_a, *kept = call(
        qkv_kernel,
        "qkv",
        [((count, group), bf16)] * 3
        + [((count, width), bf16)] * 2
        + [((count, group), bf16)] * 3
        + [((count, LANES), f32)] * 2,
        me,
        source,
        a1,
        a2,
        a3,
        b1,
        b2,
        scale_a,
        shift_a,
        qkv_all,
        cosine,
        sine,
        store=(3, 4, 5, 6, 7, 8, 9),
    )
    attended, log_total = call(
        attend_kernel,
        "attend",
        [((count, group), bf16), ((8, count), f32)],
        me,
        queries,
        keys,
        values,
    )
    attended, packed[1], packed[2] = tie(attended, packed[1], packed[2])
    pieces = [attended[:rows]] + [
        swap_seq(attended[s * rows : (s + 1) * rows], s) for s in range(1, 4)
    ]
    *pieces, packed[3] = tie(*pieces, packed[3])
    (up_half,) = call(
        stack_kernel, "stack_up", [((4 * part, width), bf16)], me, *packed, fetch=(0, 1, 2, 3)
    )
    down_other = hop(down_late, 1)
    up_other = hop(up_half, 1)
    mixed, middle, input_b = call(
        middle_kernel,
        "middle",
        [((rows, width), bf16), ((rows, width), f32), ((rows, width), bf16)],
        me,
        source,
        *pieces,
        out_all,
        scale_b,
        shift_b,
    )

    toks = spread(input_b)
    up_half, up_other, toks[0] = tie(up_half, up_other, toks[0])
    (up_all,) = call(
        weave_kernel, "weave_up", [((width, width), bf16)], me, up_half, up_other
    )
    grads, outs, hidden, grad_upper = [], [], [], []
    for r in range(4):
        if r:
            toks[r], _ = tie(toks[r], hidden[-1])
        one, two, three, four = call(
            ffn_kernel,
            "ffn",
            [((rows, width), bf16 if r else f32)] * 2 + [((rows, 2 * units), bf16)] * 2,
            me,
            toks[r],
            packed[r],
            up_all,
            w_down,
            down_other,
            scratch=[pltpu.VMEM((rows, width), f32)] * 2,
        )
        grads.append(one)
        outs.append(two)
        hidden.append(three)
        grad_upper.append(four)
    grads = deal(grads)

    hidden[0], grad_upper[0], grads[1], grads[2] = tie(
        hidden[0], grad_upper[0], grads[1], grads[2]
    )
    give, keep = call(
        grad_down_kernel,
        "grad_down",
        [((units, width), bf16), ((units, width), f32)],
        me,
        *hidden,
        *packed,
        fetch=tuple(range(8)),
    )
    down_give, down_keep = give, keep
    up_give, up_keep = call(
        grad_up_kernel,
        "grad_up",
        [((width // 2, width), bf16), ((width // 2, width), f32)],
        me,
        *grad_upper,
        *toks,
        store=(0, 1),
    )
    grads[3], down_give, up_give = tie(grads[3], down_give, up_give)
    down_take, up_take = hop(down_give, 1), hop(up_give, 1)
    grad_middle, branch, sums_b, *to_heads = call(
        back_b_kernel,
        "back_b",
        [((rows, width), f32), ((rows, width), bf16), ((2, width), f32)]
        + [((rows, group), bf16)] * 4,
        me,
        *grads,
        middle,
        cot,
        scale_b,
        out_all,
    )
    proj_give, proj_keep = call(
        grad_qkv_kernel,
        "grad_proj",
        [((width // 2, width), bf16), ((width // 2, width), f32)],
        me,
        mixed,
        branch,
        store=(0, 1),
    )
    proj_give, *to_heads = tie(proj_give, *to_heads)
    grad_heads = [to_heads[0]] + [swap_seq(to_heads[s], s) for s in range(1, 4)]
    down_mine, down_send = call(
        halve_kernel,
        "halve_down",
        [((units // 2, width), f32), ((units // 2, width), bf16)],
        me,
        down_keep,
        down_take,
    )
    up_parts = call(
        pair_up_kernel,
        "pair_up",
        [((part, 2 * width), f32)] + [((part, 2 * width), bf16)] * 3,
        me,
        up_keep,
        up_take,
        proj_keep,
        hop(proj_give, 1),
        fetch=(0, 1, 2, 3),
        store=(0, 1, 2, 3),
    )
    *grad_heads, down_mine, down_send, up_parts[0] = tie(
        *grad_heads, down_mine, down_send, up_parts[0]
    )

    up_parts = deal(up_parts)
    down_sum = Halving(down_mine, down_send, place)
    down_sum.across_ready()
    (grad_projected,) = call(
        attend_back_kernel,
        "attend_back",
        [((count, 3 * group), bf16)],
        me,
        *kept[:3],
        *grad_heads,
        log_total,
        *kept[3:],
        scratch=[pltpu.VMEM((count, LANES), f32)] * 2 + [pltpu.VMEM((group, count), f32)],
        fetch=(0, 1, 2, 8, 9),
    )
    grad_a, p2, pair, sums_a = call(
        back_a_kernel,
        "back_a",
        [((rows, width), f32)] * 2 + [((2 * rows, width), bf16), ((2, width), f32)],
        me,
        grad_projected,
        qkv_all,
        normed_a,
    )
    pair = swap_seq(pair, 1)

    down_sum.held, down_sum.send, p2 = tie(down_sum.held, down_sum.send, p2)
    down_sum.across()
    (both,) = call(
        collect_kernel,
        "collect",
        [((part, 5 * width), f32)],
        me,
        *up_parts,
        fetch=(0, 1, 2, 3),
    )
    up_sum = Halving(*halve_pair(both, place), place)
    give, keep = call(
        grad_qkv_kernel,
        "grad_qkv",
        [((width // 2, 3 * group), bf16), ((width // 2, 3 * group), f32)],
        me,
        input_a,
        grad_projected,
        fetch=(0,),
    )
    qkv_parts = call(
        pair_kernel,
        "pair",
        [((part, 3 * group), f32)] + [((part, 3 * group), bf16)] * 3,
        me,
        keep,
        hop(give, 1),
    )
    grad_condition = jnp.concatenate([sums_a, sums_b], axis=0)
    cond_cols = lax.all_to_all(
        grad_condition.reshape(8, -1), "dp", split_axis=0, concat_axis=0, tiled=True
    )
    cond_sum = cond_cols + swap_seq(cond_cols, 1)
    pair, up_sum.held, up_sum.send, down_sum.held, cond_sum, *rest = tie(
        pair, up_sum.held, up_sum.send, down_sum.held, cond_sum, *qkv_parts, *outs
    )
    qkv_parts, outs = rest[:4], rest[4:]

    mine = grad_a + pair[:rows].astype(f32)
    across = swap_seq((p2 + pair[rows:].astype(f32)).astype(bf16), 2)
    up_sum.across_ready()
    outs = deal(outs)
    across, up_sum.held, up_sum.send, down_sum.held, *rest = tie(
        across, up_sum.held, up_sum.send, down_sum.held, *qkv_parts, *outs
    )
    qkv_parts, outs = rest[:4], rest[4:]

    up_sum.across()
    down_sum.back_across()
    qkv_parts = deal(qkv_parts)
    (grad_tokens,) = call(
        tokens_kernel, "tokens", [((rows, width), f32)], me, mine, across, source, scale_a, grad_middle
    )
    result = (middle + total_of(outs)).astype(bf16)
    qkv_cols = total_of(qkv_parts).astype(bf16)
    up_sum.held, down_sum.held, qkv_cols, cond_sum = tie(
        up_sum.held, down_sum.held, qkv_cols, cond_sum
    )

    up_sum.back_across()
    down_sum.back_pair()
    qkv_pair = swap_seq(qkv_cols, 1)
    cond_sum = cond_sum + swap_seq(cond_sum, 2)
    up_sum.held, qkv_pair = tie(up_sum.held, qkv_pair)

    up_sum.back_pair()
    qkv_far = swap_seq(jnp.stack([qkv_cols, qkv_pair]), 2)
    grad_time = jnp.dot(embed_all.T, cond_sum, precision=highest)
    (grad_qkv,) = call(
        finish_qkv_kernel,
        "finish_qkv",
        [((part, 3 * width), f32)],
        me,
        qkv_cols,
        qkv_pair,
        qkv_far[0],
        qkv_far[1],
    )
    grad_down, both = down_sum.held, up_sum.held
    return (
        result[None],
        grad_tokens[None],
        grad_qkv,
        both[:, 4 * width :].astype(f32),
        both[:, : 4 * width].astype(f32),
        grad_down.astype(f32),
        grad_time,
    )


def solution(mesh):
    in_specs = (
        P("dp", "seq", None),
        P("dp"),
        P("dp", None),
        P("dp", None),
        P("dp", None),
        P("dp", None),
        P(None, "dp"),
        P("dp", "seq", None),
    )
    out_specs = (
        P("dp", "seq", None),
        P("dp", "seq", None),
        P("dp", None),
        P("dp", None),
        P("dp", None),
        P("dp", None),
        P(None, "dp"),
    )
    square = mesh.shape["dp"] == 8 and mesh.shape["seq"] == 4
    return jax.shard_map(
        per_device if square else per_device_any, mesh=mesh, in_specs=in_specs, out_specs=out_specs, check_vma=False
    )
```

```python
from functools import partial
import math

import jax
import jax.numpy as jnp
from jax import lax
from jax.experimental import pallas as pl
from jax.experimental.pallas import tpu as pltpu
from jax.sharding import PartitionSpec as P

HEAD_DIM = 64
TE = 256

highest = lax.Precision.HIGHEST
bf16 = jnp.bfloat16
f32 = jnp.float32


def normalize(values_in):
    centered = values_in - jnp.mean(values_in, axis=-1, keepdims=True)
    inverse = lax.rsqrt(jnp.mean(centered * centered, axis=-1, keepdims=True) + 1e-05)
    return (centered * inverse, inverse)


def norm_back(gradient, normed, inverse):
    return inverse * (
        gradient
        - jnp.mean(gradient, axis=-1, keepdims=True)
        - normed * jnp.mean(gradient * normed, axis=-1, keepdims=True)
    )


def time_embedding(noise_step):
    half_dim = TE // 2
    frequency = jnp.exp(-math.log(10000.0) * jnp.arange(half_dim, dtype=f32) / half_dim)
    angles = noise_step.astype(f32)[..., None] * frequency
    return jnp.concatenate([jnp.sin(angles), jnp.cos(angles)], axis=-1)


def rotate(values_in, positions, direction):
    half_dim = values_in.shape[-1] // 2
    frequency = jnp.exp(-math.log(10000.0) * jnp.arange(half_dim, dtype=f32) / half_dim)
    angles = positions[:, None, None] * frequency
    cosine = jnp.cos(angles)
    sine_wave = direction * jnp.sin(angles)
    first_half = values_in[..., :half_dim]
    second_half = values_in[..., half_dim:]
    return jnp.concatenate(
        [
            first_half * cosine - second_half * sine_wave,
            first_half * sine_wave + second_half * cosine,
        ],
        axis=-1,
    )


def hop(values_in, bit):
    count = lax.axis_size("dp")
    return lax.ppermute(values_in, "dp", [(i, i ^ bit) for i in range(count)])


def core_groups():
    count = lax.axis_size("dp")
    return [[i for i in range(count) if i % 2 == core] for core in range(2)]


def gather_chips(block):
    chips = lax.axis_size("dp") // 2
    if chips != 4:
        return lax.all_gather(block, "dp", axis=0, tiled=True, axis_index_groups=core_groups())
    rows = block.shape[0]
    half = rows // 2
    chip = lax.axis_index("dp") // 2
    from_x = hop(block, 2)
    from_y = hop(block, 4)
    far_top = hop(from_y[:half], 2)
    far_low = hop(from_x[half:], 4)
    out = jnp.zeros((chips * rows,) + block.shape[1:], block.dtype)
    for piece, other, shift in (
        (block, 0, 0),
        (from_x, 1, 0),
        (from_y, 2, 0),
        (far_top, 3, 0),
        (far_low, 3, half),
    ):
        out = lax.dynamic_update_slice_in_dim(out, piece, (chip ^ other) * rows + shift, axis=0)
    return out


def scatter_chips(parts):
    chips = lax.axis_size("dp") // 2
    if chips != 4:
        flat = parts.reshape((-1,) + parts.shape[2:])
        return lax.psum_scatter(
            flat, "dp", scatter_dimension=0, tiled=True, axis_index_groups=core_groups()
        ).astype(f32)
    half = parts.shape[1] // 2
    chip = lax.axis_index("dp") // 2
    own, to_x, to_y, to_far = [
        lax.dynamic_index_in_dim(parts, chip ^ other, 0, keepdims=False) for other in range(4)
    ]
    on_x = hop(to_far[:half], 2)
    on_y = hop(to_far[half:], 4)
    to_y = jnp.concatenate([to_y[:half] + on_x, to_y[half:]], axis=0)
    to_x = jnp.concatenate([to_x[:half], to_x[half:] + on_y], axis=0)
    return own.astype(f32) + hop(to_x, 2).astype(f32) + hop(to_y, 4).astype(f32)


def both_cores(half_block):
    chips = lax.axis_size("dp") // 2
    core = lax.axis_index("dp") % 2
    other = hop(half_block, 1)
    shape = (chips, half_block.shape[0] // chips) + half_block.shape[1:]
    mine, theirs = half_block.reshape(shape), other.reshape(shape)
    first = jnp.where(core == 0, mine, theirs)
    second = jnp.where(core == 0, theirs, mine)
    joined = jnp.stack([first, second], axis=1)
    return joined.reshape((-1,) + half_block.shape[1:])


def sum_cores(full):
    count = lax.axis_size("dp")
    core = lax.axis_index("dp") % 2
    view = full.reshape((count // 2, 2, full.shape[0] // count) + full.shape[1:])
    mine = lax.dynamic_index_in_dim(view, core, 1, keepdims=False)
    theirs = lax.dynamic_index_in_dim(view, 1 - core, 1, keepdims=False)
    return (mine.astype(f32) + hop(theirs.astype(bf16), 1).astype(f32)).astype(bf16)


def turn(values_in, step):
    count = lax.axis_size("seq")
    return lax.ppermute(values_in, "seq", [(i, (i + step) % count) for i in range(count)])


def shift(values_in, step):
    count = lax.axis_size("seq")
    return lax.ppermute(
        values_in, "seq", [(i, i + step) for i in range(count) if 0 <= i + step < count]
    )


def gather_seq(block):
    count = lax.axis_size("seq")
    place = lax.axis_index("seq")
    lower, upper = [block], [block]
    for _ in range(count - 1):
        lower.append(shift(lower[-1], 1))
        upper.append(shift(upper[-1], -1))
    return [block] + [
        jnp.where(place + step < count, upper[step], lower[count - step])
        for step in range(1, count)
    ]


def scatter_seq(blocks):
    count = len(blocks)
    right = left = None
    for step in range(1, count):
        going_right = blocks[count - step]
        going_left = blocks[step]
        if right is not None:
            going_right = going_right + right.astype(f32)
            going_left = going_left + left.astype(f32)
        right = shift(going_right.astype(bf16), 1)
        left = shift(going_left.astype(bf16), -1)
    return blocks[0] + right.astype(f32) + left.astype(f32)


def sum_seq(values_in):
    count = lax.axis_size("seq")
    if count != 4:
        return lax.psum(values_in.astype(bf16), "seq").astype(f32)
    place = lax.axis_index("seq")
    inner = lax.ppermute(values_in.astype(bf16), "seq", [(0, 1), (3, 2)])
    pair = values_in + inner.astype(f32)
    across = lax.ppermute(pair.astype(bf16), "seq", [(1, 2), (2, 1)])
    total = pair + across.astype(f32)
    outer = lax.ppermute(total.astype(bf16), "seq", [(1, 0), (2, 3)])
    return jnp.where((place == 0) | (place == 3), outer.astype(f32), total)


def attend_forward(queries, key_rows, values):
    scores = jnp.einsum("qhd,khd->hqk", queries, key_rows, preferred_element_type=f32) / math.sqrt(
        HEAD_DIM
    )
    row_top = jnp.max(scores, axis=-1, keepdims=True)
    exponent = jnp.exp(scores - row_top)
    row_total = jnp.sum(exponent, axis=-1, keepdims=True)
    probs = (exponent / row_total).astype(bf16)
    attended = jnp.einsum("hqk,khd->qhd", probs, values, preferred_element_type=f32)
    return attended.astype(bf16), (row_top + jnp.log(row_total))


def attend_backward(queries, key_rows, values, log_total, grad_attn):
    score_scale = 1.0 / math.sqrt(HEAD_DIM)
    scores = (
        jnp.einsum("qhd,khd->hqk", queries, key_rows, preferred_element_type=f32) * score_scale
    )
    probs = jnp.exp(scores - log_total)
    grad_probs = jnp.einsum("qhd,khd->hqk", grad_attn, values, preferred_element_type=f32)
    grad_scores = (
        probs * (grad_probs - jnp.sum(probs * grad_probs, axis=-1, keepdims=True))
    ).astype(bf16)
    grad_queries = (
        jnp.einsum("hqk,khd->qhd", grad_scores, key_rows, preferred_element_type=f32) * score_scale
    )
    grad_keys = (
        jnp.einsum("hqk,qhd->khd", grad_scores, queries, preferred_element_type=f32) * score_scale
    )
    grad_values = jnp.einsum(
        "hqk,qhd->khd", probs.astype(bf16), grad_attn, preferred_element_type=f32
    )
    return grad_queries.astype(bf16), grad_keys.astype(bf16), grad_values.astype(bf16)


def per_device_any(tokens, noise_steps, w_qkv, w_out, w_up, w_down, w_time, cotangent):
    dp_count, seq_parts = lax.axis_size("dp"), lax.axis_size("seq")
    chips = dp_count // 2
    core = lax.axis_index("dp") % 2
    place = lax.axis_index("seq")
    _, rows, width = tokens.shape
    group = width // seq_parts
    source = tokens[0]
    cot = cotangent[0]

    token_blocks = gather_seq(source)

    steps_all = lax.all_to_all(
        jnp.broadcast_to(noise_steps.astype(f32), (dp_count,)),
        "dp",
        split_axis=0,
        concat_axis=0,
        tiled=True,
    )
    embed_all = time_embedding(steps_all)
    cond_part = jnp.dot(embed_all, w_time.astype(f32), precision=highest)
    condition = lax.all_to_all(cond_part, "dp", split_axis=0, concat_axis=0, tiled=True).reshape(
        4, width
    )
    scale_a, shift_a, scale_b, shift_b = [condition[i][None, :] for i in range(4)]

    qkv_cols = lax.dynamic_index_in_dim(
        w_qkv.reshape(-1, 3, seq_parts, group), place, 2, keepdims=False
    ).reshape(-1, 3 * group)
    qkv_all = both_cores(gather_chips(qkv_cols))
    unit_view = w_up.reshape(w_up.shape[0], chips, 2, -1)
    up_mine = lax.dynamic_index_in_dim(unit_view, core, 2, keepdims=False).reshape(
        w_up.shape[0], -1
    )
    up_theirs = lax.dynamic_index_in_dim(unit_view, 1 - core, 2, keepdims=False).reshape(
        w_up.shape[0], -1
    )
    up_other = hop(up_theirs, 1)
    up_block = jnp.where(
        core == 0,
        jnp.concatenate([up_mine, up_other], axis=0),
        jnp.concatenate([up_other, up_mine], axis=0),
    )
    up_all = gather_chips(up_block)
    out_all = both_cores(gather_chips(w_out))
    down_all = gather_chips(w_down)
    cot_both = jnp.concatenate([cot, hop(cot, 1)], axis=0)

    full = jnp.concatenate(token_blocks, axis=0).astype(f32)
    normed_a, inverse_a = normalize(full)
    input_a = (normed_a * (1.0 + scale_a) + shift_a).astype(bf16)
    projected = jnp.dot(input_a, qkv_all, preferred_element_type=f32)
    block_place = (place + jnp.arange(seq_parts)) % seq_parts
    positions = (block_place[:, None] * rows + jnp.arange(rows)).reshape(-1).astype(f32)
    head_view = projected.reshape(seq_parts * rows, 3, -1, HEAD_DIM)
    queries = rotate(head_view[:, 0], positions, 1.0).astype(bf16)
    key_rows = rotate(head_view[:, 1], positions, 1.0).astype(bf16)
    values = head_view[:, 2].astype(bf16)
    attended, log_total = attend_forward(queries, key_rows, values)
    attended = attended.reshape(seq_parts, rows, group)
    pieces = [attended[0]] + [turn(attended[s], s) for s in range(1, seq_parts)]
    stacked = jnp.stack(pieces)
    mixed = jnp.concatenate(
        [
            lax.dynamic_index_in_dim(stacked, (place - g) % seq_parts, 0, keepdims=False)
            for g in range(seq_parts)
        ],
        axis=-1,
    )
    middle = source.astype(f32) + jnp.dot(mixed, out_all, preferred_element_type=f32)
    normed_b, inverse_b = normalize(middle)
    input_b = (normed_b * (1.0 + scale_b) + shift_b).astype(bf16)

    input_both = jnp.concatenate([input_b, hop(input_b, 1)], axis=0)
    upper = jnp.dot(input_both, up_all, preferred_element_type=f32)
    grad_hidden = lax.dot_general(
        cot_both, down_all, (((1,), (1,)), ((), ())), preferred_element_type=f32
    )
    hidden, gelu_pull = jax.vjp(partial(jax.nn.gelu, approximate=False), upper)
    hidden = hidden.astype(bf16)
    grad_upper = gelu_pull(grad_hidden)[0].astype(bf16)
    grad_in_part = lax.dot_general(
        grad_upper, up_all, (((1,), (1,)), ((), ())), preferred_element_type=f32
    )
    grad_in_b = grad_in_part[:rows] + hop(grad_in_part[rows:].astype(bf16), 1).astype(f32)
    out_part = jnp.dot(hidden, down_all, preferred_element_type=f32)
    result = (
        middle + out_part[:rows] + hop(out_part[rows:].astype(bf16), 1).astype(f32)
    ).astype(bf16)

    grad_down_part = lax.dot_general(
        hidden, cot_both, (((0,), (0,)), ((), ())), preferred_element_type=f32
    ).astype(bf16)
    grad_up_part = lax.dot_general(
        input_both, grad_upper, (((0,), (0,)), ((), ())), preferred_element_type=f32
    ).astype(bf16)

    grad_scale_b = jnp.sum(grad_in_b * normed_b, axis=0)
    grad_shift_b = jnp.sum(grad_in_b, axis=0)
    grad_middle = cot.astype(f32) + norm_back(grad_in_b * (1.0 + scale_b), normed_b, inverse_b)
    grad_branch = grad_middle.astype(bf16)
    grad_mixed = lax.dot_general(
        grad_branch, out_all, (((1,), (1,)), ((), ())), preferred_element_type=f32
    ).astype(bf16)
    to_heads = grad_mixed.reshape(rows, seq_parts, group)
    grad_pieces = [
        lax.dynamic_index_in_dim(to_heads, (place - s) % seq_parts, 1, keepdims=False)
        for s in range(seq_parts)
    ]
    grad_attn = jnp.concatenate(
        [grad_pieces[0]] + [turn(grad_pieces[s], -s) for s in range(1, seq_parts)], axis=0
    )
    grad_proj_part = lax.dot_general(
        mixed, grad_branch, (((0,), (0,)), ((), ())), preferred_element_type=f32
    )
    grad_q, grad_k, grad_v = attend_backward(
        queries,
        key_rows,
        values,
        log_total,
        grad_attn.reshape(seq_parts * rows, -1, HEAD_DIM),
    )
    grad_q = rotate(grad_q.astype(f32), positions, -1.0).astype(bf16)
    grad_k = rotate(grad_k.astype(f32), positions, -1.0).astype(bf16)
    grad_projected = jnp.stack([grad_q, grad_k, grad_v], axis=1).reshape(seq_parts * rows, -1)
    grad_in_a_part = lax.dot_general(
        grad_projected, qkv_all, (((1,), (1,)), ((), ())), preferred_element_type=f32
    )
    grad_qkv_part = lax.dot_general(
        input_a, grad_projected, (((0,), (0,)), ((), ())), preferred_element_type=f32
    )
    grad_in_a = scatter_seq(
        [grad_in_a_part[s * rows : (s + 1) * rows] for s in range(seq_parts)]
    )
    grad_scale_a = jnp.sum(grad_in_a_part * normed_a, axis=0)
    grad_shift_a = jnp.sum(grad_in_a_part, axis=0)
    grad_tokens = grad_middle + norm_back(
        grad_in_a * (1.0 + scale_a), normed_a[:rows], inverse_a[:rows]
    )

    grad_down = sum_seq(scatter_chips(grad_down_part.reshape(chips, -1, width)))
    grad_up_rows = scatter_chips(grad_up_part.reshape(chips, -1, grad_up_part.shape[1]))
    up_halves = grad_up_rows.reshape(2, -1, grad_up_rows.shape[1])
    keep = lax.dynamic_index_in_dim(up_halves, core, 0, keepdims=False)
    give = lax.dynamic_index_in_dim(up_halves, 1 - core, 0, keepdims=False)
    keep = keep.reshape(keep.shape[0], chips, -1)
    take = hop(give.astype(bf16), 1).astype(f32).reshape(keep.shape)
    grad_up = sum_seq(
        jnp.stack([jnp.where(core == 0, keep, take), jnp.where(core == 0, take, keep)], axis=2)
        .reshape(keep.shape[0], -1)
    )
    grad_proj = sum_seq(scatter_chips(sum_cores(grad_proj_part)))
    grad_qkv_cols = scatter_chips(sum_cores(grad_qkv_part)).astype(bf16)
    qkv_ring = jnp.stack(gather_seq(grad_qkv_cols))
    grad_qkv = jnp.stack(
        [
            lax.dynamic_index_in_dim(qkv_ring, (g - place) % seq_parts, 0, keepdims=False).reshape(
                -1, 3, group
            )
            for g in range(seq_parts)
        ],
        axis=2,
    )
    grad_qkv = grad_qkv.reshape(-1, 3 * width).astype(f32)
    grad_condition = jnp.concatenate([grad_scale_a, grad_shift_a, grad_scale_b, grad_shift_b])
    cond_cols = lax.all_to_all(
        grad_condition.reshape(dp_count, -1), "dp", split_axis=0, concat_axis=0, tiled=True
    )
    cond_sum = cond_cols
    for s in range(1, seq_parts):
        cond_sum = cond_sum + turn(cond_cols, s)
    grad_time = jnp.dot(embed_all.T, cond_sum, precision=highest)
    return (result[None], grad_tokens[None], grad_qkv, grad_proj, grad_up, grad_down, grad_time)


NT = (((1,), (1,)), ((), ()))
TN = (((0,), (0,)), ((), ()))
VMEM = pl.BlockSpec(memory_space=pltpu.VMEM)
SMEM = pl.BlockSpec(memory_space=pltpu.SMEM)
LANES = 128


def call(kernel, name, outs, me, *operands, scratch=(), fetch=(), store=(), limit=12):
    count, total = len(operands), len(operands) + len(outs)
    held = [(operands[n].shape, operands[n].dtype) for n in fetch] + [outs[n] for n in store]

    def body(me_ref, *refs):
        inputs, results, rest = list(refs[:count]), list(refs[count:total]), refs[total:]
        buffers, rest = rest[: len(held)], rest[len(held) :]
        sems, rest = (rest[0], rest[1:]) if held else (None, rest)
        copies = []
        for k, n in enumerate(fetch):
            copies.append(pltpu.make_async_copy(inputs[n], buffers[k], sems.at[k]))
            inputs[n] = buffers[k]
        for copy in copies:
            copy.start()
        for copy in copies:
            copy.wait()
        copies = []
        for k, n in enumerate(store, len(fetch)):
            copies.append(pltpu.make_async_copy(buffers[k], results[n], sems.at[k]))
            results[n] = buffers[k]
        kernel(me_ref, *inputs, *results, *rest)
        for copy in copies:
            copy.start()
        for copy in copies:
            copy.wait()

    own = [pltpu.VMEM(shape, kind) for shape, kind in held]
    own += [pltpu.SemaphoreType.DMA((len(held),))] if held else []
    size = sum(math.prod(shape) * jnp.dtype(kind).itemsize for shape, kind in held)
    far = pl.BlockSpec(memory_space=pltpu.HBM)
    results = pl.pallas_call(
        body,
        name=name,
        out_shape=[jax.ShapeDtypeStruct(shape, kind) for shape, kind in outs],
        in_specs=[SMEM] + [far if n in fetch else VMEM for n in range(count)],
        out_specs=[far if n in store else VMEM for n in range(len(outs))],
        scratch_shapes=own + list(scratch),
        compiler_params=pltpu.CompilerParams(vmem_limit_bytes=limit * 2**20 + size),
        cost_estimate=pl.CostEstimate(flops=0, bytes_accessed=0, transcendentals=0),
    )(me, *operands)
    return list(results)


def dot(left, right, dims=(((1,), (0,)), ((), ()))):
    return lax.dot_general(left, right, dims, preferred_element_type=f32)


def lanes(start, size):
    return pl.ds(pl.multiple_of(start, LANES), size)


def partner(values_in):
    half = HEAD_DIM // 2
    lane = lax.broadcasted_iota(jnp.int32, values_in.shape, 1)
    return jnp.where(
        lane % HEAD_DIM < half,
        pltpu.roll(values_in, values_in.shape[1] - half, 1),
        pltpu.roll(values_in, half, 1),
    )


def pick_first_kernel(me, w_qkv, w_out, out):
    width = w_out.shape[1]
    group = width // 4
    for part in range(3):
        out[:, part * group : (part + 1) * group] = w_qkv[
            :, lanes(part * width + me[2] * group, group)
        ]
    out[:, 3 * group :] = w_out[...]


def pick_rest_kernel(me, w_up, cot, *outs):
    part = w_up.shape[0]
    units = w_up.shape[1] // 4
    for r, out in enumerate(outs):
        out[:part, :] = w_up[:, lanes((me[0] ^ r) * units, units)]
        out[part:, :] = cot[...]


def stack_kernel(me, *refs):
    pieces, out = refs[:-1], refs[-1]
    part = out.shape[0] // 4
    for r, piece in enumerate(pieces):
        out[lanes((me[0] ^ r) * part, part), :] = piece[:part, :]


def weave_kernel(me, mine, theirs, *outs):
    core = me[1]
    rows = mine.shape[0] // 4
    for half, owner in ((mine, core), (theirs, 1 - core)):
        for chip in range(4):
            start = 0
            for out in outs:
                stop = start + out.shape[1]
                out[lanes((2 * chip + owner) * rows, rows), :] = half[
                    chip * rows : (chip + 1) * rows, start:stop
                ]
                start = stop


def qkv_kernel(me, *refs):
    own, a1, a2, a3, b1, b2 = refs[:6]
    scale, shift, weight, cosine, sine, q_out, k_out, v_out, normed, input_a, *again = refs[6:]
    ends = (me[2] == 0) | (me[2] == 3)
    rows, group = own.shape[0], q_out.shape[1]
    for s, (one, two) in enumerate(((own, None), (a1, None), (a2, b2), (a3, b1))):
        at = slice(s * rows, (s + 1) * rows)
        block = one[...].astype(f32)
        if two is not None:
            block = jnp.where(ends, block, two[...].astype(f32))
        centred, _ = normalize(block)
        normed[at, :] = centred.astype(bf16)
        low = (centred * (1.0 + scale[...]) + shift[...]).astype(bf16)
        input_a[at, :] = low
        for part, out in enumerate((q_out, k_out, v_out)):
            projected = dot(low, weight[:, part * group : (part + 1) * group])
            if part == 2:
                out[at, :] = projected.astype(bf16)
                continue
            for j in range(0, group, LANES):
                piece = projected[:, j : j + LANES]
                piece = piece * cosine[at, :] + partner(piece) * sine[at, :]
                if part == 0:
                    piece = piece * (1.0 / math.sqrt(HEAD_DIM))
                out[at, j : j + LANES] = piece.astype(bf16)
    for ref, kept in zip(again, (q_out, k_out, v_out, cosine, sine)):
        ref[...] = kept[...]


def attend_kernel(me, queries, keys, values, out, log_total):
    count, group = queries.shape
    step = 512
    lane = lax.broadcasted_iota(jnp.int32, (step, LANES), 1)

    def block(i, carry):
        at = pl.ds(pl.multiple_of(i * step, step), step)
        stats = jnp.zeros((step, LANES), f32)
        for j in range(group // LANES):
            cols = slice(j * LANES, (j + 1) * LANES)
            halves = []
            for side in range(2):
                query = jnp.where(
                    lane // HEAD_DIM == side, queries[at, cols], jnp.zeros((), bf16)
                )
                scores = dot(query, keys[:, cols], NT)
                top = jnp.max(scores, axis=1, keepdims=True)
                exponent = jnp.exp(scores - top)
                total = jnp.sum(exponent, axis=1, keepdims=True)
                halves.append(dot(exponent.astype(bf16), values[:, cols]) / total)
                stats = jnp.where(lane == 2 * j + side, top + jnp.log(total), stats)
            out[at, cols] = jnp.where(lane < HEAD_DIM, halves[0], halves[1]).astype(bf16)
        log_total[:, at] = jnp.transpose(stats)[:8]
        return carry

    lax.fori_loop(0, count // step, block, 0)


def attend_back_kernel(
    me, queries, keys, values, g0, g1, g2, g3, log_total, cosine, sine, out, key_sum, value_sum, query_t
):
    count, group = queries.shape
    step = 512
    rows = g0.shape[0]
    pieces = (g0, g1, g2, g3)
    keys_t = jnp.transpose(keys[...])
    lane = lax.broadcasted_iota(jnp.int32, (step, LANES), 1)
    for j in range(group // LANES):
        cols = slice(j * LANES, (j + 1) * LANES)
        for i in range(0, count, step):
            at = slice(i, i + step)
            grad = jnp.concatenate(
                [pieces[(i + n) // rows][:, cols] for n in range(0, step, rows)], axis=0
            )
            for side in range(2):
                head = 2 * j + side
                mine = slice(head * HEAD_DIM, (head + 1) * HEAD_DIM)
                keep = lane // HEAD_DIM == side
                query = jnp.where(keep, queries[at, cols], jnp.zeros((), bf16))
                grad_mine = jnp.where(keep, grad, jnp.zeros((), bf16))
                probs = jnp.exp(dot(keys[:, cols], query, NT) - log_total[head : head + 1, at])
                grad_probs = dot(values[:, cols], grad_mine, NT)
                delta = jnp.sum(probs * grad_probs, axis=0, keepdims=True)
                grad_scores = (probs * (grad_probs - delta)).astype(bf16)
                value_part = dot(probs.astype(bf16), grad_mine)
                key_part = dot(grad_scores, query)
                if i == 0 and side == 0:
                    value_sum[...] = value_part
                    key_sum[...] = key_part
                else:
                    value_sum[...] += value_part
                    key_sum[...] += key_part
                query_t[mine, at] = dot(keys_t[mine], grad_scores)
        turned = key_sum[...]
        turned = turned * cosine[...] - partner(turned) * sine[...]
        out[:, group + j * LANES : group + (j + 1) * LANES] = turned.astype(bf16)
        out[:, 2 * group + j * LANES : 2 * group + (j + 1) * LANES] = value_sum[...].astype(bf16)
        turned = jnp.transpose(query_t[cols, :]) * (1.0 / math.sqrt(HEAD_DIM))
        turned = turned * cosine[...] - partner(turned) * sine[...]
        out[:, cols] = turned.astype(bf16)


def middle_kernel(me, source, p0, p1, p2, p3, out_all, scale, shift, mixed, middle, input_b):
    place = me[2]
    group = p0.shape[1]
    for s, piece in enumerate((p0, p1, p2, p3)):
        mixed[:, lanes((place ^ s) * group, group)] = piece[...]
    value = source[...].astype(f32) + dot(mixed[...], out_all[...])
    middle[...] = value
    normed, _ = normalize(value)
    input_b[...] = (normed * (1.0 + scale[...]) + shift[...]).astype(bf16)


def ffn_kernel(
    me, inputs, packed, up, down_own, down_other, grad_in, out, hidden, grad_upper, grad_sum, out_sum
):
    core = me[1]
    units = down_own.shape[0]
    cot = packed[packed.shape[0] - inputs.shape[0] :, :]
    for n, (down, owner) in enumerate(((down_own, core), (down_other, 1 - core))):
        cols = lanes(owner * units, units)
        upper = dot(inputs[...], up[:, cols])
        bell = 0.5 + 0.5 * lax.erf(upper * math.sqrt(0.5))
        slope = bell + upper * jnp.exp(upper * upper * -0.5) * (1.0 / math.sqrt(2.0 * math.pi))
        grad = (dot(cot, down[...], NT) * slope).astype(bf16)
        grad_upper[:, cols] = grad
        value = (upper * bell).astype(bf16)
        hidden[:, n * units : (n + 1) * units] = value
        if n == 0:
            grad_sum[...] = dot(grad, up[:, cols], NT)
            out_sum[...] = dot(value, down[...])
        else:
            grad_in[...] = (grad_sum[...] + dot(grad, up[:, cols], NT)).astype(grad_in.dtype)
            out[...] = (out_sum[...] + dot(value, down[...])).astype(out.dtype)


def grad_down_kernel(me, *refs):
    hidden, cots, (give, keep) = refs[:4], refs[4:8], refs[8:]
    units = keep.shape[0]
    rows = hidden[0].shape[0]
    for out, start in ((give, units), (keep, 0)):
        total = None
        for left, packed in zip(hidden, cots):
            cot = packed[packed.shape[0] - rows :, :]
            term = dot(left[:, start : start + units], cot, TN)
            total = term if total is None else total + term
        out[...] = total.astype(out.dtype)


def grad_up_kernel(me, *refs):
    grads, tokens, (give, keep) = refs[:4], refs[4:8], refs[8:]
    core = me[1]
    part = keep.shape[0] // 4
    grad = jnp.concatenate([ref[...] for ref in grads], axis=0)
    for out, owner in ((give, 1 - core), (keep, core)):
        for chip in range(4):
            cols = lanes((2 * chip + owner) * part, part)
            left = jnp.concatenate([ref[:, cols] for ref in tokens], axis=0)
            out[chip * part : (chip + 1) * part, :] = dot(left, grad, TN).astype(out.dtype)


def pair_up_kernel(me, keep, take, proj_keep, proj_take, *outs):
    chip = me[0]
    part, width = keep.shape[0] // 4, keep.shape[1]
    for r, out in enumerate(outs):
        at = lanes((chip ^ r) * part, part)
        out[:, :width] = (keep[at, :] + take[at, :].astype(f32)).astype(out.dtype)
        out[:, width:] = (proj_keep[at, :] + proj_take[at, :].astype(f32)).astype(out.dtype)


def halve_kernel(me, keep, take, mine, send):
    low = lax.rem(me[2], 2)
    half = mine.shape[0]
    at = lanes(low * half, half)
    mine[...] = keep[at, :] + take[at, :].astype(f32)
    at = lanes((1 - low) * half, half)
    send[...] = (keep[at, :] + take[at, :].astype(f32)).astype(bf16)


def collect_kernel(me, p0, p1, p2, p3, out):
    chip = me[0]
    width = p0.shape[1] // 2
    total = None
    for r, piece in enumerate((p0, p1, p2, p3)):
        out[:, lanes((chip ^ r) * width, width)] = piece[:, :width].astype(out.dtype)
        term = piece[:, width:].astype(f32)
        total = term if total is None else total + term
    out[:, 4 * width :] = total.astype(out.dtype)


def back_b_kernel(
    me, g0, g1, g2, g3, middle, cot, scale, out_all,
    grad_middle, branch, sums, h0, h1, h2, h3,
):
    place = me[2]
    group = h0.shape[1]
    normed, inverse = normalize(middle[...])
    grad_in = g0[...]
    for more in (g1, g2, g3):
        grad_in = grad_in + more[...].astype(f32)
    sums[0:1, :] = jnp.sum(grad_in * normed, axis=0, keepdims=True)
    sums[1:2, :] = jnp.sum(grad_in, axis=0, keepdims=True)
    grad = cot[...].astype(f32) + norm_back(grad_in * (1.0 + scale[...]), normed, inverse)
    grad_middle[...] = grad
    low = grad.astype(bf16)
    branch[...] = low
    for s, piece in enumerate((h0, h1, h2, h3)):
        at = pl.ds(pl.multiple_of((place ^ s) * group, group), group)
        piece[...] = dot(low, out_all[at, :], NT).astype(bf16)


def back_a_kernel(me, grad_projected, weight, normed, own, across, pair, sums):
    rows = own.shape[0]
    first = second = None
    for s in (1, 3, 2, 0):
        at = slice(s * rows, (s + 1) * rows)
        grad = dot(grad_projected[at, :], weight[...], NT)
        if s % 2:
            pair[s // 2 * rows : (s // 2 + 1) * rows, :] = grad.astype(bf16)
        else:
            (across if s else own)[...] = grad
        one = jnp.sum(grad * normed[at, :].astype(f32), axis=0, keepdims=True)
        two = jnp.sum(grad, axis=0, keepdims=True)
        first, second = (one, two) if first is None else (first + one, second + two)
    sums[0:1, :] = first
    sums[1:2, :] = second


def grad_qkv_kernel(me, input_a, grad_projected, give, keep):
    core = me[1]
    part = keep.shape[0] // 4
    for out, owner in ((give, 1 - core), (keep, core)):
        for chip in range(4):
            cols = lanes((2 * chip + owner) * part, part)
            out[chip * part : (chip + 1) * part, :] = dot(
                input_a[:, cols], grad_projected[...], TN
            ).astype(out.dtype)


def pair_kernel(me, keep, take, *outs):
    chip = me[0]
    part = keep.shape[0] // 4
    for r, out in enumerate(outs):
        at = lanes((chip ^ r) * part, part)
        out[...] = (keep[at, :] + take[at, :].astype(f32)).astype(out.dtype)


def tokens_kernel(me, own, pair, across, source, scale, grad_middle, out):
    rows = own.shape[0]
    grad_in = own[...] + pair[:rows, :].astype(f32) + across[...].astype(f32)
    normed, inverse = normalize(source[...].astype(f32))
    out[...] = grad_middle[...] + norm_back(grad_in * (1.0 + scale[...]), normed, inverse)


def finish_qkv_kernel(me, p0, p1, p2, p3, out):
    place = me[2]
    group = p0.shape[1] // 3
    width = out.shape[1] // 3
    for s, piece in enumerate((p0, p1, p2, p3)):
        for part in range(3):
            at = part * width + (place ^ s) * group
            out[:, lanes(at, group)] = piece[:, part * group : (part + 1) * group].astype(f32)


def swap_seq(values_in, bits):
    return lax.ppermute(values_in, "seq", [(i, i ^ bits) for i in range(4)])


def halve_pair(values_in, place):
    half = values_in.shape[0] // 2
    mine = lax.dynamic_slice_in_dim(values_in, place % 2 * half, half)
    other = lax.dynamic_slice_in_dim(values_in, (1 - place % 2) * half, half)
    return mine, other.astype(bf16)


class Halving:
    def __init__(self, held, send, place):
        self.held, self.send, self.low, self.high = held, send, place % 2, place // 2

    def across_ready(self):
        self.held = self.held + swap_seq(self.send, 1).astype(f32)
        half = self.held.shape[0] // 2
        self.send = lax.dynamic_slice_in_dim(self.held, (1 - self.high) * half, half).astype(bf16)

    def across(self):
        self.got = swap_seq(self.send, 2)

    def across_done(self, *others):
        half = self.held.shape[0] // 2
        mine = lax.dynamic_slice_in_dim(self.held, self.high * half, half)
        self.held = (mine + tie(self.got, *others)[0].astype(f32)).astype(bf16)

    def join(self, bit, bits):
        other = swap_seq(self.held, bits)
        first = jnp.where(bit == 0, self.held, other)
        second = jnp.where(bit == 0, other, self.held)
        self.held = jnp.concatenate([first, second], axis=0)

    def back_across(self):
        self.join(self.high, 2)

    def back_pair(self):
        self.join(self.low, 1)


def outward(values_in):
    return lax.ppermute(values_in, "seq", [(1, 0), (2, 3)])


def middle_swap(values_in):
    return lax.ppermute(values_in, "seq", [(1, 2), (2, 1)])


def tie(*values_in):
    return lax.optimization_barrier(values_in)


def spread(values_in):
    return [values_in] + [hop(values_in, 2 * r) for r in range(1, 4)]


def deal(blocks):
    return [blocks[0]] + [hop(blocks[r].astype(bf16), 2 * r) for r in range(1, 4)]


def total_of(pieces):
    total = pieces[0]
    for piece in pieces[1:]:
        total = total + piece.astype(f32)
    return total


def per_device(tokens, noise_steps, w_qkv, w_out, w_up, w_down, w_time, cotangent):
    index, place = lax.axis_index("dp"), lax.axis_index("seq")
    me = jnp.stack([index // 2, index % 2, place]).astype(jnp.int32)
    _, rows, width = tokens.shape
    group = width // 4
    count = 4 * rows
    part = w_out.shape[0]
    units = w_down.shape[0]
    source, cot = tokens[0], cotangent[0]

    half = HEAD_DIM // 2
    lane = jnp.arange(LANES)
    frequency = jnp.exp(-math.log(10000.0) * (lane % half).astype(f32) / half)
    block_place = place ^ jnp.arange(4)
    positions = (block_place[:, None] * rows + jnp.arange(rows)).reshape(-1).astype(f32)
    angles = positions[:, None] * frequency
    cosine = jnp.cos(angles)
    sine = jnp.sin(angles) * jnp.where(lane % HEAD_DIM < half, -1.0, 1.0)

    a1, b1 = swap_seq(source, 1), middle_swap(source)
    size = 3 * group + width
    (first,) = call(
        pick_first_kernel,
        "pick_first",
        [((part, size), bf16)],
        me,
        w_qkv,
        w_out,
        fetch=(0, 1),
    )
    steps_all = lax.all_to_all(
        jnp.broadcast_to(noise_steps.astype(f32), (8,)),
        "dp",
        split_axis=0,
        concat_axis=0,
        tiled=True,
    )
    first, steps_all = tie(first, steps_all)
    first_mine = spread(first)
    a1, b1 = tie(a1, b1)

    a2, b2 = outward(b1), middle_swap(a1)
    packed = call(
        pick_rest_kernel,
        "pick_rest",
        [((part + rows, width), bf16)] * 4,
        me,
        w_up,
        cot,
        fetch=(0, 1),
        store=(0, 1, 2, 3),
    )
    embed_all = time_embedding(steps_all)
    cond_part = jnp.dot(embed_all, w_time.astype(f32), precision=highest)
    condition = lax.all_to_all(cond_part, "dp", split_axis=0, concat_axis=0, tiled=True).reshape(
        4, width
    )
    a2, b2, condition, cosine, sine, down_late, *more = tie(
        a2, b2, condition, cosine, sine, w_down, *first_mine, *packed
    )
    first_mine, packed = more[:4], more[4:]

    a3 = outward(b2)
    (first_half,) = call(
        stack_kernel, "stack_first", [((4 * part, size), bf16)], me, *first_mine, store=(0,)
    )
    first_half, *packed = tie(first_half, *packed)
    packed = deal(packed)
    qkv_all, out_all = call(
        weave_kernel,
        "weave_first",
        [((width, 3 * group), bf16), ((width, width), bf16)],
        me,
        first_half,
        hop(first_half, 1),
        fetch=(0, 1),
    )
    a3, qkv_all = tie(a3, qkv_all)
    scale_a, shift_a, scale_b, shift_b = [condition[i : i + 1] for i in range(4)]

    queries, keys, values, normed_a, input_a, *kept = call(
        qkv_kernel,
        "qkv",
        [((count, group), bf16)] * 3
        + [((count, width), bf16)] * 2
        + [((count, group), bf16)] * 3
        + [((count, LANES), f32)] * 2,
        me,
        source,
        a1,
        a2,
        a3,
        b1,
        b2,
        scale_a,
        shift_a,
        qkv_all,
        cosine,
        sine,
        store=(3, 4, 5, 6, 7, 8, 9),
    )
    attended, log_total = call(
        attend_kernel,
        "attend",
        [((count, group), bf16), ((8, count), f32)],
        me,
        queries,
        keys,
        values,
    )
    attended, packed[1] = tie(attended, packed[1])
    pieces = [attended[:rows]] + [
        swap_seq(attended[s * rows : (s + 1) * rows], s) for s in range(1, 4)
    ]
    *pieces, packed[2], packed[3] = tie(*pieces, packed[2], packed[3])
    (up_half,) = call(
        stack_kernel, "stack_up", [((4 * part, width), bf16)], me, *packed, fetch=(0, 1, 2, 3)
    )
    down_other = hop(down_late, 1)
    up_other = hop(up_half, 1)
    mixed, middle, input_b = call(
        middle_kernel,
        "middle",
        [((rows, width), bf16), ((rows, width), f32), ((rows, width), bf16)],
        me,
        source,
        *pieces,
        out_all,
        scale_b,
        shift_b,
    )

    toks = [input_b, hop(input_b, 2), None, hop(input_b, 6)]
    up_half, up_other, toks[0] = tie(up_half, up_other, toks[0])
    (up_all,) = call(
        weave_kernel, "weave_up", [((width, width), bf16)], me, up_half, up_other
    )
    grads, outs, hidden, grad_upper = [None] * 4, [None] * 4, [None] * 4, [None] * 4
    last = None
    for r in (0, 3, 1, 2):
        if r:
            toks[r], hidden[last] = tie(toks[r], hidden[last])
        if r == 3:
            late, toks[3] = tie(input_b, toks[3])
            toks[2] = hop(late, 4)
        if r == 2:
            toks[2], grads[3] = tie(toks[2], grads[3])
        grads[r], outs[r], hidden[r], grad_upper[r] = call(
            ffn_kernel,
            "ffn",
            [((rows, width), bf16 if r else f32)] * 2 + [((rows, 2 * units), bf16)] * 2,
            me,
            toks[r],
            packed[r],
            up_all,
            w_down,
            down_other,
            scratch=[pltpu.VMEM((rows, width), f32)] * 2,
        )
        if r:
            grads[r] = hop(grads[r], 2 * r)
        last = r

    hidden[0], grad_upper[0], grads[1], grads[3] = tie(
        hidden[0], grad_upper[0], grads[1], grads[3]
    )
    give, keep = call(
        grad_down_kernel,
        "grad_down",
        [((units, width), bf16), ((units, width), f32)],
        me,
        *hidden,
        *packed,
        fetch=tuple(range(8)),
    )
    down_give, down_keep = give, keep
    up_give, up_keep = call(
        grad_up_kernel,
        "grad_up",
        [((width // 2, width), bf16), ((width // 2, width), f32)],
        me,
        *grad_upper,
        *toks,
        store=(0, 1),
    )
    grads[2], down_give, up_give = tie(grads[2], down_give, up_give)
    down_take, up_take = hop(down_give, 1), hop(up_give, 1)
    grad_middle, branch, sums_b, *to_heads = call(
        back_b_kernel,
        "back_b",
        [((rows, width), f32), ((rows, width), bf16), ((2, width), f32)]
        + [((rows, group), bf16)] * 4,
        me,
        *grads,
        middle,
        cot,
        scale_b,
        out_all,
    )
    proj_give, proj_keep = call(
        grad_qkv_kernel,
        "grad_proj",
        [((width // 2, width), bf16), ((width // 2, width), f32)],
        me,
        mixed,
        branch,
        store=(0, 1),
    )
    proj_give, *to_heads = tie(proj_give, *to_heads)
    grad_heads = [to_heads[0]] + [swap_seq(to_heads[s], s) for s in range(1, 4)]
    down_mine, down_send = call(
        halve_kernel,
        "halve_down",
        [((units // 2, width), f32), ((units // 2, width), bf16)],
        me,
        down_keep,
        down_take,
    )
    up_parts = call(
        pair_up_kernel,
        "pair_up",
        [((part, 2 * width), f32)] + [((part, 2 * width), bf16)] * 3,
        me,
        up_keep,
        up_take,
        proj_keep,
        hop(proj_give, 1),
        fetch=(0, 1, 2, 3),
        store=(0, 1, 2, 3),
    )
    *grad_heads, down_mine, down_send, up_parts[0] = tie(
        *grad_heads, down_mine, down_send, up_parts[0]
    )

    up_parts = deal(up_parts)
    down_sum = Halving(down_mine, down_send, place)
    down_sum.across_ready()
    (grad_projected,) = call(
        attend_back_kernel,
        "attend_back",
        [((count, 3 * group), bf16)],
        me,
        *kept[:3],
        *grad_heads,
        log_total,
        *kept[3:],
        scratch=[pltpu.VMEM((count, LANES), f32)] * 2 + [pltpu.VMEM((group, count), f32)],
        fetch=(0, 1, 2, 8, 9),
    )
    grad_a, p2, pair, sums_a = call(
        back_a_kernel,
        "back_a",
        [((rows, width), f32)] * 2 + [((2 * rows, width), bf16), ((2, width), f32)],
        me,
        grad_projected,
        qkv_all,
        normed_a,
        fetch=(2,),
        store=(0, 1, 2),
    )
    pair = swap_seq(pair, 1)

    down_sum.held, down_sum.send, p2 = tie(down_sum.held, down_sum.send, p2)
    down_sum.across()
    (both,) = call(
        collect_kernel,
        "collect",
        [((part, 5 * width), f32)],
        me,
        *up_parts,
        fetch=(0, 1, 2, 3),
    )
    up_mine, up_send = halve_pair(both, place)
    up_sum = Halving(up_mine, up_send, place)
    give, keep = call(
        grad_qkv_kernel,
        "grad_qkv",
        [((width // 2, 3 * group), bf16), ((width // 2, 3 * group), f32)],
        me,
        input_a,
        grad_projected,
        fetch=(0,),
    )
    take, both = tie(hop(give, 1), both)
    qkv_parts = call(
        pair_kernel,
        "pair",
        [((part, 3 * group), f32)] + [((part, 3 * group), bf16)] * 3,
        me,
        keep,
        take,
    )
    sums_a, qkv_parts[1] = tie(sums_a, qkv_parts[1])
    qkv_parts = deal(qkv_parts)
    grad_condition = jnp.concatenate([sums_a, sums_b], axis=0)
    cond_cols = lax.all_to_all(
        grad_condition.reshape(8, -1), "dp", split_axis=0, concat_axis=0, tiled=True
    )
    qkv_cols = total_of(qkv_parts).astype(bf16)
    down_sum.across_done(qkv_cols, cond_cols)
    pair, up_sum.held, up_sum.send, down_sum.held, cond_cols, qkv_cols, *outs = tie(
        pair, up_sum.held, up_sum.send, down_sum.held, cond_cols, qkv_cols, *outs
    )

    across = swap_seq((p2 + pair[rows:].astype(f32)).astype(bf16), 2)
    up_sum.across_ready()
    outs = deal(outs)
    across, up_sum.held, up_sum.send, down_sum.held, qkv_cols, cond_cols, *outs = tie(
        across, up_sum.held, up_sum.send, down_sum.held, qkv_cols, cond_cols, *outs
    )

    up_sum.across()
    down_sum.back_across()
    qkv_pair = swap_seq(qkv_cols, 1)
    up_sum.across_done()
    cond_sum = cond_cols + swap_seq(cond_cols, 1)
    result = (middle + total_of(outs)).astype(bf16)
    (grad_tokens,) = call(
        tokens_kernel,
        "tokens",
        [((rows, width), f32)],
        me,
        grad_a,
        pair,
        across,
        source,
        scale_a,
        grad_middle,
    )
    up_sum.held, down_sum.held, qkv_pair, cond_sum = tie(
        up_sum.held, down_sum.held, qkv_pair, cond_sum
    )

    up_sum.back_across()
    down_sum.back_pair()
    cond_sum = cond_sum + swap_seq(cond_sum, 2)
    up_sum.held, qkv_pair = tie(up_sum.held, qkv_pair)

    qkv_far = swap_seq(jnp.stack([qkv_cols, qkv_pair]), 2)
    up_sum.back_pair()
    grad_time = jnp.dot(embed_all.T, cond_sum, precision=highest)
    (grad_qkv,) = call(
        finish_qkv_kernel,
        "finish_qkv",
        [((part, 3 * width), f32)],
        me,
        qkv_cols,
        qkv_pair,
        qkv_far[0],
        qkv_far[1],
    )
    grad_down, both = down_sum.held, up_sum.held
    return (
        result[None],
        grad_tokens[None],
        grad_qkv,
        both[:, 4 * width :].astype(f32),
        both[:, : 4 * width].astype(f32),
        grad_down.astype(f32),
        grad_time,
    )


def solution(mesh):
    in_specs = (
        P("dp", "seq", None),
        P("dp"),
        P("dp", None),
        P("dp", None),
        P("dp", None),
        P("dp", None),
        P(None, "dp"),
        P("dp", "seq", None),
    )
    out_specs = (
        P("dp", "seq", None),
        P("dp", "seq", None),
        P("dp", None),
        P("dp", None),
        P("dp", None),
        P("dp", None),
        P(None, "dp"),
    )
    square = mesh.shape["dp"] == 8 and mesh.shape["seq"] == 4
    return jax.shard_map(
        per_device if square else per_device_any, mesh=mesh, in_specs=in_specs, out_specs=out_specs, check_vma=False
    )
```

```python
from functools import partial
import math

import jax
import jax.numpy as jnp
from jax import lax
from jax.experimental import pallas as pl
from jax.experimental.pallas import tpu as pltpu
from jax.sharding import PartitionSpec as P

HEAD_DIM = 64
TE = 256

highest = lax.Precision.HIGHEST
bf16 = jnp.bfloat16
f32 = jnp.float32


def normalize(values_in):
    centered = values_in - jnp.mean(values_in, axis=-1, keepdims=True)
    inverse = lax.rsqrt(jnp.mean(centered * centered, axis=-1, keepdims=True) + 1e-05)
    return (centered * inverse, inverse)


def norm_back(gradient, normed, inverse):
    return inverse * (
        gradient
        - jnp.mean(gradient, axis=-1, keepdims=True)
        - normed * jnp.mean(gradient * normed, axis=-1, keepdims=True)
    )


def time_embedding(noise_step):
    half_dim = TE // 2
    frequency = jnp.exp(-math.log(10000.0) * jnp.arange(half_dim, dtype=f32) / half_dim)
    angles = noise_step.astype(f32)[..., None] * frequency
    return jnp.concatenate([jnp.sin(angles), jnp.cos(angles)], axis=-1)


def rotate(values_in, positions, direction):
    half_dim = values_in.shape[-1] // 2
    frequency = jnp.exp(-math.log(10000.0) * jnp.arange(half_dim, dtype=f32) / half_dim)
    angles = positions[:, None, None] * frequency
    cosine = jnp.cos(angles)
    sine_wave = direction * jnp.sin(angles)
    first_half = values_in[..., :half_dim]
    second_half = values_in[..., half_dim:]
    return jnp.concatenate(
        [
            first_half * cosine - second_half * sine_wave,
            first_half * sine_wave + second_half * cosine,
        ],
        axis=-1,
    )


def hop(values_in, bit):
    count = lax.axis_size("dp")
    return lax.ppermute(values_in, "dp", [(i, i ^ bit) for i in range(count)])


def core_groups():
    count = lax.axis_size("dp")
    return [[i for i in range(count) if i % 2 == core] for core in range(2)]


def gather_chips(block):
    chips = lax.axis_size("dp") // 2
    if chips != 4:
        return lax.all_gather(block, "dp", axis=0, tiled=True, axis_index_groups=core_groups())
    rows = block.shape[0]
    half = rows // 2
    chip = lax.axis_index("dp") // 2
    from_x = hop(block, 2)
    from_y = hop(block, 4)
    far_top = hop(from_y[:half], 2)
    far_low = hop(from_x[half:], 4)
    out = jnp.zeros((chips * rows,) + block.shape[1:], block.dtype)
    for piece, other, shift in (
        (block, 0, 0),
        (from_x, 1, 0),
        (from_y, 2, 0),
        (far_top, 3, 0),
        (far_low, 3, half),
    ):
        out = lax.dynamic_update_slice_in_dim(out, piece, (chip ^ other) * rows + shift, axis=0)
    return out


def scatter_chips(parts):
    chips = lax.axis_size("dp") // 2
    if chips != 4:
        flat = parts.reshape((-1,) + parts.shape[2:])
        return lax.psum_scatter(
            flat, "dp", scatter_dimension=0, tiled=True, axis_index_groups=core_groups()
        ).astype(f32)
    half = parts.shape[1] // 2
    chip = lax.axis_index("dp") // 2
    own, to_x, to_y, to_far = [
        lax.dynamic_index_in_dim(parts, chip ^ other, 0, keepdims=False) for other in range(4)
    ]
    on_x = hop(to_far[:half], 2)
    on_y = hop(to_far[half:], 4)
    to_y = jnp.concatenate([to_y[:half] + on_x, to_y[half:]], axis=0)
    to_x = jnp.concatenate([to_x[:half], to_x[half:] + on_y], axis=0)
    return own.astype(f32) + hop(to_x, 2).astype(f32) + hop(to_y, 4).astype(f32)


def both_cores(half_block):
    chips = lax.axis_size("dp") // 2
    core = lax.axis_index("dp") % 2
    other = hop(half_block, 1)
    shape = (chips, half_block.shape[0] // chips) + half_block.shape[1:]
    mine, theirs = half_block.reshape(shape), other.reshape(shape)
    first = jnp.where(core == 0, mine, theirs)
    second = jnp.where(core == 0, theirs, mine)
    joined = jnp.stack([first, second], axis=1)
    return joined.reshape((-1,) + half_block.shape[1:])


def sum_cores(full):
    count = lax.axis_size("dp")
    core = lax.axis_index("dp") % 2
    view = full.reshape((count // 2, 2, full.shape[0] // count) + full.shape[1:])
    mine = lax.dynamic_index_in_dim(view, core, 1, keepdims=False)
    theirs = lax.dynamic_index_in_dim(view, 1 - core, 1, keepdims=False)
    return (mine.astype(f32) + hop(theirs.astype(bf16), 1).astype(f32)).astype(bf16)


def turn(values_in, step):
    count = lax.axis_size("seq")
    return lax.ppermute(values_in, "seq", [(i, (i + step) % count) for i in range(count)])


def shift(values_in, step):
    count = lax.axis_size("seq")
    return lax.ppermute(
        values_in, "seq", [(i, i + step) for i in range(count) if 0 <= i + step < count]
    )


def gather_seq(block):
    count = lax.axis_size("seq")
    place = lax.axis_index("seq")
    lower, upper = [block], [block]
    for _ in range(count - 1):
        lower.append(shift(lower[-1], 1))
        upper.append(shift(upper[-1], -1))
    return [block] + [
        jnp.where(place + step < count, upper[step], lower[count - step])
        for step in range(1, count)
    ]


def scatter_seq(blocks):
    count = len(blocks)
    right = left = None
    for step in range(1, count):
        going_right = blocks[count - step]
        going_left = blocks[step]
        if right is not None:
            going_right = going_right + right.astype(f32)
            going_left = going_left + left.astype(f32)
        right = shift(going_right.astype(bf16), 1)
        left = shift(going_left.astype(bf16), -1)
    return blocks[0] + right.astype(f32) + left.astype(f32)


def sum_seq(values_in):
    count = lax.axis_size("seq")
    if count != 4:
        return lax.psum(values_in.astype(bf16), "seq").astype(f32)
    place = lax.axis_index("seq")
    inner = lax.ppermute(values_in.astype(bf16), "seq", [(0, 1), (3, 2)])
    pair = values_in + inner.astype(f32)
    across = lax.ppermute(pair.astype(bf16), "seq", [(1, 2), (2, 1)])
    total = pair + across.astype(f32)
    outer = lax.ppermute(total.astype(bf16), "seq", [(1, 0), (2, 3)])
    return jnp.where((place == 0) | (place == 3), outer.astype(f32), total)


def attend_forward(queries, key_rows, values):
    scores = jnp.einsum("qhd,khd->hqk", queries, key_rows, preferred_element_type=f32) / math.sqrt(
        HEAD_DIM
    )
    row_top = jnp.max(scores, axis=-1, keepdims=True)
    exponent = jnp.exp(scores - row_top)
    row_total = jnp.sum(exponent, axis=-1, keepdims=True)
    probs = (exponent / row_total).astype(bf16)
    attended = jnp.einsum("hqk,khd->qhd", probs, values, preferred_element_type=f32)
    return attended.astype(bf16), (row_top + jnp.log(row_total))


def attend_backward(queries, key_rows, values, log_total, grad_attn):
    score_scale = 1.0 / math.sqrt(HEAD_DIM)
    scores = (
        jnp.einsum("qhd,khd->hqk", queries, key_rows, preferred_element_type=f32) * score_scale
    )
    probs = jnp.exp(scores - log_total)
    grad_probs = jnp.einsum("qhd,khd->hqk", grad_attn, values, preferred_element_type=f32)
    grad_scores = (
        probs * (grad_probs - jnp.sum(probs * grad_probs, axis=-1, keepdims=True))
    ).astype(bf16)
    grad_queries = (
        jnp.einsum("hqk,khd->qhd", grad_scores, key_rows, preferred_element_type=f32) * score_scale
    )
    grad_keys = (
        jnp.einsum("hqk,qhd->khd", grad_scores, queries, preferred_element_type=f32) * score_scale
    )
    grad_values = jnp.einsum(
        "hqk,qhd->khd", probs.astype(bf16), grad_attn, preferred_element_type=f32
    )
    return grad_queries.astype(bf16), grad_keys.astype(bf16), grad_values.astype(bf16)


def per_device_any(tokens, noise_steps, w_qkv, w_out, w_up, w_down, w_time, cotangent):
    dp_count, seq_parts = lax.axis_size("dp"), lax.axis_size("seq")
    chips = dp_count // 2
    core = lax.axis_index("dp") % 2
    place = lax.axis_index("seq")
    _, rows, width = tokens.shape
    group = width // seq_parts
    source = tokens[0]
    cot = cotangent[0]

    token_blocks = gather_seq(source)

    steps_all = lax.all_to_all(
        jnp.broadcast_to(noise_steps.astype(f32), (dp_count,)),
        "dp",
        split_axis=0,
        concat_axis=0,
        tiled=True,
    )
    embed_all = time_embedding(steps_all)
    cond_part = jnp.dot(embed_all, w_time.astype(f32), precision=highest)
    condition = lax.all_to_all(cond_part, "dp", split_axis=0, concat_axis=0, tiled=True).reshape(
        4, width
    )
    scale_a, shift_a, scale_b, shift_b = [condition[i][None, :] for i in range(4)]

    qkv_cols = lax.dynamic_index_in_dim(
        w_qkv.reshape(-1, 3, seq_parts, group), place, 2, keepdims=False
    ).reshape(-1, 3 * group)
    qkv_all = both_cores(gather_chips(qkv_cols))
    unit_view = w_up.reshape(w_up.shape[0], chips, 2, -1)
    up_mine = lax.dynamic_index_in_dim(unit_view, core, 2, keepdims=False).reshape(
        w_up.shape[0], -1
    )
    up_theirs = lax.dynamic_index_in_dim(unit_view, 1 - core, 2, keepdims=False).reshape(
        w_up.shape[0], -1
    )
    up_other = hop(up_theirs, 1)
    up_block = jnp.where(
        core == 0,
        jnp.concatenate([up_mine, up_other], axis=0),
        jnp.concatenate([up_other, up_mine], axis=0),
    )
    up_all = gather_chips(up_block)
    out_all = both_cores(gather_chips(w_out))
    down_all = gather_chips(w_down)
    cot_both = jnp.concatenate([cot, hop(cot, 1)], axis=0)

    full = jnp.concatenate(token_blocks, axis=0).astype(f32)
    normed_a, inverse_a = normalize(full)
    input_a = (normed_a * (1.0 + scale_a) + shift_a).astype(bf16)
    projected = jnp.dot(input_a, qkv_all, preferred_element_type=f32)
    block_place = (place + jnp.arange(seq_parts)) % seq_parts
    positions = (block_place[:, None] * rows + jnp.arange(rows)).reshape(-1).astype(f32)
    head_view = projected.reshape(seq_parts * rows, 3, -1, HEAD_DIM)
    queries = rotate(head_view[:, 0], positions, 1.0).astype(bf16)
    key_rows = rotate(head_view[:, 1], positions, 1.0).astype(bf16)
    values = head_view[:, 2].astype(bf16)
    attended, log_total = attend_forward(queries, key_rows, values)
    attended = attended.reshape(seq_parts, rows, group)
    pieces = [attended[0]] + [turn(attended[s], s) for s in range(1, seq_parts)]
    stacked = jnp.stack(pieces)
    mixed = jnp.concatenate(
        [
            lax.dynamic_index_in_dim(stacked, (place - g) % seq_parts, 0, keepdims=False)
            for g in range(seq_parts)
        ],
        axis=-1,
    )
    middle = source.astype(f32) + jnp.dot(mixed, out_all, preferred_element_type=f32)
    normed_b, inverse_b = normalize(middle)
    input_b = (normed_b * (1.0 + scale_b) + shift_b).astype(bf16)

    input_both = jnp.concatenate([input_b, hop(input_b, 1)], axis=0)
    upper = jnp.dot(input_both, up_all, preferred_element_type=f32)
    grad_hidden = lax.dot_general(
        cot_both, down_all, (((1,), (1,)), ((), ())), preferred_element_type=f32
    )
    hidden, gelu_pull = jax.vjp(partial(jax.nn.gelu, approximate=False), upper)
    hidden = hidden.astype(bf16)
    grad_upper = gelu_pull(grad_hidden)[0].astype(bf16)
    grad_in_part = lax.dot_general(
        grad_upper, up_all, (((1,), (1,)), ((), ())), preferred_element_type=f32
    )
    grad_in_b = grad_in_part[:rows] + hop(grad_in_part[rows:].astype(bf16), 1).astype(f32)
    out_part = jnp.dot(hidden, down_all, preferred_element_type=f32)
    result = (
        middle + out_part[:rows] + hop(out_part[rows:].astype(bf16), 1).astype(f32)
    ).astype(bf16)

    grad_down_part = lax.dot_general(
        hidden, cot_both, (((0,), (0,)), ((), ())), preferred_element_type=f32
    ).astype(bf16)
    grad_up_part = lax.dot_general(
        input_both, grad_upper, (((0,), (0,)), ((), ())), preferred_element_type=f32
    ).astype(bf16)

    grad_scale_b = jnp.sum(grad_in_b * normed_b, axis=0)
    grad_shift_b = jnp.sum(grad_in_b, axis=0)
    grad_middle = cot.astype(f32) + norm_back(grad_in_b * (1.0 + scale_b), normed_b, inverse_b)
    grad_branch = grad_middle.astype(bf16)
    grad_mixed = lax.dot_general(
        grad_branch, out_all, (((1,), (1,)), ((), ())), preferred_element_type=f32
    ).astype(bf16)
    to_heads = grad_mixed.reshape(rows, seq_parts, group)
    grad_pieces = [
        lax.dynamic_index_in_dim(to_heads, (place - s) % seq_parts, 1, keepdims=False)
        for s in range(seq_parts)
    ]
    grad_attn = jnp.concatenate(
        [grad_pieces[0]] + [turn(grad_pieces[s], -s) for s in range(1, seq_parts)], axis=0
    )
    grad_proj_part = lax.dot_general(
        mixed, grad_branch, (((0,), (0,)), ((), ())), preferred_element_type=f32
    )
    grad_q, grad_k, grad_v = attend_backward(
        queries,
        key_rows,
        values,
        log_total,
        grad_attn.reshape(seq_parts * rows, -1, HEAD_DIM),
    )
    grad_q = rotate(grad_q.astype(f32), positions, -1.0).astype(bf16)
    grad_k = rotate(grad_k.astype(f32), positions, -1.0).astype(bf16)
    grad_projected = jnp.stack([grad_q, grad_k, grad_v], axis=1).reshape(seq_parts * rows, -1)
    grad_in_a_part = lax.dot_general(
        grad_projected, qkv_all, (((1,), (1,)), ((), ())), preferred_element_type=f32
    )
    grad_qkv_part = lax.dot_general(
        input_a, grad_projected, (((0,), (0,)), ((), ())), preferred_element_type=f32
    )
    grad_in_a = scatter_seq(
        [grad_in_a_part[s * rows : (s + 1) * rows] for s in range(seq_parts)]
    )
    grad_scale_a = jnp.sum(grad_in_a_part * normed_a, axis=0)
    grad_shift_a = jnp.sum(grad_in_a_part, axis=0)
    grad_tokens = grad_middle + norm_back(
        grad_in_a * (1.0 + scale_a), normed_a[:rows], inverse_a[:rows]
    )

    grad_down = sum_seq(scatter_chips(grad_down_part.reshape(chips, -1, width)))
    grad_up_rows = scatter_chips(grad_up_part.reshape(chips, -1, grad_up_part.shape[1]))
    up_halves = grad_up_rows.reshape(2, -1, grad_up_rows.shape[1])
    keep = lax.dynamic_index_in_dim(up_halves, core, 0, keepdims=False)
    give = lax.dynamic_index_in_dim(up_halves, 1 - core, 0, keepdims=False)
    keep = keep.reshape(keep.shape[0], chips, -1)
    take = hop(give.astype(bf16), 1).astype(f32).reshape(keep.shape)
    grad_up = sum_seq(
        jnp.stack([jnp.where(core == 0, keep, take), jnp.where(core == 0, take, keep)], axis=2)
        .reshape(keep.shape[0], -1)
    )
    grad_proj = sum_seq(scatter_chips(sum_cores(grad_proj_part)))
    grad_qkv_cols = scatter_chips(sum_cores(grad_qkv_part)).astype(bf16)
    qkv_ring = jnp.stack(gather_seq(grad_qkv_cols))
    grad_qkv = jnp.stack(
        [
            lax.dynamic_index_in_dim(qkv_ring, (g - place) % seq_parts, 0, keepdims=False).reshape(
                -1, 3, group
            )
            for g in range(seq_parts)
        ],
        axis=2,
    )
    grad_qkv = grad_qkv.reshape(-1, 3 * width).astype(f32)
    grad_condition = jnp.concatenate([grad_scale_a, grad_shift_a, grad_scale_b, grad_shift_b])
    cond_cols = lax.all_to_all(
        grad_condition.reshape(dp_count, -1), "dp", split_axis=0, concat_axis=0, tiled=True
    )
    cond_sum = cond_cols
    for s in range(1, seq_parts):
        cond_sum = cond_sum + turn(cond_cols, s)
    grad_time = jnp.dot(embed_all.T, cond_sum, precision=highest)
    return (result[None], grad_tokens[None], grad_qkv, grad_proj, grad_up, grad_down, grad_time)


NT = (((1,), (1,)), ((), ()))
TN = (((0,), (0,)), ((), ()))
VMEM = pl.BlockSpec(memory_space=pltpu.VMEM)
SMEM = pl.BlockSpec(memory_space=pltpu.SMEM)
LANES = 128


def call(kernel, name, outs, me, *operands, scratch=(), fetch=(), store=(), limit=12):
    count, total = len(operands), len(operands) + len(outs)
    held = [(operands[n].shape, operands[n].dtype) for n in fetch] + [outs[n] for n in store]

    def body(me_ref, *refs):
        inputs, results, rest = list(refs[:count]), list(refs[count:total]), refs[total:]
        buffers, rest = rest[: len(held)], rest[len(held) :]
        sems, rest = (rest[0], rest[1:]) if held else (None, rest)
        copies = []
        for k, n in enumerate(fetch):
            copies.append(pltpu.make_async_copy(inputs[n], buffers[k], sems.at[k]))
            inputs[n] = buffers[k]
        for copy in copies:
            copy.start()
        for copy in copies:
            copy.wait()
        copies = []
        for k, n in enumerate(store, len(fetch)):
            copies.append(pltpu.make_async_copy(buffers[k], results[n], sems.at[k]))
            results[n] = buffers[k]
        kernel(me_ref, *inputs, *results, *rest)
        for copy in copies:
            copy.start()
        for copy in copies:
            copy.wait()

    own = [pltpu.VMEM(shape, kind) for shape, kind in held]
    own += [pltpu.SemaphoreType.DMA((len(held),))] if held else []
    size = sum(math.prod(shape) * jnp.dtype(kind).itemsize for shape, kind in held)
    far = pl.BlockSpec(memory_space=pltpu.HBM)
    results = pl.pallas_call(
        body,
        name=name,
        out_shape=[jax.ShapeDtypeStruct(shape, kind) for shape, kind in outs],
        in_specs=[SMEM] + [far if n in fetch else VMEM for n in range(count)],
        out_specs=[far if n in store else VMEM for n in range(len(outs))],
        scratch_shapes=own + list(scratch),
        compiler_params=pltpu.CompilerParams(vmem_limit_bytes=limit * 2**20 + size),
        cost_estimate=pl.CostEstimate(flops=0, bytes_accessed=0, transcendentals=0),
    )(me, *operands)
    return list(results)


def dot(left, right, dims=(((1,), (0,)), ((), ()))):
    return lax.dot_general(left, right, dims, preferred_element_type=f32)


def lanes(start, size):
    return pl.ds(pl.multiple_of(start, LANES), size)


def partner(values_in):
    half = HEAD_DIM // 2
    lane = lax.broadcasted_iota(jnp.int32, values_in.shape, 1)
    return jnp.where(
        lane % HEAD_DIM < half,
        pltpu.roll(values_in, values_in.shape[1] - half, 1),
        pltpu.roll(values_in, half, 1),
    )


def pick_first_kernel(me, w_qkv, w_out, out):
    width = w_out.shape[1]
    group = width // 4
    for part in range(3):
        out[:, part * group : (part + 1) * group] = w_qkv[
            :, lanes(part * width + me[2] * group, group)
        ]
    out[:, 3 * group :] = w_out[...]


def pick_rest_kernel(me, w_up, cot, *outs):
    part = w_up.shape[0]
    units = w_up.shape[1] // 4
    for r, out in enumerate(outs):
        out[:part, :] = w_up[:, lanes((me[0] ^ r) * units, units)]
        out[part:, :] = cot[...]


def stack_kernel(me, *refs):
    pieces, out = refs[:-1], refs[-1]
    part = out.shape[0] // 4
    for r, piece in enumerate(pieces):
        out[lanes((me[0] ^ r) * part, part), :] = piece[:part, :]


def weave_kernel(me, mine, theirs, *outs):
    core = me[1]
    rows = mine.shape[0] // 4
    for half, owner in ((mine, core), (theirs, 1 - core)):
        for chip in range(4):
            start = 0
            for out in outs:
                stop = start + out.shape[1]
                out[lanes((2 * chip + owner) * rows, rows), :] = half[
                    chip * rows : (chip + 1) * rows, start:stop
                ]
                start = stop


def qkv_kernel(me, *refs):
    own, a1, a2, a3, b1, b2 = refs[:6]
    scale, shift, weight, cosine, sine, q_out, k_out, v_out, normed, input_a, *again = refs[6:]
    ends = (me[2] == 0) | (me[2] == 3)
    rows, group = own.shape[0], q_out.shape[1]
    for s, (one, two) in enumerate(((own, None), (a1, None), (a2, b2), (a3, b1))):
        at = slice(s * rows, (s + 1) * rows)
        block = one[...].astype(f32)
        if two is not None:
            block = jnp.where(ends, block, two[...].astype(f32))
        centred, _ = normalize(block)
        normed[at, :] = centred.astype(bf16)
        low = (centred * (1.0 + scale[...]) + shift[...]).astype(bf16)
        input_a[at, :] = low
        for part, out in enumerate((q_out, k_out, v_out)):
            projected = dot(low, weight[:, part * group : (part + 1) * group])
            if part == 2:
                out[at, :] = projected.astype(bf16)
                continue
            for j in range(0, group, LANES):
                piece = projected[:, j : j + LANES]
                piece = piece * cosine[at, :] + partner(piece) * sine[at, :]
                if part == 0:
                    piece = piece * (1.0 / math.sqrt(HEAD_DIM))
                out[at, j : j + LANES] = piece.astype(bf16)
    for ref, kept in zip(again, (q_out, k_out, v_out, cosine, sine)):
        ref[...] = kept[...]


def attend_kernel(me, queries, keys, values, out, log_total):
    count, group = queries.shape
    step = 512
    lane = lax.broadcasted_iota(jnp.int32, (step, LANES), 1)

    def block(i, carry):
        at = pl.ds(pl.multiple_of(i * step, step), step)
        stats = jnp.zeros((step, LANES), f32)
        for j in range(group // LANES):
            cols = slice(j * LANES, (j + 1) * LANES)
            halves = []
            for side in range(2):
                query = jnp.where(
                    lane // HEAD_DIM == side, queries[at, cols], jnp.zeros((), bf16)
                )
                scores = dot(query, keys[:, cols], NT)
                top = jnp.max(scores, axis=1, keepdims=True)
                exponent = jnp.exp(scores - top)
                total = jnp.sum(exponent, axis=1, keepdims=True)
                halves.append(dot(exponent.astype(bf16), values[:, cols]) / total)
                stats = jnp.where(lane == 2 * j + side, top + jnp.log(total), stats)
            out[at, cols] = jnp.where(lane < HEAD_DIM, halves[0], halves[1]).astype(bf16)
        log_total[:, at] = jnp.transpose(stats)[:8]
        return carry

    lax.fori_loop(0, count // step, block, 0)


def attend_back_kernel(
    me, queries, keys, values, g0, g1, g2, g3, log_total, cosine, sine, out, key_sum, value_sum, query_t
):
    count, group = queries.shape
    step = 512
    rows = g0.shape[0]
    pieces = (g0, g1, g2, g3)
    keys_t = jnp.transpose(keys[...])
    lane = lax.broadcasted_iota(jnp.int32, (step, LANES), 1)
    for j in range(group // LANES):
        cols = slice(j * LANES, (j + 1) * LANES)
        for i in range(0, count, step):
            at = slice(i, i + step)
            grad = jnp.concatenate(
                [pieces[(i + n) // rows][:, cols] for n in range(0, step, rows)], axis=0
            )
            for side in range(2):
                head = 2 * j + side
                mine = slice(head * HEAD_DIM, (head + 1) * HEAD_DIM)
                keep = lane // HEAD_DIM == side
                query = jnp.where(keep, queries[at, cols], jnp.zeros((), bf16))
                grad_mine = jnp.where(keep, grad, jnp.zeros((), bf16))
                probs = jnp.exp(dot(keys[:, cols], query, NT) - log_total[head : head + 1, at])
                grad_probs = dot(values[:, cols], grad_mine, NT)
                delta = jnp.sum(probs * grad_probs, axis=0, keepdims=True)
                grad_scores = (probs * (grad_probs - delta)).astype(bf16)
                value_part = dot(probs.astype(bf16), grad_mine)
                key_part = dot(grad_scores, query)
                if i == 0 and side == 0:
                    value_sum[...] = value_part
                    key_sum[...] = key_part
                else:
                    value_sum[...] += value_part
                    key_sum[...] += key_part
                query_t[mine, at] = dot(keys_t[mine], grad_scores)
        turned = key_sum[...]
        turned = turned * cosine[...] - partner(turned) * sine[...]
        out[:, group + j * LANES : group + (j + 1) * LANES] = turned.astype(bf16)
        out[:, 2 * group + j * LANES : 2 * group + (j + 1) * LANES] = value_sum[...].astype(bf16)
        turned = jnp.transpose(query_t[cols, :]) * (1.0 / math.sqrt(HEAD_DIM))
        turned = turned * cosine[...] - partner(turned) * sine[...]
        out[:, cols] = turned.astype(bf16)


def middle_kernel(me, source, p0, p1, p2, p3, out_all, scale, shift, mixed, middle, input_b):
    place = me[2]
    group = p0.shape[1]
    for s, piece in enumerate((p0, p1, p2, p3)):
        mixed[:, lanes((place ^ s) * group, group)] = piece[...]
    value = source[...].astype(f32) + dot(mixed[...], out_all[...])
    middle[...] = value
    normed, _ = normalize(value)
    input_b[...] = (normed * (1.0 + scale[...]) + shift[...]).astype(bf16)


def ffn_kernel(
    me, inputs, packed, up, down_own, down_other, grad_in, out, hidden, grad_upper, grad_sum, out_sum
):
    core = me[1]
    units = down_own.shape[0]
    cot = packed[packed.shape[0] - inputs.shape[0] :, :]
    for n, (down, owner) in enumerate(((down_own, core), (down_other, 1 - core))):
        cols = lanes(owner * units, units)
        upper = dot(inputs[...], up[:, cols])
        bell = 0.5 + 0.5 * lax.erf(upper * math.sqrt(0.5))
        slope = bell + upper * jnp.exp(upper * upper * -0.5) * (1.0 / math.sqrt(2.0 * math.pi))
        grad = (dot(cot, down[...], NT) * slope).astype(bf16)
        grad_upper[:, cols] = grad
        value = (upper * bell).astype(bf16)
        hidden[:, n * units : (n + 1) * units] = value
        if n == 0:
            grad_sum[...] = dot(grad, up[:, cols], NT)
            out_sum[...] = dot(value, down[...])
        else:
            grad_in[...] = (grad_sum[...] + dot(grad, up[:, cols], NT)).astype(grad_in.dtype)
            out[...] = (out_sum[...] + dot(value, down[...])).astype(out.dtype)


def grad_down_kernel(me, *refs):
    hidden, cots, (give, keep) = refs[:4], refs[4:8], refs[8:]
    units = keep.shape[0]
    rows = hidden[0].shape[0]
    for out, start in ((give, units), (keep, 0)):
        total = None
        for left, packed in zip(hidden, cots):
            cot = packed[packed.shape[0] - rows :, :]
            term = dot(left[:, start : start + units], cot, TN)
            total = term if total is None else total + term
        out[...] = total.astype(out.dtype)


def grad_up_kernel(me, *refs):
    grads, tokens, (give, keep) = refs[:4], refs[4:8], refs[8:]
    core = me[1]
    part = keep.shape[0] // 4
    grad = jnp.concatenate([ref[...] for ref in grads], axis=0)
    for out, owner in ((give, 1 - core), (keep, core)):
        for chip in range(4):
            cols = lanes((2 * chip + owner) * part, part)
            left = jnp.concatenate([ref[:, cols] for ref in tokens], axis=0)
            out[chip * part : (chip + 1) * part, :] = dot(left, grad, TN).astype(out.dtype)


def pair_up_kernel(me, keep, take, proj_keep, proj_take, *outs):
    chip = me[0]
    part, width = keep.shape[0] // 4, keep.shape[1]
    for r, out in enumerate(outs):
        at = lanes((chip ^ r) * part, part)
        out[:, :width] = (keep[at, :] + take[at, :].astype(f32)).astype(out.dtype)
        out[:, width:] = (proj_keep[at, :] + proj_take[at, :].astype(f32)).astype(out.dtype)


def halve_kernel(me, keep, take, mine, send):
    low = lax.rem(me[2], 2)
    half = mine.shape[0]
    at = lanes(low * half, half)
    mine[...] = keep[at, :] + take[at, :].astype(f32)
    at = lanes((1 - low) * half, half)
    send[...] = (keep[at, :] + take[at, :].astype(f32)).astype(bf16)


def halve_across_kernel(me, mine, take, held, send):
    half = held.shape[0]
    high = lax.div(me[2], 2)
    at = pl.ds(pl.multiple_of(high * half, half), half)
    held[...] = mine[at, :] + take[at, :].astype(f32)
    at = pl.ds(pl.multiple_of((1 - high) * half, half), half)
    send[...] = (mine[at, :] + take[at, :].astype(f32)).astype(bf16)


def collect_kernel(me, p0, p1, p2, p3, out):
    chip = me[0]
    width = p0.shape[1] // 2
    total = None
    for r, piece in enumerate((p0, p1, p2, p3)):
        out[:, lanes((chip ^ r) * width, width)] = piece[:, :width].astype(out.dtype)
        term = piece[:, width:].astype(f32)
        total = term if total is None else total + term
    out[:, 4 * width :] = total.astype(out.dtype)


def back_b_kernel(
    me, g0, g1, g2, g3, middle, cot, scale, out_all,
    grad_middle, branch, sums, h0, h1, h2, h3,
):
    place = me[2]
    group = h0.shape[1]
    normed, inverse = normalize(middle[...])
    grad_in = g0[...]
    for more in (g1, g2, g3):
        grad_in = grad_in + more[...].astype(f32)
    sums[0:1, :] = jnp.sum(grad_in * normed, axis=0, keepdims=True)
    sums[1:2, :] = jnp.sum(grad_in, axis=0, keepdims=True)
    grad = cot[...].astype(f32) + norm_back(grad_in * (1.0 + scale[...]), normed, inverse)
    grad_middle[...] = grad
    low = grad.astype(bf16)
    branch[...] = low
    for s, piece in enumerate((h0, h1, h2, h3)):
        at = pl.ds(pl.multiple_of((place ^ s) * group, group), group)
        piece[...] = dot(low, out_all[at, :], NT).astype(bf16)


def back_a_kernel(me, grad_projected, weight, normed, own, across, pair, sums):
    rows = own.shape[0]
    first = second = None
    for s in (1, 3, 2, 0):
        at = slice(s * rows, (s + 1) * rows)
        grad = dot(grad_projected[at, :], weight[...], NT)
        if s % 2:
            pair[s // 2 * rows : (s // 2 + 1) * rows, :] = grad.astype(bf16)
        else:
            (across if s else own)[...] = grad
        one = jnp.sum(grad * normed[at, :].astype(f32), axis=0, keepdims=True)
        two = jnp.sum(grad, axis=0, keepdims=True)
        first, second = (one, two) if first is None else (first + one, second + two)
    sums[0:1, :] = first
    sums[1:2, :] = second


def grad_qkv_kernel(me, input_a, grad_projected, give, keep):
    core = me[1]
    part = keep.shape[0] // 4
    for out, owner in ((give, 1 - core), (keep, core)):
        for chip in range(4):
            cols = lanes((2 * chip + owner) * part, part)
            out[chip * part : (chip + 1) * part, :] = dot(
                input_a[:, cols], grad_projected[...], TN
            ).astype(out.dtype)


def pair_kernel(me, keep, take, *outs):
    chip = me[0]
    part = keep.shape[0] // 4
    for r, out in enumerate(outs):
        at = lanes((chip ^ r) * part, part)
        out[...] = (keep[at, :] + take[at, :].astype(f32)).astype(out.dtype)


def tokens_kernel(me, own, pair, across, source, scale, grad_middle, out):
    rows = own.shape[0]
    grad_in = own[...] + pair[:rows, :].astype(f32) + across[...].astype(f32)
    normed, inverse = normalize(source[...].astype(f32))
    out[...] = grad_middle[...] + norm_back(grad_in * (1.0 + scale[...]), normed, inverse)


def finish_qkv_kernel(me, p0, p1, p2, p3, out):
    place = me[2]
    group = p0.shape[1] // 3
    width = out.shape[1] // 3
    for s, piece in enumerate((p0, p1, p2, p3)):
        for part in range(3):
            at = part * width + (place ^ s) * group
            out[:, lanes(at, group)] = piece[:, part * group : (part + 1) * group].astype(f32)


def swap_seq(values_in, bits):
    return lax.ppermute(values_in, "seq", [(i, i ^ bits) for i in range(4)])


def halve_pair(values_in, place):
    half = values_in.shape[0] // 2
    mine = lax.dynamic_slice_in_dim(values_in, place % 2 * half, half)
    other = lax.dynamic_slice_in_dim(values_in, (1 - place % 2) * half, half)
    return mine, other.astype(bf16)


class Halving:
    def __init__(self, held, send, place):
        self.held, self.send, self.low, self.high = held, send, place % 2, place // 2

    def across_ready(self, me):
        rows, cols = self.held.shape
        half = ((rows // 2, cols), f32), ((rows // 2, cols), bf16)
        self.held, self.send = call(
            halve_across_kernel, "halve", half, me, self.held, swap_seq(self.send, 1)
        )

    def across(self):
        self.got = swap_seq(self.send, 2)

    def across_done(self, *others):
        self.held = (self.held + tie(self.got, *others)[0].astype(f32)).astype(bf16)

    def join(self, bit, bits):
        other = swap_seq(self.held, bits)
        first = jnp.where(bit == 0, self.held, other)
        second = jnp.where(bit == 0, other, self.held)
        self.held = jnp.concatenate([first, second], axis=0)

    def back_across(self):
        self.join(self.high, 2)

    def back_pair(self):
        self.join(self.low, 1)


def outward(values_in):
    return lax.ppermute(values_in, "seq", [(1, 0), (2, 3)])


def middle_swap(values_in):
    return lax.ppermute(values_in, "seq", [(1, 2), (2, 1)])


def tie(*values_in):
    return lax.optimization_barrier(values_in)


def spread(values_in):
    return [values_in] + [hop(values_in, 2 * r) for r in range(1, 4)]


def deal(blocks):
    return [blocks[0]] + [hop(blocks[r].astype(bf16), 2 * r) for r in range(1, 4)]


def total_of(pieces):
    total = pieces[0]
    for piece in pieces[1:]:
        total = total + piece.astype(f32)
    return total


def per_device(tokens, noise_steps, w_qkv, w_out, w_up, w_down, w_time, cotangent):
    index, place = lax.axis_index("dp"), lax.axis_index("seq")
    me = jnp.stack([index // 2, index % 2, place]).astype(jnp.int32)
    _, rows, width = tokens.shape
    group = width // 4
    count = 4 * rows
    part = w_out.shape[0]
    units = w_down.shape[0]
    source, cot = tokens[0], cotangent[0]

    half = HEAD_DIM // 2
    lane = jnp.arange(LANES)
    frequency = jnp.exp(-math.log(10000.0) * (lane % half).astype(f32) / half)
    block_place = place ^ jnp.arange(4)
    positions = (block_place[:, None] * rows + jnp.arange(rows)).reshape(-1).astype(f32)
    angles = positions[:, None] * frequency
    cosine = jnp.cos(angles)
    sine = jnp.sin(angles) * jnp.where(lane % HEAD_DIM < half, -1.0, 1.0)

    a1, b1 = swap_seq(source, 1), middle_swap(source)
    size = 3 * group + width
    (first,) = call(
        pick_first_kernel,
        "pick_first",
        [((part, size), bf16)],
        me,
        w_qkv,
        w_out,
        fetch=(0, 1),
    )
    steps_all = lax.all_to_all(
        jnp.broadcast_to(noise_steps.astype(f32), (8,)),
        "dp",
        split_axis=0,
        concat_axis=0,
        tiled=True,
    )
    first, steps_all = tie(first, steps_all)
    first_mine = spread(first)
    a1, b1 = tie(a1, b1)

    a2, b2 = outward(b1), middle_swap(a1)
    packed = call(
        pick_rest_kernel,
        "pick_rest",
        [((part + rows, width), bf16)] * 4,
        me,
        w_up,
        cot,
        fetch=(0, 1),
        store=(0, 1, 2, 3),
    )
    embed_all = time_embedding(steps_all)
    cond_part = jnp.dot(embed_all, w_time.astype(f32), precision=highest)
    condition = lax.all_to_all(cond_part, "dp", split_axis=0, concat_axis=0, tiled=True).reshape(
        4, width
    )
    a2, b2, condition, cosine, sine, down_late, *more = tie(
        a2, b2, condition, cosine, sine, w_down, *first_mine, *packed
    )
    first_mine, packed = more[:4], more[4:]

    a3 = outward(b2)
    (first_half,) = call(
        stack_kernel, "stack_first", [((4 * part, size), bf16)], me, *first_mine, store=(0,)
    )
    first_half, *packed = tie(first_half, *packed)
    packed = deal(packed)
    qkv_all, out_all = call(
        weave_kernel,
        "weave_first",
        [((width, 3 * group), bf16), ((width, width), bf16)],
        me,
        first_half,
        hop(first_half, 1),
        fetch=(0, 1),
    )
    a3, qkv_all = tie(a3, qkv_all)
    scale_a, shift_a, scale_b, shift_b = [condition[i : i + 1] for i in range(4)]

    queries, keys, values, normed_a, input_a, *kept = call(
        qkv_kernel,
        "qkv",
        [((count, group), bf16)] * 3
        + [((count, width), bf16)] * 2
        + [((count, group), bf16)] * 3
        + [((count, LANES), f32)] * 2,
        me,
        source,
        a1,
        a2,
        a3,
        b1,
        b2,
        scale_a,
        shift_a,
        qkv_all,
        cosine,
        sine,
        store=(3, 4, 5, 6, 7, 8, 9),
    )
    attended, log_total = call(
        attend_kernel,
        "attend",
        [((count, group), bf16), ((8, count), f32)],
        me,
        queries,
        keys,
        values,
    )
    attended, packed[1] = tie(attended, packed[1])
    pieces = [attended[:rows]] + [
        swap_seq(attended[s * rows : (s + 1) * rows], s) for s in range(1, 4)
    ]
    *pieces, packed[2], packed[3] = tie(*pieces, packed[2], packed[3])
    (up_half,) = call(
        stack_kernel, "stack_up", [((4 * part, width), bf16)], me, *packed, fetch=(0, 1, 2, 3)
    )
    down_other = hop(down_late, 1)
    up_other = hop(up_half, 1)
    mixed, middle, input_b = call(
        middle_kernel,
        "middle",
        [((rows, width), bf16), ((rows, width), f32), ((rows, width), bf16)],
        me,
        source,
        *pieces,
        out_all,
        scale_b,
        shift_b,
    )

    toks = [input_b, hop(input_b, 2), None, hop(input_b, 6)]
    up_half, up_other, toks[0] = tie(up_half, up_other, toks[0])
    (up_all,) = call(
        weave_kernel, "weave_up", [((width, width), bf16)], me, up_half, up_other
    )
    grads, outs, hidden, grad_upper = [None] * 4, [None] * 4, [None] * 4, [None] * 4
    last = None
    for r in (0, 3, 1, 2):
        if r:
            toks[r], hidden[last] = tie(toks[r], hidden[last])
        if r == 3:
            late, toks[3] = tie(input_b, toks[3])
            toks[2] = hop(late, 4)
        if r == 2:
            toks[2], grads[3] = tie(toks[2], grads[3])
        grads[r], outs[r], hidden[r], grad_upper[r] = call(
            ffn_kernel,
            "ffn",
            [((rows, width), bf16 if r else f32)] * 2 + [((rows, 2 * units), bf16)] * 2,
            me,
            toks[r],
            packed[r],
            up_all,
            w_down,
            down_other,
            scratch=[pltpu.VMEM((rows, width), f32)] * 2,
        )
        if r:
            grads[r] = hop(grads[r], 2 * r)
        last = r

    hidden[0], grad_upper[0], grads[1], grads[3] = tie(
        hidden[0], grad_upper[0], grads[1], grads[3]
    )
    give, keep = call(
        grad_down_kernel,
        "grad_down",
        [((units, width), bf16), ((units, width), f32)],
        me,
        *hidden,
        *packed,
        fetch=tuple(range(8)),
    )
    down_give, down_keep = give, keep
    up_give, up_keep = call(
        grad_up_kernel,
        "grad_up",
        [((width // 2, width), bf16), ((width // 2, width), f32)],
        me,
        *grad_upper,
        *toks,
        store=(0, 1),
    )
    grads[2], down_give, up_give = tie(grads[2], down_give, up_give)
    down_take, up_take = hop(down_give, 1), hop(up_give, 1)
    grad_middle, branch, sums_b, *to_heads = call(
        back_b_kernel,
        "back_b",
        [((rows, width), f32), ((rows, width), bf16), ((2, width), f32)]
        + [((rows, group), bf16)] * 4,
        me,
        *grads,
        middle,
        cot,
        scale_b,
        out_all,
    )
    proj_give, proj_keep = call(
        grad_qkv_kernel,
        "grad_proj",
        [((width // 2, width), bf16), ((width // 2, width), f32)],
        me,
        mixed,
        branch,
        store=(0, 1),
    )
    proj_give, *to_heads = tie(proj_give, *to_heads)
    grad_heads = [to_heads[0]] + [swap_seq(to_heads[s], s) for s in range(1, 4)]
    down_mine, down_send = call(
        halve_kernel,
        "halve_down",
        [((units // 2, width), f32), ((units // 2, width), bf16)],
        me,
        down_keep,
        down_take,
    )
    up_parts = call(
        pair_up_kernel,
        "pair_up",
        [((part, 2 * width), f32)] + [((part, 2 * width), bf16)] * 3,
        me,
        up_keep,
        up_take,
        proj_keep,
        hop(proj_give, 1),
        fetch=(0, 1, 2, 3),
        store=(0, 1, 2, 3),
    )
    *grad_heads, down_mine, down_send, up_parts[0] = tie(
        *grad_heads, down_mine, down_send, up_parts[0]
    )

    up_parts = deal(up_parts)
    down_sum = Halving(down_mine, down_send, place)
    down_sum.across_ready(me)
    (grad_projected,) = call(
        attend_back_kernel,
        "attend_back",
        [((count, 3 * group), bf16)],
        me,
        *kept[:3],
        *grad_heads,
        log_total,
        *kept[3:],
        scratch=[pltpu.VMEM((count, LANES), f32)] * 2 + [pltpu.VMEM((group, count), f32)],
        fetch=(0, 1, 2, 8, 9),
    )
    grad_a, p2, pair, sums_a = call(
        back_a_kernel,
        "back_a",
        [((rows, width), f32)] * 2 + [((2 * rows, width), bf16), ((2, width), f32)],
        me,
        grad_projected,
        qkv_all,
        normed_a,
        fetch=(2,),
        store=(0, 1, 2),
    )
    pair = swap_seq(pair, 1)

    down_sum.held, down_sum.send, p2 = tie(down_sum.held, down_sum.send, p2)
    down_sum.across()
    (both,) = call(
        collect_kernel,
        "collect",
        [((part, 5 * width), f32)],
        me,
        *up_parts,
        fetch=(0, 1, 2, 3),
    )
    up_mine, up_send = halve_pair(both, place)
    up_sum = Halving(up_mine, up_send, place)
    give, keep = call(
        grad_qkv_kernel,
        "grad_qkv",
        [((width // 2, 3 * group), bf16), ((width // 2, 3 * group), f32)],
        me,
        input_a,
        grad_projected,
        fetch=(0,),
    )
    take, both = tie(hop(give, 1), both)
    qkv_parts = call(
        pair_kernel,
        "pair",
        [((part, 3 * group), f32)] + [((part, 3 * group), bf16)] * 3,
        me,
        keep,
        take,
    )
    sums_a, qkv_parts[1] = tie(sums_a, qkv_parts[1])
    qkv_parts = deal(qkv_parts)
    grad_condition = jnp.concatenate([sums_a, sums_b], axis=0)
    cond_cols = lax.all_to_all(
        grad_condition.reshape(8, -1), "dp", split_axis=0, concat_axis=0, tiled=True
    )
    qkv_cols = total_of(qkv_parts).astype(bf16)
    down_sum.across_done(qkv_cols, cond_cols)
    pair, up_sum.held, up_sum.send, down_sum.held, cond_cols, qkv_cols, *outs = tie(
        pair, up_sum.held, up_sum.send, down_sum.held, cond_cols, qkv_cols, *outs
    )

    across = swap_seq((p2 + pair[rows:].astype(f32)).astype(bf16), 2)
    up_sum.across_ready(me)
    outs = deal(outs)
    across, up_sum.held, up_sum.send, down_sum.held, qkv_cols, cond_cols, *outs = tie(
        across, up_sum.held, up_sum.send, down_sum.held, qkv_cols, cond_cols, *outs
    )

    up_sum.across()
    down_sum.back_across()
    qkv_pair = swap_seq(qkv_cols, 1)
    up_sum.across_done()
    cond_sum = cond_cols + swap_seq(cond_cols, 1)
    (grad_tokens,) = call(
        tokens_kernel,
        "tokens",
        [((rows, width), f32)],
        me,
        grad_a,
        pair,
        across,
        source,
        scale_a,
        grad_middle,
    )
    up_sum.held, down_sum.held, qkv_pair, cond_sum, *outs = tie(
        up_sum.held, down_sum.held, qkv_pair, cond_sum, *outs
    )

    up_sum.back_across()
    down_sum.back_pair()
    cond_sum = cond_sum + swap_seq(cond_sum, 2)
    result = (middle + total_of(outs)).astype(bf16)
    up_sum.held, qkv_pair = tie(up_sum.held, qkv_pair)

    qkv_far = swap_seq(jnp.stack([qkv_cols, qkv_pair]), 2)
    up_sum.back_pair()
    cond_sum, qkv_far = tie(cond_sum, qkv_far)
    grad_time = jnp.dot(embed_all.T, cond_sum, precision=highest)
    (grad_qkv,) = call(
        finish_qkv_kernel,
        "finish_qkv",
        [((part, 3 * width), f32)],
        me,
        qkv_cols,
        qkv_pair,
        qkv_far[0],
        qkv_far[1],
    )
    grad_down, both = down_sum.held, up_sum.held
    return (
        result[None],
        grad_tokens[None],
        grad_qkv,
        both[:, 4 * width :].astype(f32),
        both[:, : 4 * width].astype(f32),
        grad_down.astype(f32),
        grad_time,
    )


def solution(mesh):
    in_specs = (
        P("dp", "seq", None),
        P("dp"),
        P("dp", None),
        P("dp", None),
        P("dp", None),
        P("dp", None),
        P(None, "dp"),
        P("dp", "seq", None),
    )
    out_specs = (
        P("dp", "seq", None),
        P("dp", "seq", None),
        P("dp", None),
        P("dp", None),
        P("dp", None),
        P("dp", None),
        P(None, "dp"),
    )
    square = mesh.shape["dp"] == 8 and mesh.shape["seq"] == 4
    return jax.shard_map(
        per_device if square else per_device_any, mesh=mesh, in_specs=in_specs, out_specs=out_specs, check_vma=False
    )
```

```python
from functools import partial
import math

import jax
import jax.numpy as jnp
from jax import lax
from jax.experimental import pallas as pl
from jax.experimental.pallas import tpu as pltpu
from jax.sharding import PartitionSpec as P

HEAD_DIM = 64
TE = 256

highest = lax.Precision.HIGHEST
bf16 = jnp.bfloat16
f32 = jnp.float32


def normalize(values_in):
    centered = values_in - jnp.mean(values_in, axis=-1, keepdims=True)
    inverse = lax.rsqrt(jnp.mean(centered * centered, axis=-1, keepdims=True) + 1e-05)
    return (centered * inverse, inverse)


def norm_back(gradient, normed, inverse):
    return inverse * (
        gradient
        - jnp.mean(gradient, axis=-1, keepdims=True)
        - normed * jnp.mean(gradient * normed, axis=-1, keepdims=True)
    )


def time_embedding(noise_step):
    half_dim = TE // 2
    frequency = jnp.exp(-math.log(10000.0) * jnp.arange(half_dim, dtype=f32) / half_dim)
    angles = noise_step.astype(f32)[..., None] * frequency
    return jnp.concatenate([jnp.sin(angles), jnp.cos(angles)], axis=-1)


def rotate(values_in, positions, direction):
    half_dim = values_in.shape[-1] // 2
    frequency = jnp.exp(-math.log(10000.0) * jnp.arange(half_dim, dtype=f32) / half_dim)
    angles = positions[:, None, None] * frequency
    cosine = jnp.cos(angles)
    sine_wave = direction * jnp.sin(angles)
    first_half = values_in[..., :half_dim]
    second_half = values_in[..., half_dim:]
    return jnp.concatenate(
        [
            first_half * cosine - second_half * sine_wave,
            first_half * sine_wave + second_half * cosine,
        ],
        axis=-1,
    )


def hop(values_in, bit):
    count = lax.axis_size("dp")
    return lax.ppermute(values_in, "dp", [(i, i ^ bit) for i in range(count)])


def core_groups():
    count = lax.axis_size("dp")
    return [[i for i in range(count) if i % 2 == core] for core in range(2)]


def gather_chips(block):
    chips = lax.axis_size("dp") // 2
    if chips != 4:
        return lax.all_gather(block, "dp", axis=0, tiled=True, axis_index_groups=core_groups())
    rows = block.shape[0]
    half = rows // 2
    chip = lax.axis_index("dp") // 2
    from_x = hop(block, 2)
    from_y = hop(block, 4)
    far_top = hop(from_y[:half], 2)
    far_low = hop(from_x[half:], 4)
    out = jnp.zeros((chips * rows,) + block.shape[1:], block.dtype)
    for piece, other, shift in (
        (block, 0, 0),
        (from_x, 1, 0),
        (from_y, 2, 0),
        (far_top, 3, 0),
        (far_low, 3, half),
    ):
        out = lax.dynamic_update_slice_in_dim(out, piece, (chip ^ other) * rows + shift, axis=0)
    return out


def scatter_chips(parts):
    chips = lax.axis_size("dp") // 2
    if chips != 4:
        flat = parts.reshape((-1,) + parts.shape[2:])
        return lax.psum_scatter(
            flat, "dp", scatter_dimension=0, tiled=True, axis_index_groups=core_groups()
        ).astype(f32)
    half = parts.shape[1] // 2
    chip = lax.axis_index("dp") // 2
    own, to_x, to_y, to_far = [
        lax.dynamic_index_in_dim(parts, chip ^ other, 0, keepdims=False) for other in range(4)
    ]
    on_x = hop(to_far[:half], 2)
    on_y = hop(to_far[half:], 4)
    to_y = jnp.concatenate([to_y[:half] + on_x, to_y[half:]], axis=0)
    to_x = jnp.concatenate([to_x[:half], to_x[half:] + on_y], axis=0)
    return own.astype(f32) + hop(to_x, 2).astype(f32) + hop(to_y, 4).astype(f32)


def both_cores(half_block):
    chips = lax.axis_size("dp") // 2
    core = lax.axis_index("dp") % 2
    other = hop(half_block, 1)
    shape = (chips, half_block.shape[0] // chips) + half_block.shape[1:]
    mine, theirs = half_block.reshape(shape), other.reshape(shape)
    first = jnp.where(core == 0, mine, theirs)
    second = jnp.where(core == 0, theirs, mine)
    joined = jnp.stack([first, second], axis=1)
    return joined.reshape((-1,) + half_block.shape[1:])


def sum_cores(full):
    count = lax.axis_size("dp")
    core = lax.axis_index("dp") % 2
    view = full.reshape((count // 2, 2, full.shape[0] // count) + full.shape[1:])
    mine = lax.dynamic_index_in_dim(view, core, 1, keepdims=False)
    theirs = lax.dynamic_index_in_dim(view, 1 - core, 1, keepdims=False)
    return (mine.astype(f32) + hop(theirs.astype(bf16), 1).astype(f32)).astype(bf16)


def turn(values_in, step):
    count = lax.axis_size("seq")
    return lax.ppermute(values_in, "seq", [(i, (i + step) % count) for i in range(count)])


def shift(values_in, step):
    count = lax.axis_size("seq")
    return lax.ppermute(
        values_in, "seq", [(i, i + step) for i in range(count) if 0 <= i + step < count]
    )


def gather_seq(block):
    count = lax.axis_size("seq")
    place = lax.axis_index("seq")
    lower, upper = [block], [block]
    for _ in range(count - 1):
        lower.append(shift(lower[-1], 1))
        upper.append(shift(upper[-1], -1))
    return [block] + [
        jnp.where(place + step < count, upper[step], lower[count - step])
        for step in range(1, count)
    ]


def scatter_seq(blocks):
    count = len(blocks)
    right = left = None
    for step in range(1, count):
        going_right = blocks[count - step]
        going_left = blocks[step]
        if right is not None:
            going_right = going_right + right.astype(f32)
            going_left = going_left + left.astype(f32)
        right = shift(going_right.astype(bf16), 1)
        left = shift(going_left.astype(bf16), -1)
    return blocks[0] + right.astype(f32) + left.astype(f32)


def sum_seq(values_in):
    count = lax.axis_size("seq")
    if count != 4:
        return lax.psum(values_in.astype(bf16), "seq").astype(f32)
    place = lax.axis_index("seq")
    inner = lax.ppermute(values_in.astype(bf16), "seq", [(0, 1), (3, 2)])
    pair = values_in + inner.astype(f32)
    across = lax.ppermute(pair.astype(bf16), "seq", [(1, 2), (2, 1)])
    total = pair + across.astype(f32)
    outer = lax.ppermute(total.astype(bf16), "seq", [(1, 0), (2, 3)])
    return jnp.where((place == 0) | (place == 3), outer.astype(f32), total)


def attend_forward(queries, key_rows, values):
    scores = jnp.einsum("qhd,khd->hqk", queries, key_rows, preferred_element_type=f32) / math.sqrt(
        HEAD_DIM
    )
    row_top = jnp.max(scores, axis=-1, keepdims=True)
    exponent = jnp.exp(scores - row_top)
    row_total = jnp.sum(exponent, axis=-1, keepdims=True)
    probs = (exponent / row_total).astype(bf16)
    attended = jnp.einsum("hqk,khd->qhd", probs, values, preferred_element_type=f32)
    return attended.astype(bf16), (row_top + jnp.log(row_total))


def attend_backward(queries, key_rows, values, log_total, grad_attn):
    score_scale = 1.0 / math.sqrt(HEAD_DIM)
    scores = (
        jnp.einsum("qhd,khd->hqk", queries, key_rows, preferred_element_type=f32) * score_scale
    )
    probs = jnp.exp(scores - log_total)
    grad_probs = jnp.einsum("qhd,khd->hqk", grad_attn, values, preferred_element_type=f32)
    grad_scores = (
        probs * (grad_probs - jnp.sum(probs * grad_probs, axis=-1, keepdims=True))
    ).astype(bf16)
    grad_queries = (
        jnp.einsum("hqk,khd->qhd", grad_scores, key_rows, preferred_element_type=f32) * score_scale
    )
    grad_keys = (
        jnp.einsum("hqk,qhd->khd", grad_scores, queries, preferred_element_type=f32) * score_scale
    )
    grad_values = jnp.einsum(
        "hqk,qhd->khd", probs.astype(bf16), grad_attn, preferred_element_type=f32
    )
    return grad_queries.astype(bf16), grad_keys.astype(bf16), grad_values.astype(bf16)


def per_device_any(tokens, noise_steps, w_qkv, w_out, w_up, w_down, w_time, cotangent):
    dp_count, seq_parts = lax.axis_size("dp"), lax.axis_size("seq")
    chips = dp_count // 2
    core = lax.axis_index("dp") % 2
    place = lax.axis_index("seq")
    _, rows, width = tokens.shape
    group = width // seq_parts
    source = tokens[0]
    cot = cotangent[0]

    token_blocks = gather_seq(source)

    steps_all = lax.all_to_all(
        jnp.broadcast_to(noise_steps.astype(f32), (dp_count,)),
        "dp",
        split_axis=0,
        concat_axis=0,
        tiled=True,
    )
    embed_all = time_embedding(steps_all)
    cond_part = jnp.dot(embed_all, w_time.astype(f32), precision=highest)
    condition = lax.all_to_all(cond_part, "dp", split_axis=0, concat_axis=0, tiled=True).reshape(
        4, width
    )
    scale_a, shift_a, scale_b, shift_b = [condition[i][None, :] for i in range(4)]

    qkv_cols = lax.dynamic_index_in_dim(
        w_qkv.reshape(-1, 3, seq_parts, group), place, 2, keepdims=False
    ).reshape(-1, 3 * group)
    qkv_all = both_cores(gather_chips(qkv_cols))
    unit_view = w_up.reshape(w_up.shape[0], chips, 2, -1)
    up_mine = lax.dynamic_index_in_dim(unit_view, core, 2, keepdims=False).reshape(
        w_up.shape[0], -1
    )
    up_theirs = lax.dynamic_index_in_dim(unit_view, 1 - core, 2, keepdims=False).reshape(
        w_up.shape[0], -1
    )
    up_other = hop(up_theirs, 1)
    up_block = jnp.where(
        core == 0,
        jnp.concatenate([up_mine, up_other], axis=0),
        jnp.concatenate([up_other, up_mine], axis=0),
    )
    up_all = gather_chips(up_block)
    out_all = both_cores(gather_chips(w_out))
    down_all = gather_chips(w_down)
    cot_both = jnp.concatenate([cot, hop(cot, 1)], axis=0)

    full = jnp.concatenate(token_blocks, axis=0).astype(f32)
    normed_a, inverse_a = normalize(full)
    input_a = (normed_a * (1.0 + scale_a) + shift_a).astype(bf16)
    projected = jnp.dot(input_a, qkv_all, preferred_element_type=f32)
    block_place = (place + jnp.arange(seq_parts)) % seq_parts
    positions = (block_place[:, None] * rows + jnp.arange(rows)).reshape(-1).astype(f32)
    head_view = projected.reshape(seq_parts * rows, 3, -1, HEAD_DIM)
    queries = rotate(head_view[:, 0], positions, 1.0).astype(bf16)
    key_rows = rotate(head_view[:, 1], positions, 1.0).astype(bf16)
    values = head_view[:, 2].astype(bf16)
    attended, log_total = attend_forward(queries, key_rows, values)
    attended = attended.reshape(seq_parts, rows, group)
    pieces = [attended[0]] + [turn(attended[s], s) for s in range(1, seq_parts)]
    stacked = jnp.stack(pieces)
    mixed = jnp.concatenate(
        [
            lax.dynamic_index_in_dim(stacked, (place - g) % seq_parts, 0, keepdims=False)
            for g in range(seq_parts)
        ],
        axis=-1,
    )
    middle = source.astype(f32) + jnp.dot(mixed, out_all, preferred_element_type=f32)
    normed_b, inverse_b = normalize(middle)
    input_b = (normed_b * (1.0 + scale_b) + shift_b).astype(bf16)

    input_both = jnp.concatenate([input_b, hop(input_b, 1)], axis=0)
    upper = jnp.dot(input_both, up_all, preferred_element_type=f32)
    grad_hidden = lax.dot_general(
        cot_both, down_all, (((1,), (1,)), ((), ())), preferred_element_type=f32
    )
    hidden, gelu_pull = jax.vjp(partial(jax.nn.gelu, approximate=False), upper)
    hidden = hidden.astype(bf16)
    grad_upper = gelu_pull(grad_hidden)[0].astype(bf16)
    grad_in_part = lax.dot_general(
        grad_upper, up_all, (((1,), (1,)), ((), ())), preferred_element_type=f32
    )
    grad_in_b = grad_in_part[:rows] + hop(grad_in_part[rows:].astype(bf16), 1).astype(f32)
    out_part = jnp.dot(hidden, down_all, preferred_element_type=f32)
    result = (
        middle + out_part[:rows] + hop(out_part[rows:].astype(bf16), 1).astype(f32)
    ).astype(bf16)

    grad_down_part = lax.dot_general(
        hidden, cot_both, (((0,), (0,)), ((), ())), preferred_element_type=f32
    ).astype(bf16)
    grad_up_part = lax.dot_general(
        input_both, grad_upper, (((0,), (0,)), ((), ())), preferred_element_type=f32
    ).astype(bf16)

    grad_scale_b = jnp.sum(grad_in_b * normed_b, axis=0)
    grad_shift_b = jnp.sum(grad_in_b, axis=0)
    grad_middle = cot.astype(f32) + norm_back(grad_in_b * (1.0 + scale_b), normed_b, inverse_b)
    grad_branch = grad_middle.astype(bf16)
    grad_mixed = lax.dot_general(
        grad_branch, out_all, (((1,), (1,)), ((), ())), preferred_element_type=f32
    ).astype(bf16)
    to_heads = grad_mixed.reshape(rows, seq_parts, group)
    grad_pieces = [
        lax.dynamic_index_in_dim(to_heads, (place - s) % seq_parts, 1, keepdims=False)
        for s in range(seq_parts)
    ]
    grad_attn = jnp.concatenate(
        [grad_pieces[0]] + [turn(grad_pieces[s], -s) for s in range(1, seq_parts)], axis=0
    )
    grad_proj_part = lax.dot_general(
        mixed, grad_branch, (((0,), (0,)), ((), ())), preferred_element_type=f32
    )
    grad_q, grad_k, grad_v = attend_backward(
        queries,
        key_rows,
        values,
        log_total,
        grad_attn.reshape(seq_parts * rows, -1, HEAD_DIM),
    )
    grad_q = rotate(grad_q.astype(f32), positions, -1.0).astype(bf16)
    grad_k = rotate(grad_k.astype(f32), positions, -1.0).astype(bf16)
    grad_projected = jnp.stack([grad_q, grad_k, grad_v], axis=1).reshape(seq_parts * rows, -1)
    grad_in_a_part = lax.dot_general(
        grad_projected, qkv_all, (((1,), (1,)), ((), ())), preferred_element_type=f32
    )
    grad_qkv_part = lax.dot_general(
        input_a, grad_projected, (((0,), (0,)), ((), ())), preferred_element_type=f32
    )
    grad_in_a = scatter_seq(
        [grad_in_a_part[s * rows : (s + 1) * rows] for s in range(seq_parts)]
    )
    grad_scale_a = jnp.sum(grad_in_a_part * normed_a, axis=0)
    grad_shift_a = jnp.sum(grad_in_a_part, axis=0)
    grad_tokens = grad_middle + norm_back(
        grad_in_a * (1.0 + scale_a), normed_a[:rows], inverse_a[:rows]
    )

    grad_down = sum_seq(scatter_chips(grad_down_part.reshape(chips, -1, width)))
    grad_up_rows = scatter_chips(grad_up_part.reshape(chips, -1, grad_up_part.shape[1]))
    up_halves = grad_up_rows.reshape(2, -1, grad_up_rows.shape[1])
    keep = lax.dynamic_index_in_dim(up_halves, core, 0, keepdims=False)
    give = lax.dynamic_index_in_dim(up_halves, 1 - core, 0, keepdims=False)
    keep = keep.reshape(keep.shape[0], chips, -1)
    take = hop(give.astype(bf16), 1).astype(f32).reshape(keep.shape)
    grad_up = sum_seq(
        jnp.stack([jnp.where(core == 0, keep, take), jnp.where(core == 0, take, keep)], axis=2)
        .reshape(keep.shape[0], -1)
    )
    grad_proj = sum_seq(scatter_chips(sum_cores(grad_proj_part)))
    grad_qkv_cols = scatter_chips(sum_cores(grad_qkv_part)).astype(bf16)
    qkv_ring = jnp.stack(gather_seq(grad_qkv_cols))
    grad_qkv = jnp.stack(
        [
            lax.dynamic_index_in_dim(qkv_ring, (g - place) % seq_parts, 0, keepdims=False).reshape(
                -1, 3, group
            )
            for g in range(seq_parts)
        ],
        axis=2,
    )
    grad_qkv = grad_qkv.reshape(-1, 3 * width).astype(f32)
    grad_condition = jnp.concatenate([grad_scale_a, grad_shift_a, grad_scale_b, grad_shift_b])
    cond_cols = lax.all_to_all(
        grad_condition.reshape(dp_count, -1), "dp", split_axis=0, concat_axis=0, tiled=True
    )
    cond_sum = cond_cols
    for s in range(1, seq_parts):
        cond_sum = cond_sum + turn(cond_cols, s)
    grad_time = jnp.dot(embed_all.T, cond_sum, precision=highest)
    return (result[None], grad_tokens[None], grad_qkv, grad_proj, grad_up, grad_down, grad_time)


NT = (((1,), (1,)), ((), ()))
TN = (((0,), (0,)), ((), ()))
VMEM = pl.BlockSpec(memory_space=pltpu.VMEM)
SMEM = pl.BlockSpec(memory_space=pltpu.SMEM)
LANES = 128


def call(kernel, name, outs, me, *operands, scratch=(), fetch=(), store=(), limit=24):
    count, total = len(operands), len(operands) + len(outs)
    held = [(operands[n].shape, operands[n].dtype) for n in fetch] + [outs[n] for n in store]

    def body(me_ref, *refs):
        inputs, results, rest = list(refs[:count]), list(refs[count:total]), refs[total:]
        buffers, rest = rest[: len(held)], rest[len(held) :]
        sems, rest = (rest[0], rest[1:]) if held else (None, rest)
        copies = []
        for k, n in enumerate(fetch):
            copies.append(pltpu.make_async_copy(inputs[n], buffers[k], sems.at[k]))
            inputs[n] = buffers[k]
        for copy in copies:
            copy.start()
        for copy in copies:
            copy.wait()
        copies = []
        for k, n in enumerate(store, len(fetch)):
            copies.append(pltpu.make_async_copy(buffers[k], results[n], sems.at[k]))
            results[n] = buffers[k]
        kernel(me_ref, *inputs, *results, *rest)
        for copy in copies:
            copy.start()
        for copy in copies:
            copy.wait()

    own = [pltpu.VMEM(shape, kind) for shape, kind in held]
    own += [pltpu.SemaphoreType.DMA((len(held),))] if held else []
    size = sum(math.prod(shape) * jnp.dtype(kind).itemsize for shape, kind in held)
    far = pl.BlockSpec(memory_space=pltpu.HBM)
    results = pl.pallas_call(
        body,
        name=name,
        out_shape=[jax.ShapeDtypeStruct(shape, kind) for shape, kind in outs],
        in_specs=[SMEM] + [far if n in fetch else VMEM for n in range(count)],
        out_specs=[far if n in store else VMEM for n in range(len(outs))],
        scratch_shapes=own + list(scratch),
        compiler_params=pltpu.CompilerParams(vmem_limit_bytes=limit * 2**20 + size),
        cost_estimate=pl.CostEstimate(flops=0, bytes_accessed=0, transcendentals=0),
    )(me, *operands)
    return list(results)


def dot(left, right, dims=(((1,), (0,)), ((), ()))):
    return lax.dot_general(left, right, dims, preferred_element_type=f32)


def lanes(start, size):
    return pl.ds(pl.multiple_of(start, LANES), size)


def partner(values_in):
    half = HEAD_DIM // 2
    lane = lax.broadcasted_iota(jnp.int32, values_in.shape, 1)
    return jnp.where(
        lane % HEAD_DIM < half,
        pltpu.roll(values_in, values_in.shape[1] - half, 1),
        pltpu.roll(values_in, half, 1),
    )


def pick_first_kernel(me, w_qkv, w_out, out):
    width = w_out.shape[1]
    group = width // 4
    for part in range(3):
        out[:, part * group : (part + 1) * group] = w_qkv[
            :, lanes(part * width + me[2] * group, group)
        ]
    out[:, 3 * group :] = w_out[...]


def pick_rest_kernel(me, w_up, cot, *outs):
    part = w_up.shape[0]
    units = w_up.shape[1] // 4
    for r, out in enumerate(outs):
        out[:part, :] = w_up[:, lanes((me[0] ^ r) * units, units)]
        out[part:, :] = cot[...]


def stack_kernel(me, *refs):
    pieces, out = refs[:-1], refs[-1]
    part = out.shape[0] // 4
    for r, piece in enumerate(pieces):
        out[lanes((me[0] ^ r) * part, part), :] = piece[:part, :]


def weave_kernel(me, mine, theirs, *outs):
    core = me[1]
    rows = mine.shape[0] // 4
    for half, owner in ((mine, core), (theirs, 1 - core)):
        for chip in range(4):
            start = 0
            for out in outs:
                stop = start + out.shape[1]
                out[lanes((2 * chip + owner) * rows, rows), :] = half[
                    chip * rows : (chip + 1) * rows, start:stop
                ]
                start = stop


def qkv_kernel(me, *refs):
    own, a1, a2, a3, b1, b2 = refs[:6]
    scale, shift, weight, cosine, sine, q_out, k_out, v_out, normed, input_a, *again = refs[6:]
    ends = (me[2] == 0) | (me[2] == 3)
    rows, group = own.shape[0], q_out.shape[1]
    for s, (one, two) in enumerate(((own, None), (a1, None), (a2, b2), (a3, b1))):
        at = slice(s * rows, (s + 1) * rows)
        block = one[...].astype(f32)
        if two is not None:
            block = jnp.where(ends, block, two[...].astype(f32))
        centred, _ = normalize(block)
        normed[at, :] = centred.astype(bf16)
        low = (centred * (1.0 + scale[...]) + shift[...]).astype(bf16)
        input_a[at, :] = low
        for part, out in enumerate((q_out, k_out, v_out)):
            projected = dot(low, weight[:, part * group : (part + 1) * group])
            if part == 2:
                out[at, :] = projected.astype(bf16)
                continue
            for j in range(0, group, LANES):
                piece = projected[:, j : j + LANES]
                piece = piece * cosine[at, :] + partner(piece) * sine[at, :]
                if part == 0:
                    piece = piece * (1.0 / math.sqrt(HEAD_DIM))
                out[at, j : j + LANES] = piece.astype(bf16)
    for ref, kept in zip(again, (q_out, k_out, v_out, cosine, sine)):
        ref[...] = kept[...]


def attend_kernel(me, queries, keys, values, out, log_total):
    count, group = queries.shape
    step = 512
    lane = lax.broadcasted_iota(jnp.int32, (step, LANES), 1)

    def block(i, carry):
        at = pl.ds(pl.multiple_of(i * step, step), step)
        stats = jnp.zeros((step, LANES), f32)
        for j in range(group // LANES):
            cols = slice(j * LANES, (j + 1) * LANES)
            halves = []
            for side in range(2):
                query = jnp.where(
                    lane // HEAD_DIM == side, queries[at, cols], jnp.zeros((), bf16)
                )
                scores = dot(query, keys[:, cols], NT)
                top = jnp.max(scores, axis=1, keepdims=True)
                exponent = jnp.exp(scores - top)
                total = jnp.sum(exponent, axis=1, keepdims=True)
                halves.append(dot(exponent.astype(bf16), values[:, cols]) / total)
                stats = jnp.where(lane == 2 * j + side, top + jnp.log(total), stats)
            out[at, cols] = jnp.where(lane < HEAD_DIM, halves[0], halves[1]).astype(bf16)
        log_total[:, at] = jnp.transpose(stats)[:8]
        return carry

    lax.fori_loop(0, count // step, block, 0)


def attend_back_kernel(
    me, queries, keys, values, g0, g1, g2, g3, log_total, cosine, sine, out, key_sum, value_sum, query_t
):
    count, group = queries.shape
    step = 512
    rows = g0.shape[0]
    pieces = (g0, g1, g2, g3)
    keys_t = jnp.transpose(keys[...])
    lane = lax.broadcasted_iota(jnp.int32, (step, LANES), 1)
    for j in range(group // LANES):
        cols = slice(j * LANES, (j + 1) * LANES)
        for i in range(0, count, step):
            at = slice(i, i + step)
            grad = jnp.concatenate(
                [pieces[(i + n) // rows][:, cols] for n in range(0, step, rows)], axis=0
            )
            for side in range(2):
                head = 2 * j + side
                mine = slice(head * HEAD_DIM, (head + 1) * HEAD_DIM)
                keep = lane // HEAD_DIM == side
                query = jnp.where(keep, queries[at, cols], jnp.zeros((), bf16))
                grad_mine = jnp.where(keep, grad, jnp.zeros((), bf16))
                probs = jnp.exp(dot(keys[:, cols], query, NT) - log_total[head : head + 1, at])
                grad_probs = dot(values[:, cols], grad_mine, NT)
                delta = jnp.sum(probs * grad_probs, axis=0, keepdims=True)
                grad_scores = (probs * (grad_probs - delta)).astype(bf16)
                value_part = dot(probs.astype(bf16), grad_mine)
                key_part = dot(grad_scores, query)
                if i == 0 and side == 0:
                    value_sum[...] = value_part
                    key_sum[...] = key_part
                else:
                    value_sum[...] += value_part
                    key_sum[...] += key_part
                query_t[mine, at] = dot(keys_t[mine], grad_scores)
        turned = key_sum[...]
        turned = turned * cosine[...] - partner(turned) * sine[...]
        out[:, group + j * LANES : group + (j + 1) * LANES] = turned.astype(bf16)
        out[:, 2 * group + j * LANES : 2 * group + (j + 1) * LANES] = value_sum[...].astype(bf16)
        turned = jnp.transpose(query_t[cols, :]) * (1.0 / math.sqrt(HEAD_DIM))
        turned = turned * cosine[...] - partner(turned) * sine[...]
        out[:, cols] = turned.astype(bf16)


def middle_kernel(me, source, p0, p1, p2, p3, out_all, scale, shift, mixed, middle, input_b):
    place = me[2]
    group = p0.shape[1]
    for s, piece in enumerate((p0, p1, p2, p3)):
        mixed[:, lanes((place ^ s) * group, group)] = piece[...]
    value = source[...].astype(f32) + dot(mixed[...], out_all[...])
    middle[...] = value
    normed, _ = normalize(value)
    input_b[...] = (normed * (1.0 + scale[...]) + shift[...]).astype(bf16)


def ffn_kernel(
    me, inputs, packed, up, down_own, down_other, grad_in, out, hidden, grad_upper, grad_sum, out_sum
):
    core = me[1]
    units = down_own.shape[0]
    cot = packed[packed.shape[0] - inputs.shape[0] :, :]
    for n, (down, owner) in enumerate(((down_own, core), (down_other, 1 - core))):
        cols = lanes(owner * units, units)
        upper = dot(inputs[...], up[:, cols])
        bell = 0.5 + 0.5 * lax.erf(upper * math.sqrt(0.5))
        slope = bell + upper * jnp.exp(upper * upper * -0.5) * (1.0 / math.sqrt(2.0 * math.pi))
        grad = (dot(cot, down[...], NT) * slope).astype(bf16)
        grad_upper[:, cols] = grad
        value = (upper * bell).astype(bf16)
        hidden[:, n * units : (n + 1) * units] = value
        if n == 0:
            grad_sum[...] = dot(grad, up[:, cols], NT)
            out_sum[...] = dot(value, down[...])
        else:
            grad_in[...] = (grad_sum[...] + dot(grad, up[:, cols], NT)).astype(grad_in.dtype)
            out[...] = (out_sum[...] + dot(value, down[...])).astype(out.dtype)


def grad_down_kernel(me, *refs):
    hidden, cots, (give, keep) = refs[:4], refs[4:8], refs[8:]
    units = keep.shape[0]
    rows = hidden[0].shape[0]
    for out, start in ((give, units), (keep, 0)):
        total = None
        for left, packed in zip(hidden, cots):
            cot = packed[packed.shape[0] - rows :, :]
            term = dot(left[:, start : start + units], cot, TN)
            total = term if total is None else total + term
        out[...] = total.astype(out.dtype)


def grad_up_kernel(me, *refs):
    grads, tokens, (give, keep) = refs[:4], refs[4:8], refs[8:]
    core = me[1]
    part = keep.shape[0] // 4
    grad = jnp.concatenate([ref[...] for ref in grads], axis=0)
    for out, owner in ((give, 1 - core), (keep, core)):
        for chip in range(4):
            cols = lanes((2 * chip + owner) * part, part)
            left = jnp.concatenate([ref[:, cols] for ref in tokens], axis=0)
            out[chip * part : (chip + 1) * part, :] = dot(left, grad, TN).astype(out.dtype)


def pair_up_kernel(me, keep, take, proj_keep, proj_take, *outs):
    chip = me[0]
    part, width = keep.shape[0] // 4, keep.shape[1]
    for r, out in enumerate(outs):
        at = lanes((chip ^ r) * part, part)
        out[:, :width] = (keep[at, :] + take[at, :].astype(f32)).astype(out.dtype)
        out[:, width:] = (proj_keep[at, :] + proj_take[at, :].astype(f32)).astype(out.dtype)


def halve_kernel(me, keep, take, mine, send):
    low = lax.rem(me[2], 2)
    half = mine.shape[0]
    at = lanes(low * half, half)
    mine[...] = keep[at, :] + take[at, :].astype(f32)
    at = lanes((1 - low) * half, half)
    send[...] = (keep[at, :] + take[at, :].astype(f32)).astype(bf16)


def halve_across_kernel(me, mine, take, held, send):
    half = held.shape[0]
    high = lax.div(me[2], 2)
    at = pl.ds(pl.multiple_of(high * half, half), half)
    held[...] = mine[at, :] + take[at, :].astype(f32)
    at = pl.ds(pl.multiple_of((1 - high) * half, half), half)
    send[...] = (mine[at, :] + take[at, :].astype(f32)).astype(bf16)


def collect_kernel(me, p0, p1, p2, p3, out):
    chip = me[0]
    width = p0.shape[1] // 2
    total = None
    for r, piece in enumerate((p0, p1, p2, p3)):
        out[:, lanes((chip ^ r) * width, width)] = piece[:, :width].astype(out.dtype)
        term = piece[:, width:].astype(f32)
        total = term if total is None else total + term
    out[:, 4 * width :] = total.astype(out.dtype)


def back_b_kernel(
    me, g0, g1, g2, g3, middle, cot, scale, out_all,
    grad_middle, branch, sums, h0, h1, h2, h3,
):
    place = me[2]
    group = h0.shape[1]
    normed, inverse = normalize(middle[...])
    grad_in = g0[...]
    for more in (g1, g2, g3):
        grad_in = grad_in + more[...].astype(f32)
    sums[0:1, :] = jnp.sum(grad_in * normed, axis=0, keepdims=True)
    sums[1:2, :] = jnp.sum(grad_in, axis=0, keepdims=True)
    grad = cot[...].astype(f32) + norm_back(grad_in * (1.0 + scale[...]), normed, inverse)
    grad_middle[...] = grad
    low = grad.astype(bf16)
    branch[...] = low
    for s, piece in enumerate((h0, h1, h2, h3)):
        at = pl.ds(pl.multiple_of((place ^ s) * group, group), group)
        piece[...] = dot(low, out_all[at, :], NT).astype(bf16)


def back_a_kernel(me, grad_projected, weight, normed, own, across, pair, sums):
    rows = own.shape[0]
    first = second = None
    for s in (1, 3, 2, 0):
        at = slice(s * rows, (s + 1) * rows)
        grad = dot(grad_projected[at, :], weight[...], NT)
        if s % 2:
            pair[s // 2 * rows : (s // 2 + 1) * rows, :] = grad.astype(bf16)
        else:
            (across if s else own)[...] = grad
        one = jnp.sum(grad * normed[at, :].astype(f32), axis=0, keepdims=True)
        two = jnp.sum(grad, axis=0, keepdims=True)
        first, second = (one, two) if first is None else (first + one, second + two)
    sums[0:1, :] = first
    sums[1:2, :] = second


def grad_qkv_kernel(me, input_a, grad_projected, give, keep):
    core = me[1]
    part = keep.shape[0] // 4
    for out, owner in ((give, 1 - core), (keep, core)):
        for chip in range(4):
            cols = lanes((2 * chip + owner) * part, part)
            out[chip * part : (chip + 1) * part, :] = dot(
                input_a[:, cols], grad_projected[...], TN
            ).astype(out.dtype)


def pair_kernel(me, keep, take, *outs):
    chip = me[0]
    part = keep.shape[0] // 4
    for r, out in enumerate(outs):
        at = lanes((chip ^ r) * part, part)
        out[...] = (keep[at, :] + take[at, :].astype(f32)).astype(out.dtype)


def add_far_kernel(me, own, pair, out):
    rows = own.shape[0]
    out[...] = (own[...] + pair[rows:, :].astype(f32)).astype(bf16)


def tokens_kernel(me, own, pair, across, source, scale, grad_middle, out):
    rows = own.shape[0]
    grad_in = own[...] + pair[:rows, :].astype(f32) + across[...].astype(f32)
    normed, inverse = normalize(source[...].astype(f32))
    out[...] = grad_middle[...] + norm_back(grad_in * (1.0 + scale[...]), normed, inverse)


def finish_qkv_kernel(me, p0, p1, p2, p3, out):
    place = me[2]
    group = p0.shape[1] // 3
    width = out.shape[1] // 3
    for s, piece in enumerate((p0, p1, p2, p3)):
        for part in range(3):
            at = part * width + (place ^ s) * group
            out[:, lanes(at, group)] = piece[:, part * group : (part + 1) * group].astype(f32)


def swap_seq(values_in, bits):
    return lax.ppermute(values_in, "seq", [(i, i ^ bits) for i in range(4)])


def halve_pair(values_in, place):
    half = values_in.shape[0] // 2
    mine = lax.dynamic_slice_in_dim(values_in, place % 2 * half, half)
    other = lax.dynamic_slice_in_dim(values_in, (1 - place % 2) * half, half)
    return mine, other.astype(bf16)


class Halving:
    def __init__(self, held, send, place):
        self.held, self.send, self.low, self.high = held, send, place % 2, place // 2

    def across_ready(self, me):
        rows, cols = self.held.shape
        half = ((rows // 2, cols), f32), ((rows // 2, cols), bf16)
        self.held, self.send = call(
            halve_across_kernel, "halve", half, me, self.held, swap_seq(self.send, 1)
        )

    def across(self):
        self.got = swap_seq(self.send, 2)

    def across_done(self, *others):
        self.held = (self.held + tie(self.got, *others)[0].astype(f32)).astype(bf16)

    def join(self, bit, bits):
        other = swap_seq(self.held, bits)
        first = jnp.where(bit == 0, self.held, other)
        second = jnp.where(bit == 0, other, self.held)
        self.held = jnp.concatenate([first, second], axis=0)

    def back_across(self):
        self.join(self.high, 2)

    def back_pair(self):
        self.join(self.low, 1)


def outward(values_in):
    return lax.ppermute(values_in, "seq", [(1, 0), (2, 3)])


def middle_swap(values_in):
    return lax.ppermute(values_in, "seq", [(1, 2), (2, 1)])


def tie(*values_in):
    return lax.optimization_barrier(values_in)


def spread(values_in):
    return [values_in] + [hop(values_in, 2 * r) for r in range(1, 4)]


def deal(blocks):
    return [blocks[0]] + [hop(blocks[r].astype(bf16), 2 * r) for r in range(1, 4)]


def total_of(pieces):
    total = pieces[0]
    for piece in pieces[1:]:
        total = total + piece.astype(f32)
    return total


def per_device(tokens, noise_steps, w_qkv, w_out, w_up, w_down, w_time, cotangent):
    index, place = lax.axis_index("dp"), lax.axis_index("seq")
    me = jnp.stack([index // 2, index % 2, place]).astype(jnp.int32)
    _, rows, width = tokens.shape
    group = width // 4
    count = 4 * rows
    part = w_out.shape[0]
    units = w_down.shape[0]
    source, cot = tokens[0], cotangent[0]

    half = HEAD_DIM // 2
    lane = jnp.arange(LANES)
    frequency = jnp.exp(-math.log(10000.0) * (lane % half).astype(f32) / half)
    block_place = place ^ jnp.arange(4)
    positions = (block_place[:, None] * rows + jnp.arange(rows)).reshape(-1).astype(f32)
    angles = positions[:, None] * frequency
    cosine = jnp.cos(angles)
    sine = jnp.sin(angles) * jnp.where(lane % HEAD_DIM < half, -1.0, 1.0)

    a1, b1 = swap_seq(source, 1), middle_swap(source)
    size = 3 * group + width
    (first,) = call(
        pick_first_kernel,
        "pick_first",
        [((part, size), bf16)],
        me,
        w_qkv,
        w_out,
        fetch=(0, 1),
    )
    steps_all = lax.all_to_all(
        jnp.broadcast_to(noise_steps.astype(f32), (8,)),
        "dp",
        split_axis=0,
        concat_axis=0,
        tiled=True,
    )
    first, steps_all = tie(first, steps_all)
    first_mine = spread(first)
    a1, b1 = tie(a1, b1)

    a2, b2 = outward(b1), middle_swap(a1)
    packed = call(
        pick_rest_kernel,
        "pick_rest",
        [((part + rows, width), bf16)] * 4,
        me,
        w_up,
        cot,
        fetch=(0, 1),
        store=(0, 1, 2, 3),
    )
    embed_all = time_embedding(steps_all)
    cond_part = jnp.dot(embed_all, w_time.astype(f32), precision=highest)
    condition = lax.all_to_all(cond_part, "dp", split_axis=0, concat_axis=0, tiled=True).reshape(
        4, width
    )
    a2, b2, condition, cosine, sine, down_late, *more = tie(
        a2, b2, condition, cosine, sine, w_down, *first_mine, *packed
    )
    first_mine, packed = more[:4], more[4:]

    a3 = outward(b2)
    (first_half,) = call(
        stack_kernel, "stack_first", [((4 * part, size), bf16)], me, *first_mine, store=(0,)
    )
    first_half, *packed = tie(first_half, *packed)
    packed = deal(packed)
    qkv_all, out_all = call(
        weave_kernel,
        "weave_first",
        [((width, 3 * group), bf16), ((width, width), bf16)],
        me,
        first_half,
        hop(first_half, 1),
        fetch=(0, 1),
    )
    a3, qkv_all = tie(a3, qkv_all)
    scale_a, shift_a, scale_b, shift_b = [condition[i : i + 1] for i in range(4)]

    queries, keys, values, normed_a, input_a, *kept = call(
        qkv_kernel,
        "qkv",
        [((count, group), bf16)] * 3
        + [((count, width), bf16)] * 2
        + [((count, group), bf16)] * 3
        + [((count, LANES), f32)] * 2,
        me,
        source,
        a1,
        a2,
        a3,
        b1,
        b2,
        scale_a,
        shift_a,
        qkv_all,
        cosine,
        sine,
        store=(3, 4, 5, 6, 7, 8, 9),
    )
    attended, log_total = call(
        attend_kernel,
        "attend",
        [((count, group), bf16), ((8, count), f32)],
        me,
        queries,
        keys,
        values,
    )
    attended, packed[1] = tie(attended, packed[1])
    pieces = [attended[:rows]] + [
        swap_seq(attended[s * rows : (s + 1) * rows], s) for s in range(1, 4)
    ]
    *pieces, packed[2], packed[3] = tie(*pieces, packed[2], packed[3])
    (up_half,) = call(
        stack_kernel, "stack_up", [((4 * part, width), bf16)], me, *packed, fetch=(0, 1, 2, 3)
    )
    down_other = hop(down_late, 1)
    up_other = hop(up_half, 1)
    mixed, middle, input_b = call(
        middle_kernel,
        "middle",
        [((rows, width), bf16), ((rows, width), f32), ((rows, width), bf16)],
        me,
        source,
        *pieces,
        out_all,
        scale_b,
        shift_b,
    )

    toks = [input_b, hop(input_b, 2), None, hop(input_b, 6)]
    up_half, up_other, toks[0] = tie(up_half, up_other, toks[0])
    (up_all,) = call(
        weave_kernel, "weave_up", [((width, width), bf16)], me, up_half, up_other
    )
    grads, outs, hidden, grad_upper = [None] * 4, [None] * 4, [None] * 4, [None] * 4
    last = None
    for r in (0, 3, 1, 2):
        if r:
            toks[r], hidden[last] = tie(toks[r], hidden[last])
        if r == 3:
            late, toks[3] = tie(input_b, toks[3])
            toks[2] = hop(late, 4)
        if r == 2:
            toks[2], grads[3] = tie(toks[2], grads[3])
        grads[r], outs[r], hidden[r], grad_upper[r] = call(
            ffn_kernel,
            "ffn",
            [((rows, width), bf16 if r else f32)] * 2 + [((rows, 2 * units), bf16)] * 2,
            me,
            toks[r],
            packed[r],
            up_all,
            w_down,
            down_other,
            scratch=[pltpu.VMEM((rows, width), f32)] * 2,
        )
        if r:
            grads[r] = hop(grads[r], 2 * r)
        last = r

    hidden[0], grad_upper[0], grads[1], grads[3] = tie(
        hidden[0], grad_upper[0], grads[1], grads[3]
    )
    give, keep = call(
        grad_down_kernel,
        "grad_down",
        [((units, width), bf16), ((units, width), f32)],
        me,
        *hidden,
        *packed,
        fetch=tuple(range(8)),
    )
    down_give, down_keep = give, keep
    up_give, up_keep = call(
        grad_up_kernel,
        "grad_up",
        [((width // 2, width), bf16), ((width // 2, width), f32)],
        me,
        *grad_upper,
        *toks,
        store=(0, 1),
    )
    grads[2], down_give, up_give = tie(grads[2], down_give, up_give)
    down_take, up_take = hop(down_give, 1), hop(up_give, 1)
    grad_middle, branch, sums_b, *to_heads = call(
        back_b_kernel,
        "back_b",
        [((rows, width), f32), ((rows, width), bf16), ((2, width), f32)]
        + [((rows, group), bf16)] * 4,
        me,
        *grads,
        middle,
        cot,
        scale_b,
        out_all,
    )
    proj_give, proj_keep = call(
        grad_qkv_kernel,
        "grad_proj",
        [((width // 2, width), bf16), ((width // 2, width), f32)],
        me,
        mixed,
        branch,
        store=(0, 1),
    )
    proj_give, *to_heads = tie(proj_give, *to_heads)
    grad_heads = [to_heads[0]] + [swap_seq(to_heads[s], s) for s in range(1, 4)]
    down_mine, down_send = call(
        halve_kernel,
        "halve_down",
        [((units // 2, width), f32), ((units // 2, width), bf16)],
        me,
        down_keep,
        down_take,
    )
    up_parts = call(
        pair_up_kernel,
        "pair_up",
        [((part, 2 * width), f32)] + [((part, 2 * width), bf16)] * 3,
        me,
        up_keep,
        up_take,
        proj_keep,
        hop(proj_give, 1),
        fetch=(0, 1, 2, 3),
        store=(0, 1, 2, 3),
    )
    *grad_heads, down_mine, down_send, up_parts[0] = tie(
        *grad_heads, down_mine, down_send, up_parts[0]
    )

    up_parts = deal(up_parts)
    down_sum = Halving(down_mine, down_send, place)
    down_sum.across_ready(me)
    (grad_projected,) = call(
        attend_back_kernel,
        "attend_back",
        [((count, 3 * group), bf16)],
        me,
        *kept[:3],
        *grad_heads,
        log_total,
        *kept[3:],
        scratch=[pltpu.VMEM((count, LANES), f32)] * 2 + [pltpu.VMEM((group, count), f32)],
        fetch=(0, 1, 2, 8, 9),
    )
    grad_a, p2, pair, sums_a = call(
        back_a_kernel,
        "back_a",
        [((rows, width), f32)] * 2 + [((2 * rows, width), bf16), ((2, width), f32)],
        me,
        grad_projected,
        qkv_all,
        normed_a,
        fetch=(2,),
        store=(0, 1, 2),
    )
    pair = swap_seq(pair, 1)

    down_sum.held, down_sum.send, p2 = tie(down_sum.held, down_sum.send, p2)
    down_sum.across()
    (both,) = call(
        collect_kernel,
        "collect",
        [((part, 5 * width), f32)],
        me,
        *up_parts,
        fetch=(0, 1, 2, 3),
    )
    up_mine, up_send = halve_pair(both, place)
    up_sum = Halving(up_mine, up_send, place)
    give, keep = call(
        grad_qkv_kernel,
        "grad_qkv",
        [((width // 2, 3 * group), bf16), ((width // 2, 3 * group), f32)],
        me,
        input_a,
        grad_projected,
        fetch=(0,),
    )
    take, both = tie(hop(give, 1), both)
    qkv_parts = call(
        pair_kernel,
        "pair",
        [((part, 3 * group), f32)] + [((part, 3 * group), bf16)] * 3,
        me,
        keep,
        take,
    )
    sums_a, qkv_parts[1] = tie(sums_a, qkv_parts[1])
    qkv_parts = deal(qkv_parts)
    grad_condition = jnp.concatenate([sums_a, sums_b], axis=0)
    cond_cols = lax.all_to_all(
        grad_condition.reshape(8, -1), "dp", split_axis=0, concat_axis=0, tiled=True
    )
    qkv_cols = total_of(qkv_parts).astype(bf16)
    down_sum.across_done(qkv_cols, cond_cols)
    pair, up_sum.held, up_sum.send, down_sum.held, cond_cols, qkv_cols, *outs = tie(
        pair, up_sum.held, up_sum.send, down_sum.held, cond_cols, qkv_cols, *outs
    )

    (far,) = call(add_far_kernel, "add_far", [((rows, width), bf16)], me, p2, pair)
    far, up_sum.send = tie(far, up_sum.send)
    across = swap_seq(far, 2)
    up_sum.across_ready(me)
    outs = deal(outs)
    across, up_sum.held, up_sum.send, down_sum.held, qkv_cols, cond_cols, *outs = tie(
        across, up_sum.held, up_sum.send, down_sum.held, qkv_cols, cond_cols, *outs
    )

    up_sum.across()
    down_sum.back_across()
    qkv_pair = swap_seq(qkv_cols, 1)
    up_sum.across_done()
    cond_sum = cond_cols + swap_seq(cond_cols, 1)
    (grad_tokens,) = call(
        tokens_kernel,
        "tokens",
        [((rows, width), f32)],
        me,
        grad_a,
        pair,
        across,
        source,
        scale_a,
        grad_middle,
    )
    up_sum.held, down_sum.held, qkv_pair, cond_sum, *outs = tie(
        up_sum.held, down_sum.held, qkv_pair, cond_sum, *outs
    )

    up_sum.back_across()
    down_sum.back_pair()
    cond_sum = cond_sum + swap_seq(cond_sum, 2)
    result = (middle + total_of(outs)).astype(bf16)
    up_sum.held, qkv_pair = tie(up_sum.held, qkv_pair)

    qkv_far = swap_seq(jnp.stack([qkv_cols, qkv_pair]), 2)
    up_sum.back_pair()
    cond_sum, qkv_far = tie(cond_sum, qkv_far)
    grad_time = jnp.dot(embed_all.T, cond_sum, precision=highest)
    (grad_qkv,) = call(
        finish_qkv_kernel,
        "finish_qkv",
        [((part, 3 * width), f32)],
        me,
        qkv_cols,
        qkv_pair,
        qkv_far[0],
        qkv_far[1],
    )
    grad_down, both = down_sum.held, up_sum.held
    return (
        result[None],
        grad_tokens[None],
        grad_qkv,
        both[:, 4 * width :].astype(f32),
        both[:, : 4 * width].astype(f32),
        grad_down.astype(f32),
        grad_time,
    )


def solution(mesh):
    in_specs = (
        P("dp", "seq", None),
        P("dp"),
        P("dp", None),
        P("dp", None),
        P("dp", None),
        P("dp", None),
        P(None, "dp"),
        P("dp", "seq", None),
    )
    out_specs = (
        P("dp", "seq", None),
        P("dp", "seq", None),
        P("dp", None),
        P("dp", None),
        P("dp", None),
        P("dp", None),
        P(None, "dp"),
    )
    square = mesh.shape["dp"] == 8 and mesh.shape["seq"] == 4
    return jax.shard_map(
        per_device if square else per_device_any, mesh=mesh, in_specs=in_specs, out_specs=out_specs, check_vma=False
    )
```

```python
from functools import partial
import math

import jax
import jax.numpy as jnp
from jax import lax
from jax.experimental import pallas as pl
from jax.experimental.pallas import tpu as pltpu
from jax.sharding import PartitionSpec as P

HEAD_DIM = 64
TE = 256

highest = lax.Precision.HIGHEST
bf16 = jnp.bfloat16
f32 = jnp.float32


def normalize(values_in):
    centered = values_in - jnp.mean(values_in, axis=-1, keepdims=True)
    inverse = lax.rsqrt(jnp.mean(centered * centered, axis=-1, keepdims=True) + 1e-05)
    return (centered * inverse, inverse)


def norm_back(gradient, normed, inverse):
    return inverse * (
        gradient
        - jnp.mean(gradient, axis=-1, keepdims=True)
        - normed * jnp.mean(gradient * normed, axis=-1, keepdims=True)
    )


def time_embedding(noise_step):
    half_dim = TE // 2
    frequency = jnp.exp(-math.log(10000.0) * jnp.arange(half_dim, dtype=f32) / half_dim)
    angles = noise_step.astype(f32)[..., None] * frequency
    return jnp.concatenate([jnp.sin(angles), jnp.cos(angles)], axis=-1)


def rotate(values_in, positions, direction):
    half_dim = values_in.shape[-1] // 2
    frequency = jnp.exp(-math.log(10000.0) * jnp.arange(half_dim, dtype=f32) / half_dim)
    angles = positions[:, None, None] * frequency
    cosine = jnp.cos(angles)
    sine_wave = direction * jnp.sin(angles)
    first_half = values_in[..., :half_dim]
    second_half = values_in[..., half_dim:]
    return jnp.concatenate(
        [
            first_half * cosine - second_half * sine_wave,
            first_half * sine_wave + second_half * cosine,
        ],
        axis=-1,
    )


def hop(values_in, bit):
    count = lax.axis_size("dp")
    return lax.ppermute(values_in, "dp", [(i, i ^ bit) for i in range(count)])


def core_groups():
    count = lax.axis_size("dp")
    return [[i for i in range(count) if i % 2 == core] for core in range(2)]


def gather_chips(block):
    chips = lax.axis_size("dp") // 2
    if chips != 4:
        return lax.all_gather(block, "dp", axis=0, tiled=True, axis_index_groups=core_groups())
    rows = block.shape[0]
    half = rows // 2
    chip = lax.axis_index("dp") // 2
    from_x = hop(block, 2)
    from_y = hop(block, 4)
    far_top = hop(from_y[:half], 2)
    far_low = hop(from_x[half:], 4)
    out = jnp.zeros((chips * rows,) + block.shape[1:], block.dtype)
    for piece, other, shift in (
        (block, 0, 0),
        (from_x, 1, 0),
        (from_y, 2, 0),
        (far_top, 3, 0),
        (far_low, 3, half),
    ):
        out = lax.dynamic_update_slice_in_dim(out, piece, (chip ^ other) * rows + shift, axis=0)
    return out


def scatter_chips(parts):
    chips = lax.axis_size("dp") // 2
    if chips != 4:
        flat = parts.reshape((-1,) + parts.shape[2:])
        return lax.psum_scatter(
            flat, "dp", scatter_dimension=0, tiled=True, axis_index_groups=core_groups()
        ).astype(f32)
    half = parts.shape[1] // 2
    chip = lax.axis_index("dp") // 2
    own, to_x, to_y, to_far = [
        lax.dynamic_index_in_dim(parts, chip ^ other, 0, keepdims=False) for other in range(4)
    ]
    on_x = hop(to_far[:half], 2)
    on_y = hop(to_far[half:], 4)
    to_y = jnp.concatenate([to_y[:half] + on_x, to_y[half:]], axis=0)
    to_x = jnp.concatenate([to_x[:half], to_x[half:] + on_y], axis=0)
    return own.astype(f32) + hop(to_x, 2).astype(f32) + hop(to_y, 4).astype(f32)


def both_cores(half_block):
    chips = lax.axis_size("dp") // 2
    core = lax.axis_index("dp") % 2
    other = hop(half_block, 1)
    shape = (chips, half_block.shape[0] // chips) + half_block.shape[1:]
    mine, theirs = half_block.reshape(shape), other.reshape(shape)
    first = jnp.where(core == 0, mine, theirs)
    second = jnp.where(core == 0, theirs, mine)
    joined = jnp.stack([first, second], axis=1)
    return joined.reshape((-1,) + half_block.shape[1:])


def sum_cores(full):
    count = lax.axis_size("dp")
    core = lax.axis_index("dp") % 2
    view = full.reshape((count // 2, 2, full.shape[0] // count) + full.shape[1:])
    mine = lax.dynamic_index_in_dim(view, core, 1, keepdims=False)
    theirs = lax.dynamic_index_in_dim(view, 1 - core, 1, keepdims=False)
    return (mine.astype(f32) + hop(theirs.astype(bf16), 1).astype(f32)).astype(bf16)


def turn(values_in, step):
    count = lax.axis_size("seq")
    return lax.ppermute(values_in, "seq", [(i, (i + step) % count) for i in range(count)])


def shift(values_in, step):
    count = lax.axis_size("seq")
    return lax.ppermute(
        values_in, "seq", [(i, i + step) for i in range(count) if 0 <= i + step < count]
    )


def gather_seq(block):
    count = lax.axis_size("seq")
    place = lax.axis_index("seq")
    lower, upper = [block], [block]
    for _ in range(count - 1):
        lower.append(shift(lower[-1], 1))
        upper.append(shift(upper[-1], -1))
    return [block] + [
        jnp.where(place + step < count, upper[step], lower[count - step])
        for step in range(1, count)
    ]


def scatter_seq(blocks):
    count = len(blocks)
    right = left = None
    for step in range(1, count):
        going_right = blocks[count - step]
        going_left = blocks[step]
        if right is not None:
            going_right = going_right + right.astype(f32)
            going_left = going_left + left.astype(f32)
        right = shift(going_right.astype(bf16), 1)
        left = shift(going_left.astype(bf16), -1)
    return blocks[0] + right.astype(f32) + left.astype(f32)


def sum_seq(values_in):
    count = lax.axis_size("seq")
    if count != 4:
        return lax.psum(values_in.astype(bf16), "seq").astype(f32)
    place = lax.axis_index("seq")
    inner = lax.ppermute(values_in.astype(bf16), "seq", [(0, 1), (3, 2)])
    pair = values_in + inner.astype(f32)
    across = lax.ppermute(pair.astype(bf16), "seq", [(1, 2), (2, 1)])
    total = pair + across.astype(f32)
    outer = lax.ppermute(total.astype(bf16), "seq", [(1, 0), (2, 3)])
    return jnp.where((place == 0) | (place == 3), outer.astype(f32), total)


def attend_forward(queries, key_rows, values):
    scores = jnp.einsum("qhd,khd->hqk", queries, key_rows, preferred_element_type=f32) / math.sqrt(
        HEAD_DIM
    )
    row_top = jnp.max(scores, axis=-1, keepdims=True)
    exponent = jnp.exp(scores - row_top)
    row_total = jnp.sum(exponent, axis=-1, keepdims=True)
    probs = (exponent / row_total).astype(bf16)
    attended = jnp.einsum("hqk,khd->qhd", probs, values, preferred_element_type=f32)
    return attended.astype(bf16), (row_top + jnp.log(row_total))


def attend_backward(queries, key_rows, values, log_total, grad_attn):
    score_scale = 1.0 / math.sqrt(HEAD_DIM)
    scores = (
        jnp.einsum("qhd,khd->hqk", queries, key_rows, preferred_element_type=f32) * score_scale
    )
    probs = jnp.exp(scores - log_total)
    grad_probs = jnp.einsum("qhd,khd->hqk", grad_attn, values, preferred_element_type=f32)
    grad_scores = (
        probs * (grad_probs - jnp.sum(probs * grad_probs, axis=-1, keepdims=True))
    ).astype(bf16)
    grad_queries = (
        jnp.einsum("hqk,khd->qhd", grad_scores, key_rows, preferred_element_type=f32) * score_scale
    )
    grad_keys = (
        jnp.einsum("hqk,qhd->khd", grad_scores, queries, preferred_element_type=f32) * score_scale
    )
    grad_values = jnp.einsum(
        "hqk,qhd->khd", probs.astype(bf16), grad_attn, preferred_element_type=f32
    )
    return grad_queries.astype(bf16), grad_keys.astype(bf16), grad_values.astype(bf16)


def per_device_any(tokens, noise_steps, w_qkv, w_out, w_up, w_down, w_time, cotangent):
    dp_count, seq_parts = lax.axis_size("dp"), lax.axis_size("seq")
    chips = dp_count // 2
    core = lax.axis_index("dp") % 2
    place = lax.axis_index("seq")
    _, rows, width = tokens.shape
    group = width // seq_parts
    source = tokens[0]
    cot = cotangent[0]

    token_blocks = gather_seq(source)

    steps_all = lax.all_to_all(
        jnp.broadcast_to(noise_steps.astype(f32), (dp_count,)),
        "dp",
        split_axis=0,
        concat_axis=0,
        tiled=True,
    )
    embed_all = time_embedding(steps_all)
    cond_part = jnp.dot(embed_all, w_time.astype(f32), precision=highest)
    condition = lax.all_to_all(cond_part, "dp", split_axis=0, concat_axis=0, tiled=True).reshape(
        4, width
    )
    scale_a, shift_a, scale_b, shift_b = [condition[i][None, :] for i in range(4)]

    qkv_cols = lax.dynamic_index_in_dim(
        w_qkv.reshape(-1, 3, seq_parts, group), place, 2, keepdims=False
    ).reshape(-1, 3 * group)
    qkv_all = both_cores(gather_chips(qkv_cols))
    unit_view = w_up.reshape(w_up.shape[0], chips, 2, -1)
    up_mine = lax.dynamic_index_in_dim(unit_view, core, 2, keepdims=False).reshape(
        w_up.shape[0], -1
    )
    up_theirs = lax.dynamic_index_in_dim(unit_view, 1 - core, 2, keepdims=False).reshape(
        w_up.shape[0], -1
    )
    up_other = hop(up_theirs, 1)
    up_block = jnp.where(
        core == 0,
        jnp.concatenate([up_mine, up_other], axis=0),
        jnp.concatenate([up_other, up_mine], axis=0),
    )
    up_all = gather_chips(up_block)
    out_all = both_cores(gather_chips(w_out))
    down_all = gather_chips(w_down)
    cot_both = jnp.concatenate([cot, hop(cot, 1)], axis=0)

    full = jnp.concatenate(token_blocks, axis=0).astype(f32)
    normed_a, inverse_a = normalize(full)
    input_a = (normed_a * (1.0 + scale_a) + shift_a).astype(bf16)
    projected = jnp.dot(input_a, qkv_all, preferred_element_type=f32)
    block_place = (place + jnp.arange(seq_parts)) % seq_parts
    positions = (block_place[:, None] * rows + jnp.arange(rows)).reshape(-1).astype(f32)
    head_view = projected.reshape(seq_parts * rows, 3, -1, HEAD_DIM)
    queries = rotate(head_view[:, 0], positions, 1.0).astype(bf16)
    key_rows = rotate(head_view[:, 1], positions, 1.0).astype(bf16)
    values = head_view[:, 2].astype(bf16)
    attended, log_total = attend_forward(queries, key_rows, values)
    attended = attended.reshape(seq_parts, rows, group)
    pieces = [attended[0]] + [turn(attended[s], s) for s in range(1, seq_parts)]
    stacked = jnp.stack(pieces)
    mixed = jnp.concatenate(
        [
            lax.dynamic_index_in_dim(stacked, (place - g) % seq_parts, 0, keepdims=False)
            for g in range(seq_parts)
        ],
        axis=-1,
    )
    middle = source.astype(f32) + jnp.dot(mixed, out_all, preferred_element_type=f32)
    normed_b, inverse_b = normalize(middle)
    input_b = (normed_b * (1.0 + scale_b) + shift_b).astype(bf16)

    input_both = jnp.concatenate([input_b, hop(input_b, 1)], axis=0)
    upper = jnp.dot(input_both, up_all, preferred_element_type=f32)
    grad_hidden = lax.dot_general(
        cot_both, down_all, (((1,), (1,)), ((), ())), preferred_element_type=f32
    )
    hidden, gelu_pull = jax.vjp(partial(jax.nn.gelu, approximate=False), upper)
    hidden = hidden.astype(bf16)
    grad_upper = gelu_pull(grad_hidden)[0].astype(bf16)
    grad_in_part = lax.dot_general(
        grad_upper, up_all, (((1,), (1,)), ((), ())), preferred_element_type=f32
    )
    grad_in_b = grad_in_part[:rows] + hop(grad_in_part[rows:].astype(bf16), 1).astype(f32)
    out_part = jnp.dot(hidden, down_all, preferred_element_type=f32)
    result = (
        middle + out_part[:rows] + hop(out_part[rows:].astype(bf16), 1).astype(f32)
    ).astype(bf16)

    grad_down_part = lax.dot_general(
        hidden, cot_both, (((0,), (0,)), ((), ())), preferred_element_type=f32
    ).astype(bf16)
    grad_up_part = lax.dot_general(
        input_both, grad_upper, (((0,), (0,)), ((), ())), preferred_element_type=f32
    ).astype(bf16)

    grad_scale_b = jnp.sum(grad_in_b * normed_b, axis=0)
    grad_shift_b = jnp.sum(grad_in_b, axis=0)
    grad_middle = cot.astype(f32) + norm_back(grad_in_b * (1.0 + scale_b), normed_b, inverse_b)
    grad_branch = grad_middle.astype(bf16)
    grad_mixed = lax.dot_general(
        grad_branch, out_all, (((1,), (1,)), ((), ())), preferred_element_type=f32
    ).astype(bf16)
    to_heads = grad_mixed.reshape(rows, seq_parts, group)
    grad_pieces = [
        lax.dynamic_index_in_dim(to_heads, (place - s) % seq_parts, 1, keepdims=False)
        for s in range(seq_parts)
    ]
    grad_attn = jnp.concatenate(
        [grad_pieces[0]] + [turn(grad_pieces[s], -s) for s in range(1, seq_parts)], axis=0
    )
    grad_proj_part = lax.dot_general(
        mixed, grad_branch, (((0,), (0,)), ((), ())), preferred_element_type=f32
    )
    grad_q, grad_k, grad_v = attend_backward(
        queries,
        key_rows,
        values,
        log_total,
        grad_attn.reshape(seq_parts * rows, -1, HEAD_DIM),
    )
    grad_q = rotate(grad_q.astype(f32), positions, -1.0).astype(bf16)
    grad_k = rotate(grad_k.astype(f32), positions, -1.0).astype(bf16)
    grad_projected = jnp.stack([grad_q, grad_k, grad_v], axis=1).reshape(seq_parts * rows, -1)
    grad_in_a_part = lax.dot_general(
        grad_projected, qkv_all, (((1,), (1,)), ((), ())), preferred_element_type=f32
    )
    grad_qkv_part = lax.dot_general(
        input_a, grad_projected, (((0,), (0,)), ((), ())), preferred_element_type=f32
    )
    grad_in_a = scatter_seq(
        [grad_in_a_part[s * rows : (s + 1) * rows] for s in range(seq_parts)]
    )
    grad_scale_a = jnp.sum(grad_in_a_part * normed_a, axis=0)
    grad_shift_a = jnp.sum(grad_in_a_part, axis=0)
    grad_tokens = grad_middle + norm_back(
        grad_in_a * (1.0 + scale_a), normed_a[:rows], inverse_a[:rows]
    )

    grad_down = sum_seq(scatter_chips(grad_down_part.reshape(chips, -1, width)))
    grad_up_rows = scatter_chips(grad_up_part.reshape(chips, -1, grad_up_part.shape[1]))
    up_halves = grad_up_rows.reshape(2, -1, grad_up_rows.shape[1])
    keep = lax.dynamic_index_in_dim(up_halves, core, 0, keepdims=False)
    give = lax.dynamic_index_in_dim(up_halves, 1 - core, 0, keepdims=False)
    keep = keep.reshape(keep.shape[0], chips, -1)
    take = hop(give.astype(bf16), 1).astype(f32).reshape(keep.shape)
    grad_up = sum_seq(
        jnp.stack([jnp.where(core == 0, keep, take), jnp.where(core == 0, take, keep)], axis=2)
        .reshape(keep.shape[0], -1)
    )
    grad_proj = sum_seq(scatter_chips(sum_cores(grad_proj_part)))
    grad_qkv_cols = scatter_chips(sum_cores(grad_qkv_part)).astype(bf16)
    qkv_ring = jnp.stack(gather_seq(grad_qkv_cols))
    grad_qkv = jnp.stack(
        [
            lax.dynamic_index_in_dim(qkv_ring, (g - place) % seq_parts, 0, keepdims=False).reshape(
                -1, 3, group
            )
            for g in range(seq_parts)
        ],
        axis=2,
    )
    grad_qkv = grad_qkv.reshape(-1, 3 * width).astype(f32)
    grad_condition = jnp.concatenate([grad_scale_a, grad_shift_a, grad_scale_b, grad_shift_b])
    cond_cols = lax.all_to_all(
        grad_condition.reshape(dp_count, -1), "dp", split_axis=0, concat_axis=0, tiled=True
    )
    cond_sum = cond_cols
    for s in range(1, seq_parts):
        cond_sum = cond_sum + turn(cond_cols, s)
    grad_time = jnp.dot(embed_all.T, cond_sum, precision=highest)
    return (result[None], grad_tokens[None], grad_qkv, grad_proj, grad_up, grad_down, grad_time)


NT = (((1,), (1,)), ((), ()))
TN = (((0,), (0,)), ((), ()))
VMEM = pl.BlockSpec(memory_space=pltpu.VMEM)
SMEM = pl.BlockSpec(memory_space=pltpu.SMEM)
LANES = 128


def call(kernel, name, outs, me, *operands, scratch=(), fetch=(), store=(), limit=24):
    count, total = len(operands), len(operands) + len(outs)
    held = [(operands[n].shape, operands[n].dtype) for n in fetch] + [outs[n] for n in store]

    def body(me_ref, *refs):
        inputs, results, rest = list(refs[:count]), list(refs[count:total]), refs[total:]
        buffers, rest = rest[: len(held)], rest[len(held) :]
        sems, rest = (rest[0], rest[1:]) if held else (None, rest)
        copies = []
        for k, n in enumerate(fetch):
            copies.append(pltpu.make_async_copy(inputs[n], buffers[k], sems.at[k]))
            inputs[n] = buffers[k]
        for copy in copies:
            copy.start()
        for copy in copies:
            copy.wait()
        copies = []
        for k, n in enumerate(store, len(fetch)):
            copies.append(pltpu.make_async_copy(buffers[k], results[n], sems.at[k]))
            results[n] = buffers[k]
        kernel(me_ref, *inputs, *results, *rest)
        for copy in copies:
            copy.start()
        for copy in copies:
            copy.wait()

    own = [pltpu.VMEM(shape, kind) for shape, kind in held]
    own += [pltpu.SemaphoreType.DMA((len(held),))] if held else []
    size = sum(math.prod(shape) * jnp.dtype(kind).itemsize for shape, kind in held)
    far = pl.BlockSpec(memory_space=pltpu.HBM)
    results = pl.pallas_call(
        body,
        name=name,
        out_shape=[jax.ShapeDtypeStruct(shape, kind) for shape, kind in outs],
        in_specs=[SMEM] + [far if n in fetch else VMEM for n in range(count)],
        out_specs=[far if n in store else VMEM for n in range(len(outs))],
        scratch_shapes=own + list(scratch),
        compiler_params=pltpu.CompilerParams(vmem_limit_bytes=limit * 2**20 + size),
        cost_estimate=pl.CostEstimate(flops=0, bytes_accessed=0, transcendentals=0),
    )(me, *operands)
    return list(results)


def dot(left, right, dims=(((1,), (0,)), ((), ()))):
    return lax.dot_general(left, right, dims, preferred_element_type=f32)


def lanes(start, size):
    return pl.ds(pl.multiple_of(start, LANES), size)


def partner(values_in):
    half = HEAD_DIM // 2
    lane = lax.broadcasted_iota(jnp.int32, values_in.shape, 1)
    return jnp.where(
        lane % HEAD_DIM < half,
        pltpu.roll(values_in, values_in.shape[1] - half, 1),
        pltpu.roll(values_in, half, 1),
    )


def pick_first_kernel(me, w_qkv, w_out, out):
    width = w_out.shape[1]
    group = width // 4
    for part in range(3):
        out[:, part * group : (part + 1) * group] = w_qkv[
            :, lanes(part * width + me[2] * group, group)
        ]
    out[:, 3 * group :] = w_out[...]


def pick_rest_kernel(me, w_up, cot, *outs):
    part = w_up.shape[0]
    units = w_up.shape[1] // 4
    for r, out in enumerate(outs):
        out[:part, :] = w_up[:, lanes((me[0] ^ r) * units, units)]
        out[part:, :] = cot[...]


def stack_kernel(me, *refs):
    pieces, out = refs[:-1], refs[-1]
    part = out.shape[0] // 4
    for r, piece in enumerate(pieces):
        out[lanes((me[0] ^ r) * part, part), :] = piece[:part, :]


def weave_kernel(me, mine, theirs, *outs):
    core = me[1]
    rows = mine.shape[0] // 4
    for half, owner in ((mine, core), (theirs, 1 - core)):
        for chip in range(4):
            start = 0
            for out in outs:
                stop = start + out.shape[1]
                out[lanes((2 * chip + owner) * rows, rows), :] = half[
                    chip * rows : (chip + 1) * rows, start:stop
                ]
                start = stop


def qkv_kernel(me, *refs):
    own, a1, a2, a3, b1, b2 = refs[:6]
    scale, shift, weight, cosine, sine, q_out, k_out, v_out, normed, input_a = refs[6:]
    ends = (me[2] == 0) | (me[2] == 3)
    rows, group = own.shape[0], q_out.shape[1]
    for s, (one, two) in enumerate(((own, None), (a1, None), (a2, b2), (a3, b1))):
        at = slice(s * rows, (s + 1) * rows)
        block = one[...].astype(f32)
        if two is not None:
            block = jnp.where(ends, block, two[...].astype(f32))
        centred, _ = normalize(block)
        normed[at, :] = centred.astype(bf16)
        low = (centred * (1.0 + scale[...]) + shift[...]).astype(bf16)
        input_a[at, :] = low
        for part, out in enumerate((q_out, k_out, v_out)):
            projected = dot(low, weight[:, part * group : (part + 1) * group])
            if part == 2:
                out[at, :] = projected.astype(bf16)
                continue
            for j in range(0, group, LANES):
                piece = projected[:, j : j + LANES]
                piece = piece * cosine[at, :] + partner(piece) * sine[at, :]
                if part == 0:
                    piece = piece * (1.0 / math.sqrt(HEAD_DIM))
                out[at, j : j + LANES] = piece.astype(bf16)


def attend_kernel(me, queries, keys, values, out, log_total):
    count, group = queries.shape
    step = 512
    lane = lax.broadcasted_iota(jnp.int32, (step, LANES), 1)

    def block(i, carry):
        at = pl.ds(pl.multiple_of(i * step, step), step)
        stats = jnp.zeros((step, LANES), f32)
        for j in range(group // LANES):
            cols = slice(j * LANES, (j + 1) * LANES)
            halves = []
            for side in range(2):
                query = jnp.where(
                    lane // HEAD_DIM == side, queries[at, cols], jnp.zeros((), bf16)
                )
                scores = dot(query, keys[:, cols], NT)
                top = jnp.max(scores, axis=1, keepdims=True)
                exponent = jnp.exp(scores - top)
                total = jnp.sum(exponent, axis=1, keepdims=True)
                halves.append(dot(exponent.astype(bf16), values[:, cols]) / total)
                stats = jnp.where(lane == 2 * j + side, top + jnp.log(total), stats)
            out[at, cols] = jnp.where(lane < HEAD_DIM, halves[0], halves[1]).astype(bf16)
        log_total[:, at] = jnp.transpose(stats)[:8]
        return carry

    lax.fori_loop(0, count // step, block, 0)


def attend_back_kernel(
    me, queries, keys, values, g0, g1, g2, g3, log_total, cosine, sine, out, key_sum, value_sum, query_t
):
    count, group = queries.shape
    step = 512
    rows = g0.shape[0]
    pieces = (g0, g1, g2, g3)
    keys_t = jnp.transpose(keys[...])
    lane = lax.broadcasted_iota(jnp.int32, (step, LANES), 1)
    for j in range(group // LANES):
        cols = slice(j * LANES, (j + 1) * LANES)
        for i in range(0, count, step):
            at = slice(i, i + step)
            grad = jnp.concatenate(
                [pieces[(i + n) // rows][:, cols] for n in range(0, step, rows)], axis=0
            )
            for side in range(2):
                head = 2 * j + side
                mine = slice(head * HEAD_DIM, (head + 1) * HEAD_DIM)
                keep = lane // HEAD_DIM == side
                query = jnp.where(keep, queries[at, cols], jnp.zeros((), bf16))
                grad_mine = jnp.where(keep, grad, jnp.zeros((), bf16))
                probs = jnp.exp(dot(keys[:, cols], query, NT) - log_total[head : head + 1, at])
                grad_probs = dot(values[:, cols], grad_mine, NT)
                delta = jnp.sum(probs * grad_probs, axis=0, keepdims=True)
                grad_scores = (probs * (grad_probs - delta)).astype(bf16)
                value_part = dot(probs.astype(bf16), grad_mine)
                key_part = dot(grad_scores, query)
                if i == 0 and side == 0:
                    value_sum[...] = value_part
                    key_sum[...] = key_part
                else:
                    value_sum[...] += value_part
                    key_sum[...] += key_part
                query_t[mine, at] = dot(keys_t[mine], grad_scores)
        turned = key_sum[...]
        turned = turned * cosine[...] - partner(turned) * sine[...]
        out[:, group + j * LANES : group + (j + 1) * LANES] = turned.astype(bf16)
        out[:, 2 * group + j * LANES : 2 * group + (j + 1) * LANES] = value_sum[...].astype(bf16)
        turned = jnp.transpose(query_t[cols, :]) * (1.0 / math.sqrt(HEAD_DIM))
        turned = turned * cosine[...] - partner(turned) * sine[...]
        out[:, cols] = turned.astype(bf16)


def middle_kernel(me, source, p0, p1, p2, p3, out_all, scale, shift, mixed, middle, input_b):
    place = me[2]
    group = p0.shape[1]
    for s, piece in enumerate((p0, p1, p2, p3)):
        mixed[:, lanes((place ^ s) * group, group)] = piece[...]
    value = source[...].astype(f32) + dot(mixed[...], out_all[...])
    middle[...] = value
    normed, _ = normalize(value)
    input_b[...] = (normed * (1.0 + scale[...]) + shift[...]).astype(bf16)


def ffn_kernel(
    me, inputs, packed, up, down_own, down_other, grad_in, out, hidden, grad_upper, grad_sum, out_sum
):
    core = me[1]
    units = down_own.shape[0]
    cot = packed[packed.shape[0] - inputs.shape[0] :, :]
    for n, (down, owner) in enumerate(((down_own, core), (down_other, 1 - core))):
        cols = lanes(owner * units, units)
        upper = dot(inputs[...], up[:, cols])
        bell = 0.5 + 0.5 * lax.erf(upper * math.sqrt(0.5))
        slope = bell + upper * jnp.exp(upper * upper * -0.5) * (1.0 / math.sqrt(2.0 * math.pi))
        grad = (dot(cot, down[...], NT) * slope).astype(bf16)
        grad_upper[:, cols] = grad
        value = (upper * bell).astype(bf16)
        hidden[:, n * units : (n + 1) * units] = value
        if n == 0:
            grad_sum[...] = dot(grad, up[:, cols], NT)
            out_sum[...] = dot(value, down[...])
        else:
            grad_in[...] = (grad_sum[...] + dot(grad, up[:, cols], NT)).astype(grad_in.dtype)
            out[...] = (out_sum[...] + dot(value, down[...])).astype(out.dtype)


def grad_down_kernel(me, *refs):
    hidden, cots, (give, keep) = refs[:4], refs[4:8], refs[8:]
    units = keep.shape[0]
    rows = hidden[0].shape[0]
    for out, start in ((give, units), (keep, 0)):
        total = None
        for left, packed in zip(hidden, cots):
            cot = packed[packed.shape[0] - rows :, :]
            term = dot(left[:, start : start + units], cot, TN)
            total = term if total is None else total + term
        out[...] = total.astype(out.dtype)


def grad_up_kernel(me, *refs):
    grads, tokens, (give, keep) = refs[:4], refs[4:8], refs[8:]
    core = me[1]
    part = keep.shape[0] // 4
    grad = jnp.concatenate([ref[...] for ref in grads], axis=0)
    for out, owner in ((give, 1 - core), (keep, core)):
        for chip in range(4):
            cols = lanes((2 * chip + owner) * part, part)
            left = jnp.concatenate([ref[:, cols] for ref in tokens], axis=0)
            out[chip * part : (chip + 1) * part, :] = dot(left, grad, TN).astype(out.dtype)


def pair_up_kernel(me, keep, take, proj_keep, proj_take, *outs):
    chip = me[0]
    part, width = keep.shape[0] // 4, keep.shape[1]
    for r, out in enumerate(outs):
        at = lanes((chip ^ r) * part, part)
        out[:, :width] = (keep[at, :] + take[at, :].astype(f32)).astype(out.dtype)
        out[:, width:] = (proj_keep[at, :] + proj_take[at, :].astype(f32)).astype(out.dtype)


def halve_kernel(me, keep, take, mine, send):
    low = lax.rem(me[2], 2)
    half = mine.shape[0]
    at = lanes(low * half, half)
    mine[...] = keep[at, :] + take[at, :].astype(f32)
    at = lanes((1 - low) * half, half)
    send[...] = (keep[at, :] + take[at, :].astype(f32)).astype(bf16)


def halve_across_kernel(me, mine, take, held, send):
    half = held.shape[0]
    high = lax.div(me[2], 2)
    at = pl.ds(pl.multiple_of(high * half, half), half)
    held[...] = mine[at, :] + take[at, :].astype(f32)
    at = pl.ds(pl.multiple_of((1 - high) * half, half), half)
    send[...] = (mine[at, :] + take[at, :].astype(f32)).astype(bf16)


def collect_kernel(me, p0, p1, p2, p3, out):
    chip = me[0]
    width = p0.shape[1] // 2
    total = None
    for r, piece in enumerate((p0, p1, p2, p3)):
        out[:, lanes((chip ^ r) * width, width)] = piece[:, :width].astype(out.dtype)
        term = piece[:, width:].astype(f32)
        total = term if total is None else total + term
    out[:, 4 * width :] = total.astype(out.dtype)


def back_b_kernel(
    me, g0, g1, g2, g3, middle, cot, scale, out_all,
    grad_middle, branch, sums, h0, h1, h2, h3,
):
    place = me[2]
    group = h0.shape[1]
    normed, inverse = normalize(middle[...])
    grad_in = g0[...]
    for more in (g1, g2, g3):
        grad_in = grad_in + more[...].astype(f32)
    sums[0:1, :] = jnp.sum(grad_in * normed, axis=0, keepdims=True)
    sums[1:2, :] = jnp.sum(grad_in, axis=0, keepdims=True)
    grad = cot[...].astype(f32) + norm_back(grad_in * (1.0 + scale[...]), normed, inverse)
    grad_middle[...] = grad
    low = grad.astype(bf16)
    branch[...] = low
    for s, piece in enumerate((h0, h1, h2, h3)):
        at = pl.ds(pl.multiple_of((place ^ s) * group, group), group)
        piece[...] = dot(low, out_all[at, :], NT).astype(bf16)


def back_a_kernel(me, grad_projected, weight, normed, own, across, pair, sums):
    rows = own.shape[0]
    first = second = None
    for s in (1, 3, 2, 0):
        at = slice(s * rows, (s + 1) * rows)
        grad = dot(grad_projected[at, :], weight[...], NT)
        if s % 2:
            pair[s // 2 * rows : (s // 2 + 1) * rows, :] = grad.astype(bf16)
        else:
            (across if s else own)[...] = grad
        one = jnp.sum(grad * normed[at, :].astype(f32), axis=0, keepdims=True)
        two = jnp.sum(grad, axis=0, keepdims=True)
        first, second = (one, two) if first is None else (first + one, second + two)
    sums[0:1, :] = first
    sums[1:2, :] = second


def grad_qkv_kernel(me, input_a, grad_projected, give, keep):
    core = me[1]
    part = keep.shape[0] // 4
    for out, owner in ((give, 1 - core), (keep, core)):
        for chip in range(4):
            cols = lanes((2 * chip + owner) * part, part)
            out[chip * part : (chip + 1) * part, :] = dot(
                input_a[:, cols], grad_projected[...], TN
            ).astype(out.dtype)


def pair_kernel(me, keep, take, *outs):
    chip = me[0]
    part = keep.shape[0] // 4
    for r, out in enumerate(outs):
        at = lanes((chip ^ r) * part, part)
        out[...] = (keep[at, :] + take[at, :].astype(f32)).astype(out.dtype)


def add_far_kernel(me, own, pair, out):
    rows = own.shape[0]
    out[...] = (own[...] + pair[rows:, :].astype(f32)).astype(bf16)


def tokens_kernel(me, own, pair, across, source, scale, grad_middle, out):
    rows = own.shape[0]
    grad_in = own[...] + pair[:rows, :].astype(f32) + across[...].astype(f32)
    normed, inverse = normalize(source[...].astype(f32))
    out[...] = grad_middle[...] + norm_back(grad_in * (1.0 + scale[...]), normed, inverse)


def finish_qkv_kernel(me, p0, p1, p2, p3, out):
    place = me[2]
    group = p0.shape[1] // 3
    width = out.shape[1] // 3
    for s, piece in enumerate((p0, p1, p2, p3)):
        for part in range(3):
            at = part * width + (place ^ s) * group
            out[:, lanes(at, group)] = piece[:, part * group : (part + 1) * group].astype(f32)


def swap_seq(values_in, bits):
    return lax.ppermute(values_in, "seq", [(i, i ^ bits) for i in range(4)])


def halve_pair(values_in, place):
    half = values_in.shape[0] // 2
    mine = lax.dynamic_slice_in_dim(values_in, place % 2 * half, half)
    other = lax.dynamic_slice_in_dim(values_in, (1 - place % 2) * half, half)
    return mine, other.astype(bf16)


class Halving:
    def __init__(self, held, send, place):
        self.held, self.send, self.low, self.high = held, send, place % 2, place // 2

    def across_ready(self, me):
        rows, cols = self.held.shape
        half = ((rows // 2, cols), f32), ((rows // 2, cols), bf16)
        self.held, self.send = call(
            halve_across_kernel, "halve", half, me, self.held, swap_seq(self.send, 1)
        )

    def across(self):
        self.got = swap_seq(self.send, 2)

    def across_done(self, *others):
        self.held = (self.held + tie(self.got, *others)[0].astype(f32)).astype(bf16)

    def join(self, bit, bits):
        other = swap_seq(self.held, bits)
        first = jnp.where(bit == 0, self.held, other)
        second = jnp.where(bit == 0, other, self.held)
        self.held = jnp.concatenate([first, second], axis=0)

    def back_across(self):
        self.join(self.high, 2)

    def back_pair(self):
        self.join(self.low, 1)


def outward(values_in):
    return lax.ppermute(values_in, "seq", [(1, 0), (2, 3)])


def middle_swap(values_in):
    return lax.ppermute(values_in, "seq", [(1, 2), (2, 1)])


def tie(*values_in):
    return lax.optimization_barrier(values_in)


def spread(values_in):
    return [values_in] + [hop(values_in, 2 * r) for r in range(1, 4)]


def deal(blocks):
    return [blocks[0]] + [hop(blocks[r].astype(bf16), 2 * r) for r in range(1, 4)]


def total_of(pieces):
    total = pieces[0]
    for piece in pieces[1:]:
        total = total + piece.astype(f32)
    return total


def per_device(tokens, noise_steps, w_qkv, w_out, w_up, w_down, w_time, cotangent):
    index, place = lax.axis_index("dp"), lax.axis_index("seq")
    me = jnp.stack([index // 2, index % 2, place]).astype(jnp.int32)
    _, rows, width = tokens.shape
    group = width // 4
    count = 4 * rows
    part = w_out.shape[0]
    units = w_down.shape[0]
    source, cot = tokens[0], cotangent[0]

    half = HEAD_DIM // 2
    lane = jnp.arange(LANES)
    frequency = jnp.exp(-math.log(10000.0) * (lane % half).astype(f32) / half)
    block_place = place ^ jnp.arange(4)
    positions = (block_place[:, None] * rows + jnp.arange(rows)).reshape(-1).astype(f32)
    angles = positions[:, None] * frequency
    cosine = jnp.cos(angles)
    sine = jnp.sin(angles) * jnp.where(lane % HEAD_DIM < half, -1.0, 1.0)

    a1, b1 = swap_seq(source, 1), middle_swap(source)
    size = 3 * group + width
    (first,) = call(
        pick_first_kernel,
        "pick_first",
        [((part, size), bf16)],
        me,
        w_qkv,
        w_out,
        fetch=(0, 1),
    )
    steps_all = lax.all_to_all(
        jnp.broadcast_to(noise_steps.astype(f32), (8,)),
        "dp",
        split_axis=0,
        concat_axis=0,
        tiled=True,
    )
    first, steps_all = tie(first, steps_all)
    first_mine = spread(first)
    a1, b1 = tie(a1, b1)

    a2, b2 = outward(b1), middle_swap(a1)
    packed = call(
        pick_rest_kernel,
        "pick_rest",
        [((part + rows, width), bf16)] * 4,
        me,
        w_up,
        cot,
        fetch=(0, 1),
        store=(0, 1, 2, 3),
    )
    embed_all = time_embedding(steps_all)
    cond_part = jnp.dot(embed_all, w_time.astype(f32), precision=highest)
    condition = lax.all_to_all(cond_part, "dp", split_axis=0, concat_axis=0, tiled=True).reshape(
        4, width
    )
    a2, b2, condition, cosine, sine, down_late, *more = tie(
        a2, b2, condition, cosine, sine, w_down, *first_mine, *packed
    )
    first_mine, packed = more[:4], more[4:]

    a3 = outward(b2)
    (first_half,) = call(
        stack_kernel, "stack_first", [((4 * part, size), bf16)], me, *first_mine, store=(0,)
    )
    first_half, *packed = tie(first_half, *packed)
    packed = deal(packed)
    qkv_all, out_all = call(
        weave_kernel,
        "weave_first",
        [((width, 3 * group), bf16), ((width, width), bf16)],
        me,
        first_half,
        hop(first_half, 1),
        fetch=(0, 1),
    )
    a3, qkv_all = tie(a3, qkv_all)
    scale_a, shift_a, scale_b, shift_b = [condition[i : i + 1] for i in range(4)]

    queries, keys, values, normed_a, input_a = call(
        qkv_kernel,
        "qkv",
        [((count, group), bf16)] * 3
        + [((count, width), bf16)] * 2,
        me,
        source,
        a1,
        a2,
        a3,
        b1,
        b2,
        scale_a,
        shift_a,
        qkv_all,
        cosine,
        sine,
        store=(3, 4),
    )
    attended, log_total = call(
        attend_kernel,
        "attend",
        [((count, group), bf16), ((8, count), f32)],
        me,
        queries,
        keys,
        values,
    )
    attended, packed[1] = tie(attended, packed[1])
    pieces = [attended[:rows]] + [
        swap_seq(attended[s * rows : (s + 1) * rows], s) for s in range(1, 4)
    ]
    *pieces, packed[2], packed[3] = tie(*pieces, packed[2], packed[3])
    (up_half,) = call(
        stack_kernel, "stack_up", [((4 * part, width), bf16)], me, *packed, fetch=(0, 1, 2, 3)
    )
    down_other = hop(down_late, 1)
    up_other = hop(up_half, 1)
    mixed, middle, input_b = call(
        middle_kernel,
        "middle",
        [((rows, width), bf16), ((rows, width), f32), ((rows, width), bf16)],
        me,
        source,
        *pieces,
        out_all,
        scale_b,
        shift_b,
    )

    toks = [input_b, hop(input_b, 2), None, hop(input_b, 6)]
    up_half, up_other, toks[0] = tie(up_half, up_other, toks[0])
    (up_all,) = call(
        weave_kernel, "weave_up", [((width, width), bf16)], me, up_half, up_other
    )
    grads, outs, hidden, grad_upper = [None] * 4, [None] * 4, [None] * 4, [None] * 4
    last = None
    for r in (0, 3, 1, 2):
        if r:
            toks[r], hidden[last] = tie(toks[r], hidden[last])
        if r == 3:
            late, toks[3] = tie(input_b, toks[3])
            toks[2] = hop(late, 4)
        if r == 2:
            toks[2], grads[3] = tie(toks[2], grads[3])
        grads[r], outs[r], hidden[r], grad_upper[r] = call(
            ffn_kernel,
            "ffn",
            [((rows, width), bf16 if r else f32)] * 2 + [((rows, 2 * units), bf16)] * 2,
            me,
            toks[r],
            packed[r],
            up_all,
            w_down,
            down_other,
            scratch=[pltpu.VMEM((rows, width), f32)] * 2,
        )
        if r:
            grads[r] = hop(grads[r], 2 * r)
        last = r

    hidden[0], grad_upper[0], grads[1], grads[3] = tie(
        hidden[0], grad_upper[0], grads[1], grads[3]
    )
    give, keep = call(
        grad_down_kernel,
        "grad_down",
        [((units, width), bf16), ((units, width), f32)],
        me,
        *hidden,
        *packed,
        fetch=tuple(range(8)),
    )
    down_give, down_keep = give, keep
    up_give, up_keep = call(
        grad_up_kernel,
        "grad_up",
        [((width // 2, width), bf16), ((width // 2, width), f32)],
        me,
        *grad_upper,
        *toks,
        store=(0, 1),
    )
    grads[2], down_give, up_give = tie(grads[2], down_give, up_give)
    down_take, up_take = hop(down_give, 1), hop(up_give, 1)
    grad_middle, branch, sums_b, *to_heads = call(
        back_b_kernel,
        "back_b",
        [((rows, width), f32), ((rows, width), bf16), ((2, width), f32)]
        + [((rows, group), bf16)] * 4,
        me,
        *grads,
        middle,
        cot,
        scale_b,
        out_all,
    )
    proj_give, proj_keep = call(
        grad_qkv_kernel,
        "grad_proj",
        [((width // 2, width), bf16), ((width // 2, width), f32)],
        me,
        mixed,
        branch,
        store=(0, 1),
    )
    proj_give, *to_heads = tie(proj_give, *to_heads)
    grad_heads = [to_heads[0]] + [swap_seq(to_heads[s], s) for s in range(1, 4)]
    down_mine, down_send = call(
        halve_kernel,
        "halve_down",
        [((units // 2, width), f32), ((units // 2, width), bf16)],
        me,
        down_keep,
        down_take,
    )
    up_parts = call(
        pair_up_kernel,
        "pair_up",
        [((part, 2 * width), f32)] + [((part, 2 * width), bf16)] * 3,
        me,
        up_keep,
        up_take,
        proj_keep,
        hop(proj_give, 1),
        fetch=(0, 1, 2, 3),
        store=(0, 1, 2, 3),
    )
    *grad_heads, down_mine, down_send, up_parts[0] = tie(
        *grad_heads, down_mine, down_send, up_parts[0]
    )

    up_parts = deal(up_parts)
    down_sum = Halving(down_mine, down_send, place)
    down_sum.across_ready(me)
    (grad_projected,) = call(
        attend_back_kernel,
        "attend_back",
        [((count, 3 * group), bf16)],
        me,
        queries,
        keys,
        values,
        *grad_heads,
        log_total,
        cosine,
        sine,
        scratch=[pltpu.VMEM((count, LANES), f32)] * 2 + [pltpu.VMEM((group, count), f32)],
        fetch=(0, 1, 2, 8, 9),
    )
    grad_a, p2, pair, sums_a = call(
        back_a_kernel,
        "back_a",
        [((rows, width), f32)] * 2 + [((2 * rows, width), bf16), ((2, width), f32)],
        me,
        grad_projected,
        qkv_all,
        normed_a,
        fetch=(2,),
        store=(0, 1, 2),
    )
    pair = swap_seq(pair, 1)

    down_sum.held, down_sum.send, p2 = tie(down_sum.held, down_sum.send, p2)
    down_sum.across()
    (both,) = call(
        collect_kernel,
        "collect",
        [((part, 5 * width), f32)],
        me,
        *up_parts,
        fetch=(0, 1, 2, 3),
    )
    up_mine, up_send = halve_pair(both, place)
    up_sum = Halving(up_mine, up_send, place)
    give, keep = call(
        grad_qkv_kernel,
        "grad_qkv",
        [((width // 2, 3 * group), bf16), ((width // 2, 3 * group), f32)],
        me,
        input_a,
        grad_projected,
        fetch=(0,),
    )
    take, both = tie(hop(give, 1), both)
    qkv_parts = call(
        pair_kernel,
        "pair",
        [((part, 3 * group), f32)] + [((part, 3 * group), bf16)] * 3,
        me,
        keep,
        take,
    )
    sums_a, qkv_parts[1] = tie(sums_a, qkv_parts[1])
    qkv_parts = deal(qkv_parts)
    grad_condition = jnp.concatenate([sums_a, sums_b], axis=0)
    cond_cols = lax.all_to_all(
        grad_condition.reshape(8, -1), "dp", split_axis=0, concat_axis=0, tiled=True
    )
    qkv_cols = total_of(qkv_parts).astype(bf16)
    down_sum.across_done(qkv_cols, cond_cols)
    pair, up_sum.held, up_sum.send, down_sum.held, cond_cols, qkv_cols, *outs = tie(
        pair, up_sum.held, up_sum.send, down_sum.held, cond_cols, qkv_cols, *outs
    )

    (far,) = call(add_far_kernel, "add_far", [((rows, width), bf16)], me, p2, pair)
    far, up_sum.send = tie(far, up_sum.send)
    across = swap_seq(far, 2)
    up_sum.across_ready(me)
    outs = deal(outs)
    across, up_sum.held, up_sum.send, down_sum.held, qkv_cols, cond_cols, *outs = tie(
        across, up_sum.held, up_sum.send, down_sum.held, qkv_cols, cond_cols, *outs
    )

    up_sum.across()
    down_sum.back_across()
    qkv_pair = swap_seq(qkv_cols, 1)
    up_sum.across_done()
    cond_sum = cond_cols + swap_seq(cond_cols, 1)
    (grad_tokens,) = call(
        tokens_kernel,
        "tokens",
        [((rows, width), f32)],
        me,
        grad_a,
        pair,
        across,
        source,
        scale_a,
        grad_middle,
    )
    up_sum.held, down_sum.held, qkv_pair, cond_sum, *outs = tie(
        up_sum.held, down_sum.held, qkv_pair, cond_sum, *outs
    )

    up_sum.back_across()
    down_sum.back_pair()
    cond_sum = cond_sum + swap_seq(cond_sum, 2)
    result = (middle + total_of(outs)).astype(bf16)
    up_sum.held, qkv_pair = tie(up_sum.held, qkv_pair)

    qkv_far = swap_seq(jnp.stack([qkv_cols, qkv_pair]), 2)
    up_sum.back_pair()
    cond_sum, qkv_far = tie(cond_sum, qkv_far)
    grad_time = jnp.dot(embed_all.T, cond_sum, precision=highest)
    (grad_qkv,) = call(
        finish_qkv_kernel,
        "finish_qkv",
        [((part, 3 * width), f32)],
        me,
        qkv_cols,
        qkv_pair,
        qkv_far[0],
        qkv_far[1],
    )
    grad_down, both = down_sum.held, up_sum.held
    return (
        result[None],
        grad_tokens[None],
        grad_qkv,
        both[:, 4 * width :].astype(f32),
        both[:, : 4 * width].astype(f32),
        grad_down.astype(f32),
        grad_time,
    )


def solution(mesh):
    in_specs = (
        P("dp", "seq", None),
        P("dp"),
        P("dp", None),
        P("dp", None),
        P("dp", None),
        P("dp", None),
        P(None, "dp"),
        P("dp", "seq", None),
    )
    out_specs = (
        P("dp", "seq", None),
        P("dp", "seq", None),
        P("dp", None),
        P("dp", None),
        P("dp", None),
        P("dp", None),
        P(None, "dp"),
    )
    square = mesh.shape["dp"] == 8 and mesh.shape["seq"] == 4
    return jax.shard_map(
        per_device if square else per_device_any, mesh=mesh, in_specs=in_specs, out_specs=out_specs, check_vma=False
    )
```
